32 devices in a mesh: dp: 4 (over y, x), seq: 8 (over z, core).
Axes of the slice: x: 2, y: 2, z: 4, core: 2. Of those that a mesh axis runs over, the one named last changes fastest.
Arguments:
- tokens: bfloat16 [16384, 512], P(('dp', 'seq')), may hold values from -6 to 6
- cotangent: bfloat16 [16384, 512], P(('dp', 'seq')), may hold values from -6 to 6
- seq_lengths: int32 [4, 3], P('dp'), may hold values from 0 to 4096, as said below
- norm1_gain: float32 [512], replicated, may hold values from 0.5 to 1.5
- value_weight: bfloat16 [512, 1024], replicated, may hold values from -0.25 to 0.25
- ema_delta: float32 [512, 16], replicated, may hold values from -2 to 2
- ema_alpha: float32 [512, 16], replicated, may hold values from -30 to 0
- ema_beta: float32 [512, 16], replicated, may hold values from -9 to 9
- ema_eta: float32 [512, 16], replicated, may hold values from -5 to 5
- ema_omega: float32 [512], replicated, may hold values from -4 to 4
- mix_weight: bfloat16 [512, 2176], replicated, may hold values from -0.25 to 0.25
- qk_gain: float32 [2, 128], replicated, may hold values from -8 to 8
- qk_bias: float32 [2, 128], replicated, may hold values from -3 to 3
- rel_bias: float32 [128], replicated, may hold values from -4 to 4
- out_weight: bfloat16 [1024, 512], replicated, may hold values from -0.75 to 0.75
- norm2_gain: float32 [512], replicated, may hold values from 0.5 to 1.5
- ffn_in: bfloat16 [512, 1024], replicated, may hold values from -0.25 to 0.25
- ffn_out: bfloat16 [1024, 512], replicated, may hold values from -0.1875 to 0.1875
Outputs:
- block_out: float32 [16384, 512], P(('dp', 'seq'))
- input_grad: float32 [16384, 512], P(('dp', 'seq'))
- norm1_gain_grad: float32 [512], replicated
- value_weight_grad: float32 [512, 1024], replicated
- ema_delta_grad: float32 [512, 16], replicated
- ema_alpha_grad: float32 [512, 16], replicated
- ema_beta_grad: float32 [512, 16], replicated
- ema_eta_grad: float32 [512, 16], replicated
- ema_omega_grad: float32 [512], replicated
- mix_weight_grad: float32 [512, 2176], replicated
- qk_gain_grad: float32 [2, 128], replicated
- qk_bias_grad: float32 [2, 128], replicated
- rel_bias_grad: float32 [128], replicated
- out_weight_grad: float32 [1024, 512], replicated
- norm2_gain_grad: float32 [512], replicated
- ffn_in_grad: float32 [512, 1024], replicated
- ffn_out_grad: float32 [1024, 512], replicated
The draws below stay inside these ranges and needn't reach their ends.
Inputs may be any that keep to these rules, and one draw needn't show every extreme that they name: `seq_lengths`: row g lists the lengths of group g's sequences in order, each a multiple of 128, summing to 4096, zeros after the last; one sequence of each group begins within the group's first 1024 tokens and ends within its last 1024. Some group holds a single sequence of 4096 tokens.
All inputs are finite; a program needn't handle non-finite values.
Results may differ from the reference program's by a relative error of at most 0.022.
Values sent between devices are 32-bit elements; how exact they have to be, the bound alone decides.
No kernel may reach another device: no remote copies, remote signals or barrier semaphores. Data moves between devices by JAX's collectives and lax.ppermute only.
A program may use at most 256 MiB of HBM per device.

```python
import math
from functools import partial
import jax
import jax.numpy as jnp
from jax import lax

D = 512
ZDIM = 128
VDIM = 1024
NDIM = 16
FF = 1024
SPAN = 128
TOK_DEV = 512
GROUPS = 4
GROUP_TOK = 4096
TOKENS = 16384
MIXW = 2176


def decay_parts(key, slow_share):
    key_logits, key_choice, key_fraction = jax.random.split(key, 3)
    logits = jnp.clip(jax.random.normal(key_logits, (D, NDIM), jnp.float32), -2.0, 2.0)
    chosen = jax.random.uniform(key_choice, (D, NDIM), jnp.float32) < slow_share
    fraction = jax.random.uniform(key_fraction, (D, NDIM), jnp.float32)
    chain_length = 1.0 * GROUP_TOK
    slow_rate = 0.25 / chain_length * jnp.exp(fraction * jnp.log(8.0))
    fast_rate = 1.0 / 50.0 * jnp.exp(fraction * jnp.log(50.0 / 30.0))
    decay_rates = jnp.where(chosen, slow_rate, fast_rate)
    return (logits, decay_rates, jax.nn.sigmoid(logits))


def draw_ema_delta(key, part):
    slow_share = 0.5
    logits, decay_rates, shares = decay_parts(key, slow_share)
    return logits


def draw_ema_alpha(key, part):
    slow_share = 0.5
    logits, decay_rates, shares = decay_parts(key, slow_share)
    forget_ratio = decay_rates / shares
    return jnp.log(forget_ratio) - jnp.log1p(-forget_ratio)


def draw_ema_beta(key, part):
    slow_share = 0.5
    logits, decay_rates, shares = decay_parts(key, slow_share)
    key = jax.random.fold_in(key, 7)
    noise_draw = jnp.clip(jax.random.normal(key, (D, NDIM), jnp.float32), -4.0, 4.0)
    return noise_draw * jnp.sqrt(2.0 * decay_rates) / shares


def draw_seq_lengths(key, part):
    key = jax.random.fold_in(key, 5)
    key_lead, key_trail = jax.random.split(key)
    per_device = TOK_DEV // SPAN
    total_spans = GROUP_TOK // SPAN
    whole_group = jnp.arange(GROUPS, dtype=jnp.int32) == 0
    lead_spans = jnp.where(whole_group, 0, jax.random.randint(key_lead, (GROUPS,), 0, per_device))
    trail_spans = jnp.where(whole_group, 0, jax.random.randint(key_trail, (GROUPS,), 0, per_device))
    middle = total_spans - lead_spans - trail_spans
    has_lead = lead_spans > 0
    first_len = jnp.where(has_lead, lead_spans, middle)
    second_len = jnp.where(has_lead, middle, trail_spans)
    third_len = jnp.where(has_lead, trail_spans, 0)
    return (jnp.stack([first_len, second_len, third_len], axis=1) * SPAN).astype(jnp.int32)


def block_scale(rng, shape, cuts, least, top_value):
    def one(axis_at, blocks):
        heights = jax.random.uniform(jax.random.fold_in(jax.random.fold_in(rng, 6), axis_at), (blocks,), jnp.float32, least / len(cuts), top_value / len(cuts))
        return jnp.repeat(jnp.exp(heights), shape[axis_at] // blocks).reshape((-1,) + (1,) * (len(shape) - axis_at - 1))

    level = one(*cuts[0])
    for cut in cuts[1:]:
        level = level * one(*cut)
    return level


def scatter_about(stream_key, shape, scale, most, shards=(), kind=jnp.bfloat16):
    level = block_scale(stream_key, shape, shards, -0.22, 0.18) if shards else 1.0
    entries = jax.random.normal(stream_key, shape, jnp.float32) * scale * level
    return jnp.minimum(jnp.maximum(entries, -most), most).astype(kind)


def setup_inputs(seed: int = 0) -> dict:
    arg_keys = jax.random.split(jax.random.key(seed), 19)
    tokens = scatter_about(arg_keys[0], (TOKENS, D), 1.0, 6.0, ((0, 32),))
    cotangent = scatter_about(arg_keys[1], (TOKENS, D), 1.0, 6.0, ((0, 32),))
    seq_lengths = draw_seq_lengths(jax.random.fold_in(arg_keys[18], 71), 0)
    norm1_gain = jnp.clip(1.0 + 0.1 * jax.random.normal(arg_keys[3], (D,), jnp.float32), 0.5, 1.5)
    value_weight = scatter_about(arg_keys[4], (D, VDIM), D ** -0.5, 0.25)
    ema_delta = draw_ema_delta(jax.random.fold_in(arg_keys[18], 71), 0)
    ema_alpha = draw_ema_alpha(jax.random.fold_in(arg_keys[18], 71), 0)
    ema_beta = draw_ema_beta(jax.random.fold_in(arg_keys[18], 71), 0)
    ema_eta = scatter_about(arg_keys[8], (D, NDIM), 1.0, 5.0, (), jnp.float32)
    ema_omega = scatter_about(arg_keys[9], (D,), 1.0, 4.0, (), jnp.float32)
    mix_weight = scatter_about(arg_keys[10], (D, MIXW), D ** -0.5, 0.25)
    qk_gain = scatter_about(arg_keys[11], (2, ZDIM), 2.0, 8.0, (), jnp.float32)
    qk_bias = scatter_about(arg_keys[12], (2, ZDIM), 0.5, 3.0, (), jnp.float32)
    rel_bias = scatter_about(arg_keys[13], (SPAN,), 1.0, 4.0, (), jnp.float32)
    out_weight = scatter_about(arg_keys[14], (VDIM, D), (VDIM // 16) ** -0.5, 0.75)
    norm2_gain = jnp.clip(1.0 + 0.1 * jax.random.normal(arg_keys[15], (D,), jnp.float32), 0.5, 1.5)
    ffn_in = scatter_about(arg_keys[16], (D, FF), D ** -0.5, 0.25)
    ffn_out = scatter_about(arg_keys[17], (FF, D), FF ** -0.5, 0.1875)
    return dict(tokens=tokens, cotangent=cotangent, seq_lengths=seq_lengths, norm1_gain=norm1_gain, value_weight=value_weight, ema_delta=ema_delta, ema_alpha=ema_alpha, ema_beta=ema_beta, ema_eta=ema_eta, ema_omega=ema_omega, mix_weight=mix_weight, qk_gain=qk_gain, qk_bias=qk_bias, rel_bias=rel_bias, out_weight=out_weight, norm2_gain=norm2_gain, ffn_in=ffn_in, ffn_out=ffn_out)


@jax.custom_vjp
def lowrank_factor(v):
    return lax.optimization_barrier(v.astype(jnp.bfloat16)).astype(jnp.float32)

@jax.custom_vjp
def lowrank_backprop(v):
    return v

def low_keep(v):
    return (lowrank_factor(v), None)

def low_pass(kept, grad):
    return (grad,)

def back_keep(v):
    return (v, None)

def back_low(kept, grad):
    return (lowrank_factor(grad),)
lowrank_factor.defvjp(low_keep, low_pass)
lowrank_backprop.defvjp(back_keep, back_low)

def layer_norm(rows, gain):
    average = lax.optimization_barrier(jnp.mean(rows, axis=-1, keepdims=True))
    centered = rows - average
    spread = lax.optimization_barrier(jnp.mean(centered * centered, axis=-1, keepdims=True))
    return centered * lax.rsqrt(spread + 1e-05) * gain

def project(operand, matrix):
    return lowrank_backprop(jnp.dot(lowrank_factor(operand), matrix, precision=lax.Precision.HIGHEST))

def start_flags(lengths):
    positions = jnp.arange(GROUP_TOK, dtype=jnp.int32)
    begins = jnp.cumsum(lengths) - lengths
    hits = (positions[:, None] == begins[None, :]) & (lengths > 0)[None, :]
    return jnp.any(hits, axis=1).astype(jnp.float32)

def moving_average(normed, starts, log_keep, inflow, outflow):
    keep_step = jnp.exp(log_keep)
    blocks = normed.reshape(-1, SPAN, D)
    block_flags = starts.reshape(-1, SPAN)
    lag_steps = jnp.arange(SPAN).astype(jnp.float32)
    rise_powers = jnp.exp((lag_steps + 1.0)[:, None, None] * log_keep) * outflow
    span_keep = jnp.exp(SPAN * log_keep)

    def token_step(running, pieces):
        value_row, flag_value = pieces
        running = (1.0 - flag_value) * keep_step * running + inflow * value_row[:, None]
        return (running, lax.optimization_barrier(jnp.sum(outflow * running, axis=1)))

    @jax.checkpoint
    def block_step(entering, pieces):
        block_rows, flag_rows = pieces
        entering = entering * (1.0 - flag_rows[0])
        local_end, local_out = lax.scan(token_step, jnp.zeros_like(entering), (block_rows, flag_rows))
        smooth = local_out + jnp.einsum('dh,tdh->td', entering, rise_powers, precision=lax.Precision.HIGHEST)
        return (span_keep * entering + local_end, smooth)
    start_state = jnp.zeros((D, NDIM), jnp.float32)
    final_state, smooth = lax.scan(block_step, start_state, (blocks, block_flags))
    return smooth.reshape(-1, D)

def span_attention(queries, key_rows, values, rel_bias):
    offsets = jnp.arange(SPAN)[:, None] - jnp.arange(SPAN)[None, :]
    causal = offsets >= 0
    bias_table = jnp.where(causal, rel_bias[jnp.maximum(offsets, 0)], 0.0)
    score_scale = 1.0 / math.sqrt(ZDIM)

    def attend_block(pieces):
        query_block, key_block, value_tile_block = pieces
        scores = lowrank_backprop(jnp.einsum('nqz,nkz->nqk', lowrank_factor(query_block), lowrank_factor(key_block), precision=lax.Precision.HIGHEST)) * score_scale + bias_table
        scores = jnp.where(causal, scores, -1e+30)
        highest = lax.optimization_barrier(jnp.max(scores, axis=-1, keepdims=True))
        powers = jnp.exp(scores - highest)
        attention_weight_matrix = powers / lax.optimization_barrier(jnp.sum(powers, axis=-1, keepdims=True))
        return lowrank_backprop(jnp.einsum('dlj,djh->dlh', lowrank_factor(attention_weight_matrix), lowrank_factor(value_tile_block), precision=lax.Precision.HIGHEST))
    shaped = (queries.reshape(-1, 4, SPAN, ZDIM), key_rows.reshape(-1, 4, SPAN, ZDIM), values.reshape(-1, 4, SPAN, VDIM))
    return lax.map(jax.checkpoint(attend_block), shaped).reshape(-1, VDIM)

def group_layer(params, pieces):
    group_rows, starts = pieces
    norm1_gain, value_weight, ema_delta, ema_alpha, ema_beta, ema_eta, ema_omega, mix_weight, qk_gain, qk_bias, rel_bias, out_weight, norm2_gain, ffn_in, ffn_out = params
    normed = layer_norm(group_rows, norm1_gain)
    values = jax.nn.silu(project(normed, value_weight))
    shares = jax.nn.sigmoid(ema_delta)
    log_keep = jnp.log1p(-shares * jax.nn.sigmoid(ema_alpha))
    smooth = moving_average(normed, starts, log_keep, shares * ema_beta, ema_eta / math.sqrt(NDIM))
    smoothed = jax.nn.silu(smooth + ema_omega * normed)
    mixed_rows = project(smoothed, mix_weight)
    update = jax.nn.sigmoid(mixed_rows[:, :D])
    shared = jax.nn.silu(mixed_rows[:, D:D + ZDIM])
    reset_gate = jax.nn.silu(mixed_rows[:, D + ZDIM:D + ZDIM + VDIM])
    candidate = mixed_rows[:, D + ZDIM + VDIM:]
    queries = shared * qk_gain[0] + qk_bias[0]
    key_rows = shared * qk_gain[1] + qk_bias[1]
    attended = span_attention(queries, key_rows, values, rel_bias)
    hidden = jax.nn.silu(candidate + project(reset_gate * attended, out_weight))
    residual = group_rows + update * (hidden - group_rows)
    expanded = jax.nn.silu(project(layer_norm(residual, norm2_gain), ffn_in))
    return residual + project(expanded, ffn_out)

def reference(tokens, cotangent, seq_lengths, norm1_gain, value_weight, ema_delta, ema_alpha, ema_beta, ema_eta, ema_omega, mix_weight, qk_gain, qk_bias, rel_bias, out_weight, norm2_gain, ffn_in, ffn_out):
    starts = jax.vmap(start_flags)(seq_lengths)
    params = (norm1_gain.astype(jnp.float32), value_weight.astype(jnp.float32), ema_delta.astype(jnp.float32), ema_alpha.astype(jnp.float32), ema_beta.astype(jnp.float32), ema_eta.astype(jnp.float32), ema_omega.astype(jnp.float32), mix_weight.astype(jnp.float32), qk_gain.astype(jnp.float32), qk_bias.astype(jnp.float32), rel_bias.astype(jnp.float32), out_weight.astype(jnp.float32), norm2_gain.astype(jnp.float32), ffn_in.astype(jnp.float32), ffn_out.astype(jnp.float32))

    def forward(inputs, weights):
        step_fn = jax.checkpoint(partial(group_layer, weights))
        outputs = lax.map(step_fn, (inputs.reshape(GROUPS, GROUP_TOK, D), starts))
        return outputs.reshape(TOKENS, D)
    block_out, backward = jax.vjp(forward, tokens.astype(jnp.float32), params)
    input_grad, weight_grads = backward(cotangent.astype(jnp.float32))
    return (block_out, input_grad, weight_grads[0], weight_grads[1], weight_grads[2], weight_grads[3], weight_grads[4], weight_grads[5], weight_grads[6], weight_grads[7], weight_grads[8], weight_grads[9], weight_grads[10], weight_grads[11], weight_grads[12], weight_grads[13], weight_grads[14])
```

```python
import math

import jax
import jax.numpy as jnp
from jax import lax
from jax.experimental import pallas as pl
from jax.experimental.pallas import tpu as pltpu
from jax.sharding import PartitionSpec as P

SPAN = 128
CHUNK = 64
EPS = 1e-05
BF16 = jnp.bfloat16
F32 = jnp.float32
VMEM_LIMIT = 58 * 1024 * 1024


def sigmoid(a):
    return 0.5 * jnp.tanh(0.5 * a) + 0.5


def mm(a, b):
    return lax.dot_general(a, b, (((1,), (0,)), ((), ())), preferred_element_type=F32)


def mm_nt(a, b):
    return lax.dot_general(a, b, (((1,), (1,)), ((), ())), preferred_element_type=F32)


def mm_tn(a, b):
    return lax.dot_general(a, b, (((0,), (0,)), ((), ())), preferred_element_type=F32)


def call(body, ins, outs, scratch=(), flops=0, name=None):
    specs = []
    for a in ins:
        if a.dtype == jnp.int32:
            specs.append(pl.BlockSpec(memory_space=pltpu.SMEM))
        else:
            specs.append(pl.BlockSpec(memory_space=pltpu.VMEM))
    moved = sum(a.size * a.dtype.itemsize for a in ins)
    moved += sum(math.prod(s) * jnp.dtype(d).itemsize for s, d in outs)
    return pl.pallas_call(
        body,
        in_specs=specs,
        out_specs=[pl.BlockSpec(memory_space=pltpu.VMEM)] * len(outs),
        out_shape=[jax.ShapeDtypeStruct(s, d) for s, d in outs],
        scratch_shapes=[pltpu.VMEM(s, d) for s, d in scratch],
        compiler_params=pltpu.CompilerParams(vmem_limit_bytes=VMEM_LIMIT),
        cost_estimate=pl.CostEstimate(flops=int(flops), bytes_accessed=int(moved), transcendentals=0),
        name=name,
    )(*ins)


def clear_range(meta, low, high):
    count = meta.shape[0] - 1
    begin = jnp.int32(0)
    hit = jnp.bool_(False)
    for i in range(count):
        length = meta[1 + i]
        hit = hit | ((length > 0) & (begin >= low) & (begin < high))
        begin = begin + length
    return jnp.where(hit, 0.0, 1.0).astype(F32)


def chunk_masks(meta, first, chunks):
    rows = lax.broadcasted_iota(jnp.int32, (chunks, 128), 0)
    free = jnp.ones((chunks, 128), F32)
    for s in range(0, chunks, SPAN // CHUNK):
        position = first + s * CHUNK
        free = jnp.where(rows == s, clear_range(meta, position, position + 1), free)
    return free


def lanes_of(tile):
    return pl.ds(tile * 128, 128)


def tiled(ref):
    return jnp.concatenate([ref[i] for i in range(ref.shape[0])], axis=1)


def put_tiled(ref, value):
    for i in range(ref.shape[0]):
        ref[i] = value[:, i * 128 : (i + 1) * 128]


def scan_step(masks, values, decay_row, shifts, chunks):
    power = decay_row
    for i, mask in enumerate(masks):
        values = values + power * (mask * pltpu.roll(values, shifts[i], 0))
        power = power * power
    return values


def doubling_masks(mask, chunks, backward):
    masks = []
    distance = 1
    while distance < chunks:
        masks.append(mask)
        shift = chunks - distance if backward else distance
        mask = mask * pltpu.roll(mask, shift, 0)
        distance *= 2
    shifts = []
    distance = 1
    while distance < chunks:
        shifts.append(chunks - distance if backward else distance)
        distance *= 2
    return masks, shifts


def edge_masks(free, chunks, backward):
    rows = lax.broadcasted_iota(jnp.int32, (chunks, 128), 0)
    if backward:
        return jnp.where(rows == chunks - 1, 0.0, pltpu.roll(free, chunks - 1, 0))
    return jnp.where(rows == 0, 0.0, free)


def prefix_mask(free, chunks, backward):
    rows = lax.broadcasted_iota(jnp.int32, (chunks, 128), 0)
    if backward:
        reach = jnp.where(rows == chunks - 1, 1.0, pltpu.roll(free, chunks - 1, 0))
    else:
        reach = free
    distance = 1
    while distance < chunks:
        if backward:
            moved = jnp.where(rows >= chunks - distance, 1.0, pltpu.roll(reach, chunks - distance, 0))
        else:
            moved = jnp.where(rows < distance, 1.0, pltpu.roll(reach, distance, 0))
        reach = reach * moved
        distance *= 2
    return reach


def start_body(meta, tok, gain, delta, alpha, beta, eta, normed, low, enter, end, logk, keep, mix):
    tokens, width = tok.shape
    hidden = delta.shape[1]
    chunks = tokens // CHUNK
    x = tok[...].astype(F32)
    centered = x - jnp.mean(x, axis=1, keepdims=True)
    spread = jnp.mean(centered * centered, axis=1, keepdims=True)
    rows = centered * lax.rsqrt(spread + EPS) * gain[...]
    put_tiled(normed, rows)
    low[...] = rows.astype(BF16)
    share = jax.nn.sigmoid(delta[...].T)
    log_keep = jnp.log1p(-share * jax.nn.sigmoid(alpha[...].T))
    logk[...] = log_keep
    keep[...] = jnp.exp(log_keep)
    mix[...] = share * beta[...].T * (eta[...].T * (1.0 / math.sqrt(hidden)))
    free = chunk_masks(meta, meta[0] * tokens, chunks)
    edge = edge_masks(free, chunks, False)
    masks, shifts = doubling_masks(edge, chunks, False)
    for tile in range(width // 128):
        lanes = lanes_of(tile)
        keeps = [keep[h : h + 1, lanes] for h in range(hidden)]

        def step(t, state):
            value = normed[tile, pl.ds(t, chunks, stride=CHUNK), :]
            return tuple(k * u + value for k, u in zip(keeps, state))

        zero = jnp.zeros((chunks, 128), F32)
        state = lax.fori_loop(0, CHUNK, step, (zero,) * hidden, unroll=8)
        for h in range(hidden):
            decay = jnp.exp(CHUNK * logk[h : h + 1, lanes])
            reached = scan_step(masks, state[h], decay, shifts, chunks)
            enter[h, :, lanes] = edge * pltpu.roll(reached, 1, 0)
            end[h : h + 1, lanes] = reached[chunks - 1 : chunks]


def values_body(low, weight, values, slope):
    blocks = weight.shape[1] // 256
    for b in range(blocks):
        cols = pl.ds(b * 256, 256)
        raw = mm(low[...], weight[:, cols])
        gate = sigmoid(raw)
        out = raw * gate
        values[:, cols] = out.astype(BF16)
        slope[:, cols] = gate + out * (1.0 - gate)


def pair_body(backward, tokens, meta, own, other, logk, out):
    core = meta[0] % 2
    first = (meta[0] - core) * tokens
    middle = first + tokens
    decay = jnp.exp(tokens * logk[...])
    if backward:
        reach = clear_range(meta, first + 1, middle + 1)
        near = jnp.where(core == 0, own[...], other[...])
        far = jnp.where(core == 0, other[...], own[...])
    else:
        reach = clear_range(meta, middle, middle + tokens)
        near = jnp.where(core == 0, other[...], own[...])
        far = jnp.where(core == 0, own[...], other[...])
    out[...] = near + (reach * decay) * far


def carry_of(backward, tokens, meta, other, arrived, logk):
    core = meta[0] % 2
    first = (meta[0] - core) * tokens
    span = 2 * tokens
    chip_decay = jnp.exp(span * logk[...])
    total = None
    power = None
    for k, part in enumerate(arrived):
        if backward:
            reach = clear_range(meta, first + span, first + (k + 1) * span + 1)
        else:
            reach = clear_range(meta, first - k * span, first)
        term = part[...] * reach
        if power is not None:
            term = term * power
        total = term if total is None else total + term
        power = chip_decay if power is None else power * chip_decay
    decay = jnp.exp(tokens * logk[...])
    middle = first + tokens
    if backward:
        crossing = clear_range(meta, middle, middle + 1)
        through = clear_range(meta, middle + 1, middle + tokens)
        passed = crossing * (other[...] + (through * decay) * total)
        return jnp.where(core == 0, passed, total)
    through = clear_range(meta, first, middle)
    return jnp.where(core == 0, total, other[...] + (through * decay) * total)


def layer_grad(weighted, normal, inverse):
    mean_one = jnp.mean(weighted, axis=1, keepdims=True)
    mean_two = jnp.mean(weighted * normal, axis=1, keepdims=True)
    return (weighted - mean_one - normal * mean_two) * inverse


def shift_rows(table, down):
    size = table.shape[0]
    rows = lax.broadcasted_iota(jnp.int32, table.shape, 0)
    bit = 1
    while bit < size:
        moved = pltpu.roll(table, bit if down else size - bit, 1)
        table = jnp.where((rows & bit) != 0, moved, table)
        bit *= 2
    return table


def forward_body(
    chips,
    meta,
    tok,
    cot,
    normed,
    enter,
    other,
    *rest,
):
    arrived = rest[:chips]
    (
        logk,
        keep,
        mix,
        omega,
        mix_weight,
        qk_gain,
        qk_bias,
        rel_rev,
        values,
        out_weight,
        gain2,
        ffn_in,
        ffn_out,
        block_out,
        kept,
        sent,
        states,
        slope_pre,
        low_smoothed,
        update_grad,
        reset_raw,
        attended,
        weights,
        queries,
        keys,
        shared,
        shared_slope,
        out_grad,
        input_part,
        gain2_grad,
        carry,
        smooth,
        update,
        candidate,
        gated,
        expanded,
        slope_exp,
        normal2,
        expand_grad,
    ) = rest[chips:]
    tokens, width = tok.shape
    hidden = mix.shape[0]
    chunks = tokens // CHUNK
    shared_width = qk_gain.shape[1]
    value_width = out_weight.shape[0]
    core = meta[0] % 2
    carry[...] = carry_of(False, tokens, meta, other, arrived, logk)
    free = chunk_masks(meta, meta[0] * tokens, chunks)
    reach = prefix_mask(free, chunks, False)
    offset = (lax.broadcasted_iota(jnp.int32, (chunks, 128), 0) * CHUNK).astype(F32)
    for tile in range(width // 128):
        lanes = lanes_of(tile)
        state = []
        for h in range(hidden):
            entry = jnp.exp(offset * logk[h : h + 1, lanes]) * reach
            first = enter[h, :, lanes] + carry[h : h + 1, lanes] * entry
            states[h, :, lanes] = first
            state.append(first)
        keeps = [keep[h : h + 1, lanes] for h in range(hidden)]
        mixes = [mix[h : h + 1, lanes] for h in range(hidden)]

        def step(t, state):
            place = (tile, pl.ds(t, chunks, stride=CHUNK), slice(None))
            value = normed[place]
            state = tuple(k * u + value for k, u in zip(keeps, state))
            parts = [c * u for c, u in zip(mixes, state)]
            while len(parts) > 1:
                parts = [a + b for a, b in zip(parts[::2], parts[1::2])]
            smooth[place] = parts[0]
            return state

        lax.fori_loop(0, CHUNK, step, tuple(state), unroll=4)
    pre = tiled(smooth) + omega[...] * tiled(normed)
    gate = sigmoid(pre)
    smoothed = pre * gate
    low_smoothed[...] = smoothed.astype(BF16)
    slope_pre[...] = gate + smoothed * (1.0 - gate)
    base = width + shared_width
    for b in range(width // 256):
        cols = pl.ds(b * 256, 256)
        update[:, cols] = sigmoid(mm(low_smoothed[...], mix_weight[:, cols]))
    raw = mm(low_smoothed[...], mix_weight[:, width:base])
    gate = sigmoid(raw)
    silu = raw * gate
    shared[...] = silu
    shared_slope[...] = gate + silu * (1.0 - gate)
    queries[...] = (silu * qk_gain[0:1] + qk_bias[0:1]).astype(BF16)
    keys[...] = (silu * qk_gain[1:2] + qk_bias[1:2]).astype(BF16)
    for b in range(value_width // 256):
        reset_raw[:, b * 256 : (b + 1) * 256] = mm(
            low_smoothed[...], mix_weight[:, base + b * 256 : base + (b + 1) * 256]
        )
    for b in range(width // 256):
        low = base + value_width + b * 256
        candidate[:, b * 256 : (b + 1) * 256] = mm(low_smoothed[...], mix_weight[:, low : low + 256])
    place = lax.broadcasted_iota(jnp.int32, (SPAN, SPAN), 0)
    causal = place >= lax.broadcasted_iota(jnp.int32, (SPAN, SPAN), 1)
    bias = shift_rows(jnp.broadcast_to(rel_rev[...], (SPAN, SPAN)), True)
    scale = 1.0 / math.sqrt(shared_width)
    for s in range(tokens // SPAN):
        rows = pl.ds(s * SPAN, SPAN)
        scores = mm_nt(queries[rows, :], keys[rows, :]) * scale + bias
        scores = jnp.where(causal, scores, -1e30)
        powers = jnp.exp(scores - jnp.max(scores, axis=1, keepdims=True))
        share = powers / jnp.sum(powers, axis=1, keepdims=True)
        weights[rows, :] = share
        attended[rows, :] = mm(share.astype(BF16), values[rows, :])
    for b in range(value_width // 256):
        cols = pl.ds(b * 256, 256)
        raw = reset_raw[:, cols]
        gated[:, cols] = (raw * sigmoid(raw) * attended[:, cols]).astype(BF16)
    total = candidate[...] + mm(gated[...], out_weight[...])
    gate = sigmoid(total)
    hidden_rows = total * gate
    slope_hidden = gate + hidden_rows * (1.0 - gate)
    x = tok[...].astype(F32)
    change = hidden_rows - x
    gates = update[...]
    residual = x + gates * change
    centered = residual - jnp.mean(residual, axis=1, keepdims=True)
    inverse = lax.rsqrt(jnp.mean(centered * centered, axis=1, keepdims=True) + EPS)
    normal = centered * inverse
    normal2[...] = normal
    low2 = (normal * gain2[...]).astype(BF16)
    for b in range(ffn_in.shape[1] // 256):
        cols = pl.ds(b * 256, 256)
        raw = mm(low2, ffn_in[:, cols])
        gate = sigmoid(raw)
        silu = raw * gate
        expanded[:, cols] = silu.astype(BF16)
        slope_exp[:, cols] = gate + silu * (1.0 - gate)
    block_out[...] = residual + mm(expanded[...], ffn_out[...])
    half = width // 2
    low_cot = cot[...]
    mine = core * half
    theirs = (1 - core) * half
    for target, begin in ((sent, theirs), (kept, mine)):
        begin = pl.multiple_of(begin, 128)
        target[:, :width] = mm_tn(expanded[:, pl.ds(begin, half)], low_cot)
        second = pl.multiple_of(begin + width, 128)
        target[:, width : 2 * width] = mm_tn(expanded[:, pl.ds(second, half)], low_cot)
    for b in range(ffn_in.shape[1] // 256):
        cols = pl.ds(b * 256, 256)
        rise = mm_nt(low_cot, ffn_out[cols, :])
        expand_grad[:, cols] = (rise * slope_exp[:, cols]).astype(BF16)
    expanded[:, :width] = low2
    for target, begin in ((sent, theirs), (kept, mine)):
        begin = pl.multiple_of(begin, 128)
        target[:, 2 * width : 4 * width] = mm_tn(expanded[:, pl.ds(begin, half)], expand_grad[...])
    norm_out = mm_nt(expand_grad[...], ffn_in[...])
    normal = normal2[...]
    gain2_grad[...] = jnp.sum(norm_out * normal, axis=0, keepdims=True)
    upstream = low_cot.astype(F32) + layer_grad(norm_out * gain2[...], normal, inverse)
    input_part[...] = upstream * (1.0 - gates)
    update_grad[...] = (upstream * change * gates * (1.0 - gates)).astype(BF16)
    low_out = (upstream * gates * slope_hidden).astype(BF16)
    out_grad[...] = low_out
    for target, begin in ((sent, theirs), (kept, mine)):
        begin = pl.multiple_of(begin, 128)
        target[:, 4 * width : 5 * width] = mm_tn(gated[:, pl.ds(begin, half)], low_out)
        second = pl.multiple_of(begin + width, 128)
        target[:, 5 * width :] = mm_tn(gated[:, pl.ds(second, half)], low_out)


def middle_body(
    meta,
    out_grad,
    out_weight,
    reset_raw,
    attended,
    weights,
    queries,
    keys,
    shared,
    shared_slope,
    values,
    values_slope,
    low_smoothed,
    update_grad,
    normed_low,
    qk_gain,
    kept,
    sent,
    mixed_grad,
    value_grad,
    small,
    attend_grad,
):
    tokens, width = out_grad.shape
    shared_width = qk_gain.shape[1]
    value_width = out_weight.shape[0]
    core = meta[0] % 2
    base = width + shared_width
    mixed_grad[:, :width] = update_grad[...]
    mixed_grad[:, base + value_width :] = out_grad[...]
    for b in range(value_width // 256):
        cols = pl.ds(b * 256, 256)
        rise = mm_nt(out_grad[...], out_weight[cols, :])
        raw = reset_raw[:, cols]
        gate = sigmoid(raw)
        silu = raw * gate
        mixed_grad[:, base + b * 256 : base + (b + 1) * 256] = (
            rise * attended[:, cols] * (gate + silu * (1.0 - gate))
        ).astype(BF16)
        attend_grad[:, cols] = (rise * silu).astype(BF16)
    scale = 1.0 / math.sqrt(shared_width)
    slopes = jnp.zeros((SPAN, SPAN), F32)
    for s in range(tokens // SPAN):
        rows = pl.ds(s * SPAN, SPAN)
        upstream = attend_grad[rows, :]
        share = weights[rows, :]
        rise = mm_nt(upstream, values[rows, :])
        value_rise = mm_tn(share.astype(BF16), upstream)
        value_grad[rows, :] = (value_rise * values_slope[rows, :]).astype(BF16)
        score_grad = share * (rise - jnp.sum(share * rise, axis=1, keepdims=True))
        slopes = slopes + score_grad
        low = (score_grad * scale).astype(BF16)
        query_grad = mm(low, keys[rows, :])
        key_grad = mm_tn(low, queries[rows, :])
        silu = shared[rows, :]
        pieces = (
            jnp.sum(query_grad * silu, axis=0, keepdims=True),
            jnp.sum(key_grad * silu, axis=0, keepdims=True),
            jnp.sum(query_grad, axis=0, keepdims=True),
            jnp.sum(key_grad, axis=0, keepdims=True),
        )
        sums = pieces if s == 0 else tuple(a + b for a, b in zip(sums, pieces))
        shared_grad = query_grad * qk_gain[0:1] + key_grad * qk_gain[1:2]
        mixed_grad[rows, width:base] = (shared_grad * shared_slope[rows, :]).astype(BF16)
    small[...] = jnp.zeros_like(small)
    for i in range(4):
        small[i : i + 1, :] = sums[i]
    small[4:5, :] = jnp.sum(shift_rows(slopes, False), axis=0, keepdims=True)
    half = width // 2
    cut = mixed_grad.shape[1]
    for target, begin in ((sent, (1 - core) * half), (kept, core * half)):
        begin = pl.multiple_of(begin, 128)
        target[:, :cut] = mm_tn(low_smoothed[:, pl.ds(begin, half)], mixed_grad[...])
        target[:, cut:] = mm_tn(normed_low[:, pl.ds(begin, half)], value_grad[...])


def rise_body(
    meta,
    mixed_grad,
    value_grad,
    mix_weight,
    value_weight,
    slope_pre,
    normed,
    omega,
    logk,
    keep,
    smooth_grad,
    norm_grad,
    enter,
    end,
    omega_grad,
):
    width = value_weight.shape[0]
    tokens = value_grad.shape[0]
    hidden = keep.shape[0]
    chunks = tokens // CHUNK
    grad = mm_nt(mixed_grad[...], mix_weight[...]) * slope_pre[...]
    put_tiled(smooth_grad, grad)
    put_tiled(norm_grad, mm_nt(value_grad[...], value_weight[...]) + omega[...] * grad)
    omega_grad[...] = jnp.sum(grad * tiled(normed), axis=0, keepdims=True)
    free = chunk_masks(meta, meta[0] * tokens, chunks)
    edge = edge_masks(free, chunks, True)
    masks, shifts = doubling_masks(edge, chunks, True)
    for tile in range(width // 128):
        lanes = lanes_of(tile)
        keeps = [keep[h : h + 1, lanes] for h in range(hidden)]

        def step(t, state):
            value = smooth_grad[tile, pl.ds(CHUNK - 1 - t, chunks, stride=CHUNK), :]
            return tuple(k * u + value for k, u in zip(keeps, state))

        zero = jnp.zeros((chunks, 128), F32)
        state = lax.fori_loop(0, CHUNK, step, (zero,) * hidden, unroll=8)
        for h in range(hidden):
            decay = jnp.exp(CHUNK * logk[h : h + 1, lanes])
            reached = scan_step(masks, state[h], decay, shifts, chunks)
            enter[h, :, lanes] = edge * pltpu.roll(reached, chunks - 1, 0)
            end[h : h + 1, lanes] = reached[0:1]


def close_body(
    chips,
    meta,
    tok,
    gain,
    normed,
    smooth_grad,
    norm_grad,
    states,
    enter,
    other,
    *rest,
):
    arrived = rest[:chips]
    (
        logk,
        keep,
        mix,
        input_part,
        omega_grad,
        gain2_grad,
        small,
        input_grad,
        packed,
        carry,
        history,
        total,
    ) = rest[chips:]
    tokens, width = tok.shape
    hidden = keep.shape[0]
    chunks = tokens // CHUNK
    carry[...] = carry_of(True, tokens, meta, other, arrived, logk)
    free = chunk_masks(meta, meta[0] * tokens, chunks)
    reach = prefix_mask(free, chunks, True)
    offset = ((chunks - 1 - lax.broadcasted_iota(jnp.int32, (chunks, 128), 0)) * CHUNK).astype(F32)
    group = history.shape[1]
    total[...] = norm_grad[...]
    for tile in range(width // 128):
        lanes = lanes_of(tile)
        for low in range(0, hidden, group):
            heads = range(low, low + group)
            keeps = [keep[h : h + 1, lanes] for h in heads]
            mixes = [mix[h : h + 1, lanes] for h in heads]

            def rise(t, state):
                value = normed[tile, pl.ds(t, chunks, stride=CHUNK), :]
                state = tuple(k * u + value for k, u in zip(keeps, state))
                for i in range(group):
                    history[t, i] = state[i]
                return state

            lax.fori_loop(0, CHUNK, rise, tuple(states[h, :, lanes] for h in heads), unroll=4)
            first = []
            for h in heads:
                entry = jnp.exp(offset * logk[h : h + 1, lanes]) * reach
                first.append(enter[h, :, lanes] + carry[h : h + 1, lanes] * entry)

            def fall(i, held):
                state, reads, marks = held
                t = CHUNK - 1 - i
                place = (tile, pl.ds(t, chunks, stride=CHUNK), slice(None))
                value = smooth_grad[place]
                row = normed[place]
                state = tuple(k * w + value for k, w in zip(keeps, state))
                reads = tuple(r + w * row for r, w in zip(reads, state))
                marks = tuple(m + w * history[t, j] for j, (m, w) in enumerate(zip(marks, state)))
                parts = [c * w for c, w in zip(mixes, state)]
                while len(parts) > 1:
                    parts = [a + b for a, b in zip(parts[::2], parts[1::2])]
                total[place] = total[place] + parts[0]
                return state, reads, marks

            zeros = (jnp.zeros((chunks, 128), F32),) * group
            _, reads, marks = lax.fori_loop(0, CHUNK, fall, (tuple(first), zeros, zeros), unroll=4)
            for j, h in enumerate(heads):
                packed[h : h + 1, lanes] = jnp.sum(reads[j], axis=0, keepdims=True)
                packed[hidden + h : hidden + h + 1, lanes] = jnp.sum(marks[j], axis=0, keepdims=True)
    x = tok[...].astype(F32)
    centered = x - jnp.mean(x, axis=1, keepdims=True)
    inverse = lax.rsqrt(jnp.mean(centered * centered, axis=1, keepdims=True) + EPS)
    normal = centered * inverse
    upstream = tiled(total)
    input_grad[...] = input_part[...] + layer_grad(upstream * gain[...], normal, inverse)
    at = 2 * hidden
    packed[at : at + 8, :] = jnp.zeros((8, width), F32)
    packed[at : at + 1, :] = jnp.sum(upstream * normal, axis=0, keepdims=True)
    packed[at + 1 : at + 2, :] = gain2_grad[...]
    packed[at + 2 : at + 3, :] = omega_grad[...]
    for i in range(5):
        packed[at + 3 + i : at + 4 + i, 0 : small.shape[1]] = small[i : i + 1, :]


def finish_body(packed, delta, alpha, beta, eta, delta_grad, alpha_grad, beta_grad, eta_grad):
    hidden = delta.shape[1]
    scale = 1.0 / math.sqrt(hidden)
    read = packed[0:hidden, :]
    mark = packed[hidden : 2 * hidden, :]
    share = jax.nn.sigmoid(delta[...].T)
    damp = jax.nn.sigmoid(alpha[...].T)
    inflow = share * beta[...].T
    outflow = eta[...].T * scale
    eta_grad[...] = (inflow * read * scale).T
    inflow_grad = outflow * read
    beta_grad[...] = (share * inflow_grad).T
    rate = inflow * outflow * (mark - read) / (share * damp - 1.0)
    share_grad = beta[...].T * inflow_grad + damp * rate
    delta_grad[...] = (share_grad * share * (1.0 - share)).T
    alpha_grad[...] = (share * rate * damp * (1.0 - damp)).T


def swap(a, axis, bit):
    count = lax.axis_size(axis)
    return lax.ppermute(a, axis, [(i, i ^ bit) for i in range(count)])


def bit_of(axis, bit):
    return (lax.axis_index(axis) // bit) % 2


def chip_parts(state, backward):
    count = lax.axis_size("seq")
    parts = []
    for k in range(1, count // 2):
        if backward:
            moves = [(i, i - 2 * k) for i in range(2 * k, count)]
        else:
            moves = [(i, i + 2 * k) for i in range(count - 2 * k)]
        parts.append(lax.ppermute(state, "seq", moves))
    return parts


def axis_bits(axis, least):
    bits = []
    bit = least
    while bit < lax.axis_size(axis):
        bits.append((axis, bit))
        bit *= 2
    return bits


def scatter_sum(kept, arrived, bits):
    for axis, bit in bits:
        total = kept + arrived
        half = total.shape[0] // 2
        place = bit_of(axis, bit)
        arrived = swap(lax.dynamic_slice_in_dim(total, (1 - place) * half, half), axis, bit)
        kept = lax.dynamic_slice_in_dim(total, place * half, half)
    return kept + arrived


def join(own, other, place):
    own_first = jnp.concatenate([own, other], axis=0)
    other_first = jnp.concatenate([other, own], axis=0)
    return jnp.where(place == 0, own_first, other_first)


def gather(part, bits):
    for axis, bit in reversed(bits):
        part = join(part, swap(part, axis, bit), bit_of(axis, bit))
    return part


def sum_stage(kept, sent):
    arrived = swap(sent, "seq", 1)
    flat = axis_bits("dp", 1)
    deep = axis_bits("seq", 2)
    half = kept.shape[0] // 2
    done = []
    for i, order in enumerate((flat + deep, flat[::-1] + deep)):
        part = slice(i * half, (i + 1) * half)
        done.append(gather(scatter_sum(kept[part], arrived[part], order), order))
    own = jnp.concatenate(done, axis=0)
    return join(own, swap(own, "seq", 1), bit_of("seq", 1))


def sum_small(part):
    for axis, bit in axis_bits("seq", 1) + axis_bits("dp", 1):
        part = part + swap(part, axis, bit)
    return part


def shards(
    tokens,
    cotangent,
    seq_lengths,
    norm1_gain,
    value_weight,
    ema_delta,
    ema_alpha,
    ema_beta,
    ema_eta,
    ema_omega,
    mix_weight,
    qk_gain,
    qk_bias,
    rel_bias,
    out_weight,
    norm2_gain,
    ffn_in,
    ffn_out,
):
    rows, width = tokens.shape
    hidden = ema_delta.shape[1]
    chunks = rows // CHUNK
    value_width = value_weight.shape[1]
    inner = ffn_in.shape[1]
    mixed = mix_weight.shape[1]
    shared_width = qk_gain.shape[1]
    meta = jnp.concatenate([lax.axis_index("seq")[None].astype(jnp.int32), seq_lengths[0]])
    gain1 = norm1_gain[None]
    gain2 = norm2_gain[None]
    omega = ema_omega[None]
    rel_rev = jnp.roll(rel_bias[::-1], 1)[None]
    full = (rows, width)
    tiles = (width // 128, rows, 128)
    state = (hidden, width)
    states = (hidden, chunks, width)
    normed, normed_low, enter, end, logk, keep, mix = call(
        start_body,
        (meta, tokens, gain1, ema_delta, ema_alpha, ema_beta, ema_eta),
        [(tiles, F32), (full, BF16), (states, F32), (state, F32), (state, F32), (state, F32), (state, F32)],
        name="norm_and_states",
    )
    other = swap(end, "seq", 1)
    chip_end = call(
        lambda *refs: pair_body(False, rows, *refs),
        (meta, end, other, logk),
        [(state, F32)],
        name="chip_state",
    )[0]
    arrived = chip_parts(chip_end, False)
    values, values_slope = call(
        values_body,
        (normed_low, value_weight),
        [((rows, value_width), BF16), ((rows, value_width), F32)],
        flops=2 * rows * width * value_width,
        name="values",
    )
    half = width // 2
    first_cols = 2 * width + inner + 2 * width
    wide = (rows, value_width)
    thin = (rows, shared_width)
    (
        block_out,
        kept1,
        sent1,
        entering,
        slope_pre,
        low_smoothed,
        update_grad,
        reset_raw,
        attended,
        weights,
        queries,
        keys,
        shared,
        shared_slope,
        out_grad,
        input_part,
        gain2_grad,
    ) = call(
        lambda *refs: forward_body(len(arrived), *refs),
        (meta, tokens, cotangent, normed, enter, other, *arrived, logk, keep, mix, omega, mix_weight)
        + (qk_gain, qk_bias, rel_rev, values, out_weight, gain2, ffn_in, ffn_out),
        [
            (full, F32),
            ((half, first_cols), F32),
            ((half, first_cols), F32),
            (states, F32),
            (full, F32),
            (full, BF16),
            (full, BF16),
            (wide, F32),
            (wide, F32),
            ((rows, SPAN), F32),
            (thin, BF16),
            (thin, BF16),
            (thin, F32),
            (thin, F32),
            (full, BF16),
            (full, F32),
            ((1, width), F32),
        ],
        scratch=[
            (state, F32),
            (tiles, F32),
            (full, F32),
            (full, F32),
            (wide, BF16),
            ((rows, inner), BF16),
            ((rows, inner), F32),
            (full, F32),
            ((rows, inner), BF16),
        ],
        flops=2 * rows * width * (mixed + 4 * value_width + 2 * inner * 3),
        name="forward",
    )
    first = sum_stage(kept1, sent1)
    kept2, sent2, mixed_grad, value_grad, small = call(
        middle_body,
        (meta, out_grad, out_weight, reset_raw, attended, weights, queries, keys, shared, shared_slope)
        + (values, values_slope, low_smoothed, update_grad, normed_low, qk_gain),
        [
            ((half, mixed + value_width), F32),
            ((half, mixed + value_width), F32),
            ((rows, mixed), BF16),
            (wide, BF16),
            ((8, shared_width), F32),
        ],
        scratch=[(wide, BF16)],
        flops=2 * rows * width * (mixed + 2 * value_width),
        name="attention_back",
    )
    second = sum_stage(kept2, sent2)
    smooth_grad, norm_grad, later, begin, omega_grad = call(
        rise_body,
        (meta, mixed_grad, value_grad, mix_weight, value_weight, slope_pre, normed, omega, logk, keep),
        [(tiles, F32), (tiles, F32), (states, F32), (state, F32), ((1, width), F32)],
        flops=2 * rows * width * (mixed + value_width),
        name="smooth_back",
    )
    other_begin = swap(begin, "seq", 1)
    chip_begin = call(
        lambda *refs: pair_body(True, rows, *refs),
        (meta, begin, other_begin, logk),
        [(state, F32)],
        name="chip_grad",
    )[0]
    returned = chip_parts(chip_begin, True)
    input_grad, packed = call(
        lambda *refs: close_body(len(returned), *refs),
        (meta, tokens, gain1, normed, smooth_grad, norm_grad, entering, later, other_begin, *returned)
        + (logk, keep, mix, input_part, omega_grad, gain2_grad, small),
        [(full, F32), ((2 * hidden + 8, width), F32)],
        scratch=[(state, F32), ((CHUNK, hidden // 2, chunks, 128), F32), (tiles, F32)],
        name="state_back",
    )
    packed = sum_small(packed)
    delta_grad, alpha_grad, beta_grad, eta_grad = call(
        finish_body,
        (packed, ema_delta, ema_alpha, ema_beta, ema_eta),
        [((width, hidden), F32)] * 4,
        name="state_parameters",
    )
    at = 2 * hidden
    tail = packed[at + 3 :, :shared_width]
    upper = lambda low: jnp.concatenate([first[:, low : low + width], first[:, low + width : low + 2 * width]], axis=0)
    return (
        block_out,
        input_grad,
        packed[at],
        second[:, mixed:],
        delta_grad,
        alpha_grad,
        beta_grad,
        eta_grad,
        packed[at + 2],
        second[:, :mixed],
        tail[0:2],
        tail[2:4],
        jnp.roll(tail[4][::-1], 1),
        upper(2 * width + inner),
        packed[at + 1],
        first[:, 2 * width : 2 * width + inner],
        upper(0),
    )


def solution(mesh):
    rows = P(("dp", "seq"), None)
    in_specs = (rows, rows, P("dp", None)) + (P(),) * 15
    out_specs = (rows, rows) + (P(),) * 15
    return jax.shard_map(shards, mesh=mesh, in_specs=in_specs, out_specs=out_specs, check_vma=False)
```

```python
import math

import jax
import jax.numpy as jnp
from jax import lax
from jax.experimental import pallas as pl
from jax.experimental.pallas import tpu as pltpu
from jax.sharding import PartitionSpec as P

SPAN = 128
CHUNK = 64
EPS = 1e-05
BF16 = jnp.bfloat16
F32 = jnp.float32
ROOM = 2 * 1024 * 1024


def sigmoid(a):
    return 0.5 * jnp.tanh(0.5 * a) + 0.5


def mm(a, b):
    return lax.dot_general(a, b, (((1,), (0,)), ((), ())), preferred_element_type=F32)


def mm_nt(a, b):
    return lax.dot_general(a, b, (((1,), (1,)), ((), ())), preferred_element_type=F32)


def mm_tn(a, b):
    return lax.dot_general(a, b, (((0,), (0,)), ((), ())), preferred_element_type=F32)


COSTS = {
    "norm_and_states": 2.7,
    "values": 1.0,
    "local_average": 3.1,
    "carried_average": 2.7,
    "mix": 1.4,
    "attention": 1.9,
    "hidden": 1.4,
    "expand": 1.1,
    "expand_back": 0.8,
    "hidden_back": 1.4,
    "reset_back": 1.2,
    "attention_back": 1.9,
    "smooth_back": 2.0,
    "states_back": 2.5,
    "state_back": 2.7,
    "norm_back": 1.8,
    "block_out": 1.7,
    "grad": 1.4,
    "split": 0.35,
    "join": 0.35,
    "sum": 0.25,
    "out": 1.6,
}
PACE = 1e10


def cost_of(name):
    return COSTS.get(name, COSTS.get(name.split("_")[-1], 0.6))


class Line:
    def __init__(self):
        self.token = None

    def __call__(self, body, ins, outs, scratch=(), name=None, held=None, alias=None, dma=0):
        count = len(ins)
        before = () if self.token is None else (self.token,)
        alias = alias or {}
        specs = []
        for i, a in enumerate(ins):
            if i in alias:
                specs.append(pl.BlockSpec(memory_space=pl.ANY))
            else:
                specs.append(pl.BlockSpec(memory_space=pltpu.SMEM if a.dtype == jnp.int32 else pltpu.VMEM))
        specs += [pl.BlockSpec(memory_space=pl.ANY)] * len(before)
        if held is None:
            held = sum(a.size * a.dtype.itemsize for a in ins if a.dtype != jnp.int32)
            held += sum(math.prod(s) * jnp.dtype(d).itemsize for s, d in tuple(outs) + tuple(scratch))

        def run(*refs):
            body(*refs[:count], *refs[count + len(before) : count + len(before) + len(outs)], *refs[count + len(before) + len(outs) + 1 :])
            refs[count + len(before) + len(outs)][...] = jnp.zeros((8, 128), F32)

        place = pl.ANY if dma else pltpu.VMEM
        scratches = [pltpu.VMEM(s, d) for s, d in scratch]
        if dma:
            scratches.append(pltpu.SemaphoreType.DMA((dma,)))
        result = pl.pallas_call(
            run,
            in_specs=specs,
            out_specs=[pl.BlockSpec(memory_space=place)] * len(outs) + [pl.BlockSpec(memory_space=pltpu.VMEM)],
            out_shape=[jax.ShapeDtypeStruct(s, d) for s, d in outs] + [jax.ShapeDtypeStruct((8, 128), F32)],
            scratch_shapes=scratches,
            input_output_aliases=alias,
            compiler_params=pltpu.CompilerParams(vmem_limit_bytes=int(held * 1.05) + ROOM),
            cost_estimate=pl.CostEstimate(flops=int(cost_of(name) * PACE), bytes_accessed=0, transcendentals=0),
            name=name,
        )(*ins, *before)
        self.token = result[-1]
        return result[:-1]


def clear_range(meta, low, high):
    count = meta.shape[0] - 2
    begin = jnp.int32(0)
    hit = jnp.bool_(False)
    for i in range(count):
        length = meta[1 + i]
        hit = hit | ((length > 0) & (begin >= low) & (begin < high))
        begin = begin + length
    return jnp.where(hit, 0.0, 1.0).astype(F32)


def chunk_masks(meta, first, chunks):
    rows = lax.broadcasted_iota(jnp.int32, (chunks, 128), 0)
    free = jnp.ones((chunks, 128), F32)
    for s in range(0, chunks, SPAN // CHUNK):
        position = first + s * CHUNK
        free = jnp.where(rows == s, clear_range(meta, position, position + 1), free)
    return free


def lanes_of(tile):
    return pl.ds(tile * 128, 128)


def tiled(ref):
    return jnp.concatenate([ref[i] for i in range(ref.shape[0])], axis=1)


def put_tiled(ref, value):
    for i in range(ref.shape[0]):
        ref[i] = value[:, i * 128 : (i + 1) * 128]


def scan_step(masks, values, decay_row, shifts, chunks):
    power = decay_row
    for i, mask in enumerate(masks):
        values = values + power * (mask * pltpu.roll(values, shifts[i], 0))
        power = power * power
    return values


def doubling_masks(mask, chunks, backward):
    masks = []
    distance = 1
    while distance < chunks:
        masks.append(mask)
        shift = chunks - distance if backward else distance
        mask = mask * pltpu.roll(mask, shift, 0)
        distance *= 2
    shifts = []
    distance = 1
    while distance < chunks:
        shifts.append(chunks - distance if backward else distance)
        distance *= 2
    return masks, shifts


def edge_masks(free, chunks, backward):
    rows = lax.broadcasted_iota(jnp.int32, (chunks, 128), 0)
    if backward:
        return jnp.where(rows == chunks - 1, 0.0, pltpu.roll(free, chunks - 1, 0))
    return jnp.where(rows == 0, 0.0, free)


def prefix_mask(free, chunks, backward):
    rows = lax.broadcasted_iota(jnp.int32, (chunks, 128), 0)
    if backward:
        reach = jnp.where(rows == chunks - 1, 1.0, pltpu.roll(free, chunks - 1, 0))
    else:
        reach = free
    distance = 1
    while distance < chunks:
        if backward:
            moved = jnp.where(rows >= chunks - distance, 1.0, pltpu.roll(reach, chunks - distance, 0))
        else:
            moved = jnp.where(rows < distance, 1.0, pltpu.roll(reach, distance, 0))
        reach = reach * moved
        distance *= 2
    return reach


def start_body(meta, tok, gain, delta, alpha, beta, eta, normed, low, enter, end, logk, keep, mix):
    tokens, width = tok.shape
    hidden = delta.shape[0]
    chunks = tokens // CHUNK
    x = tok[...].astype(F32)
    centered = x - jnp.mean(x, axis=1, keepdims=True)
    spread = jnp.mean(centered * centered, axis=1, keepdims=True)
    rows = centered * lax.rsqrt(spread + EPS) * gain[...]
    put_tiled(normed, rows)
    low[...] = rows.astype(BF16)
    share = jax.nn.sigmoid(delta[...])
    log_keep = jnp.log1p(-share * jax.nn.sigmoid(alpha[...]))
    logk[...] = log_keep
    keep[...] = jnp.exp(log_keep)
    mix[...] = share * beta[...] * (eta[...] * (1.0 / math.sqrt(hidden)))
    free = chunk_masks(meta, meta[0] * tokens, chunks)
    edge = edge_masks(free, chunks, False)
    masks, shifts = doubling_masks(edge, chunks, False)
    for tile in range(width // 128):
        lanes = lanes_of(tile)
        keeps = [keep[h : h + 1, lanes] for h in range(hidden)]

        def step(t, state):
            value = normed[tile, pl.ds(t, chunks, stride=CHUNK), :]
            return tuple(k * u + value for k, u in zip(keeps, state))

        zero = jnp.zeros((chunks, 128), F32)
        state = lax.fori_loop(0, CHUNK, step, (zero,) * hidden, unroll=8)
        for h in range(hidden):
            decay = jnp.exp(CHUNK * logk[h : h + 1, lanes])
            reached = scan_step(masks, state[h], decay, shifts, chunks)
            enter[h, :, lanes] = edge * pltpu.roll(reached, 1, 0)
            end[h : h + 1, lanes] = reached[chunks - 1 : chunks]


def values_body(low, weight, values, slope):
    for b in range(weight.shape[1] // 256):
        cols = pl.ds(b * 256, 256)
        raw = mm(low[...], weight[:, cols])
        gate = sigmoid(raw)
        out = raw * gate
        values[:, cols] = out.astype(BF16)
        slope[:, cols] = gate + out * (1.0 - gate)


def add_up(parts):
    while len(parts) > 1:
        parts = [a + b for a, b in zip(parts[::2], parts[1::2])]
    return parts[0]


def local_body(normed, enter, keep, mix, smooth):
    chunks = enter.shape[1]
    hidden = keep.shape[0]
    for tile in range(normed.shape[0]):
        lanes = lanes_of(tile)
        keeps = [keep[h : h + 1, lanes] for h in range(hidden)]
        mixes = [mix[h : h + 1, lanes] for h in range(hidden)]

        def step(t, state):
            place = (tile, pl.ds(t, chunks, stride=CHUNK), slice(None))
            value = normed[place]
            state = tuple(k * u + value for k, u in zip(keeps, state))
            smooth[place] = add_up([c * u for c, u in zip(mixes, state)])
            return state

        lax.fori_loop(0, CHUNK, step, tuple(enter[h, :, lanes] for h in range(hidden)), unroll=8)


def pair_body(backward, tokens, meta, own, other, logk, out):
    core = meta[0] % 2
    first = (meta[0] - core) * tokens
    middle = first + tokens
    decay = jnp.exp(tokens * logk[...])
    if backward:
        reach = clear_range(meta, first + 1, middle + 1)
        near = jnp.where(core == 0, own[...], other[...])
        far = jnp.where(core == 0, other[...], own[...])
    else:
        reach = clear_range(meta, middle, middle + tokens)
        near = jnp.where(core == 0, other[...], own[...])
        far = jnp.where(core == 0, own[...], other[...])
    out[...] = near + (reach * decay) * far


def carry_of(backward, tokens, meta, other, arrived, logk):
    core = meta[0] % 2
    first = (meta[0] - core) * tokens
    span = 2 * tokens
    chip_decay = jnp.exp(span * logk[...])
    total = None
    power = None
    for k, part in enumerate(arrived):
        if backward:
            reach = clear_range(meta, first + span, first + (k + 1) * span + 1)
        else:
            reach = clear_range(meta, first - k * span, first)
        term = part[...] * reach
        if power is not None:
            term = term * power
        total = term if total is None else total + term
        power = chip_decay if power is None else power * chip_decay
    decay = jnp.exp(tokens * logk[...])
    middle = first + tokens
    if backward:
        crossing = clear_range(meta, middle, middle + 1)
        through = clear_range(meta, middle + 1, middle + tokens)
        passed = crossing * (other[...] + (through * decay) * total)
        return jnp.where(core == 0, passed, total)
    through = clear_range(meta, first, middle)
    return jnp.where(core == 0, total, other[...] + (through * decay) * total)


def carried_body(chips, meta, other, *rest):
    arrived = rest[:chips]
    logk, keep, mix, omega, normed, smooth, enter, low, slope, states, carry, extra = rest[chips:]
    tiles, tokens, _ = normed.shape
    hidden = keep.shape[0]
    chunks = tokens // CHUNK
    carry[...] = carry_of(False, tokens, meta, other, arrived, logk)
    free = chunk_masks(meta, meta[0] * tokens, chunks)
    reach = prefix_mask(free, chunks, False)
    offset = (lax.broadcasted_iota(jnp.int32, (chunks, 128), 0) * CHUNK).astype(F32)
    for tile in range(tiles):
        lanes = lanes_of(tile)
        state = []
        for h in range(hidden):
            entry = jnp.exp(offset * logk[h : h + 1, lanes]) * reach
            first = carry[h : h + 1, lanes] * entry
            states[h, :, lanes] = enter[h, :, lanes] + first
            state.append(mix[h : h + 1, lanes] * first)
        keeps = [keep[h : h + 1, lanes] for h in range(hidden)]

        def step(t, state):
            place = pl.ds(t, chunks, stride=CHUNK)
            state = tuple(k * u for k, u in zip(keeps, state))
            extra[place, :] = add_up(list(state))
            return state

        lax.fori_loop(0, CHUNK, step, tuple(state), unroll=8)
        pre = smooth[tile] + extra[...] + omega[:, lanes] * normed[tile]
        gate = sigmoid(pre)
        smoothed = pre * gate
        low[:, lanes] = smoothed.astype(BF16)
        slope[:, lanes] = gate + smoothed * (1.0 - gate)


def layer_grad(weighted, normal, inverse):
    mean_one = jnp.mean(weighted, axis=1, keepdims=True)
    mean_two = jnp.mean(weighted * normal, axis=1, keepdims=True)
    return (weighted - mean_one - normal * mean_two) * inverse


def shift_rows(table, down):
    size = table.shape[0]
    rows = lax.broadcasted_iota(jnp.int32, table.shape, 0)
    bit = 1
    while bit < size:
        moved = pltpu.roll(table, bit if down else size - bit, 1)
        table = jnp.where((rows & bit) != 0, moved, table)
        bit *= 2
    return table


def mix_body(low, mix_weight, qk_gain, qk_bias, update, candidate, reset, queries, keys, shared, shared_slope):
    width = update.shape[1]
    base = width + shared.shape[1]
    top = base + reset.shape[1]
    raw = mm(low[...], mix_weight[:, width:base])
    gate = sigmoid(raw)
    silu = raw * gate
    shared[...] = silu
    shared_slope[...] = gate + silu * (1.0 - gate)
    queries[...] = (silu * qk_gain[0:1] + qk_bias[0:1]).astype(BF16)
    keys[...] = (silu * qk_gain[1:2] + qk_bias[1:2]).astype(BF16)
    for b in range(width // 256):
        update[:, b * 256 : (b + 1) * 256] = sigmoid(mm(low[...], mix_weight[:, b * 256 : (b + 1) * 256]))
    for b in range(reset.shape[1] // 256):
        reset[:, b * 256 : (b + 1) * 256] = mm(low[...], mix_weight[:, base + b * 256 : base + (b + 1) * 256])
    for b in range(width // 256):
        candidate[:, b * 256 : (b + 1) * 256] = mm(low[...], mix_weight[:, top + b * 256 : top + (b + 1) * 256])


def attend_body(queries, keys, values, rel_rev, reset, weights, attended, gated):
    tokens, shared_width = queries.shape
    place = lax.broadcasted_iota(jnp.int32, (SPAN, SPAN), 0)
    causal = place >= lax.broadcasted_iota(jnp.int32, (SPAN, SPAN), 1)
    bias = shift_rows(jnp.broadcast_to(rel_rev[...], (SPAN, SPAN)), True)
    scale = 1.0 / math.sqrt(shared_width)
    for s in range(tokens // SPAN):
        rows = pl.ds(s * SPAN, SPAN)
        scores = mm_nt(queries[rows, :], keys[rows, :]) * scale + bias
        scores = jnp.where(causal, scores, -1e30)
        powers = jnp.exp(scores - jnp.max(scores, axis=1, keepdims=True))
        share = powers / jnp.sum(powers, axis=1, keepdims=True)
        weights[rows, :] = share
        rise = mm(share.astype(BF16), values[rows, :])
        attended[rows, :] = rise
        raw = reset[rows, :]
        gated[rows, :] = (raw * sigmoid(raw) * rise).astype(BF16)


def hidden_body(
    gated, out_weight, candidate, update, tok, gain2, residual, change, slope_hidden, normal2, inverse2, low2
):
    total = candidate[...] + mm(gated[...], out_weight[...])
    gate = sigmoid(total)
    hidden_rows = total * gate
    slope_hidden[...] = gate + hidden_rows * (1.0 - gate)
    x = tok[...].astype(F32)
    moved = hidden_rows - x
    change[...] = moved
    rows = x + update[...] * moved
    residual[...] = rows
    centered = rows - jnp.mean(rows, axis=1, keepdims=True)
    inverse = lax.rsqrt(jnp.mean(centered * centered, axis=1, keepdims=True) + EPS)
    normal = centered * inverse
    normal2[...] = normal
    inverse2[...] = jnp.broadcast_to(inverse, inverse2.shape)
    low2[...] = (normal * gain2[...]).astype(BF16)


def expand_body(low2, ffn_in, expanded, slope_exp):
    for b in range(ffn_in.shape[1] // 256):
        cols = pl.ds(b * 256, 256)
        raw = mm(low2[...], ffn_in[:, cols])
        gate = sigmoid(raw)
        silu = raw * gate
        expanded[:, cols] = silu.astype(BF16)
        slope_exp[:, cols] = gate + silu * (1.0 - gate)


def weights_body(parts, meta, *refs):
    kept, sent = refs[-2:]
    pairs = refs[:-2]
    half = kept.shape[0]
    core = meta[0] % 2
    for target, side in ((sent, 1 - core), (kept, core)):
        for i, (column, block) in enumerate(parts):
            left, right = pairs[2 * i], pairs[2 * i + 1]
            begin = pl.multiple_of(side * half + block, 128)
            target[:, column : column + right.shape[1]] = mm_tn(left[:, pl.ds(begin, half)], right[...])


def block_body(residual, expanded, ffn_out, out):
    out[...] = residual[...] + mm(expanded[...], ffn_out[...])


def expand_back_body(cot, ffn_out, slope_exp, expand_grad):
    for b in range(ffn_out.shape[0] // 256):
        cols = pl.ds(b * 256, 256)
        expand_grad[:, cols] = (mm_nt(cot[...], ffn_out[cols, :]) * slope_exp[:, cols]).astype(BF16)


def hidden_back_body(
    expand_grad,
    ffn_in,
    normal2,
    inverse2,
    gain2,
    cot,
    update,
    change,
    slope_hidden,
    input_part,
    update_grad,
    out_grad,
    gain2_grad,
):
    norm_out = mm_nt(expand_grad[...], ffn_in[...])
    normal = normal2[...]
    gain2_grad[...] = jnp.sum(norm_out * normal, axis=0, keepdims=True)
    upstream = cot[...].astype(F32) + layer_grad(norm_out * gain2[...], normal, inverse2[:, 0:1])
    gates = update[...]
    input_part[...] = upstream * (1.0 - gates)
    update_grad[...] = (upstream * change[...] * gates * (1.0 - gates)).astype(BF16)
    out_grad[...] = (upstream * gates * slope_hidden[...]).astype(BF16)


def reset_back_body(out_grad, out_weight, reset, attended, reset_grad, attend_grad):
    for b in range(reset.shape[1] // 256):
        cols = pl.ds(b * 256, 256)
        rise = mm_nt(out_grad[...], out_weight[cols, :])
        raw = reset[:, cols]
        gate = sigmoid(raw)
        silu = raw * gate
        reset_grad[:, cols] = (rise * attended[:, cols] * (gate + silu * (1.0 - gate))).astype(BF16)
        attend_grad[:, cols] = (rise * silu).astype(BF16)


def attend_back_body(
    attend_grad,
    weights,
    queries,
    keys,
    shared,
    shared_slope,
    values,
    values_slope,
    qk_gain,
    value_grad,
    shared_grad,
    small,
):
    tokens, shared_width = queries.shape
    scale = 1.0 / math.sqrt(shared_width)
    slopes = jnp.zeros((SPAN, SPAN), F32)
    for s in range(tokens // SPAN):
        rows = pl.ds(s * SPAN, SPAN)
        upstream = attend_grad[rows, :]
        share = weights[rows, :]
        rise = mm_nt(upstream, values[rows, :])
        value_rise = mm_tn(share.astype(BF16), upstream)
        value_grad[rows, :] = (value_rise * values_slope[rows, :]).astype(BF16)
        score_grad = share * (rise - jnp.sum(share * rise, axis=1, keepdims=True))
        slopes = slopes + score_grad
        low = (score_grad * scale).astype(BF16)
        query_grad = mm(low, keys[rows, :])
        key_grad = mm_tn(low, queries[rows, :])
        silu = shared[rows, :]
        pieces = (
            jnp.sum(query_grad * silu, axis=0, keepdims=True),
            jnp.sum(key_grad * silu, axis=0, keepdims=True),
            jnp.sum(query_grad, axis=0, keepdims=True),
            jnp.sum(key_grad, axis=0, keepdims=True),
        )
        sums = pieces if s == 0 else tuple(a + b for a, b in zip(sums, pieces))
        back = query_grad * qk_gain[0:1] + key_grad * qk_gain[1:2]
        shared_grad[rows, :] = (back * shared_slope[rows, :]).astype(BF16)
    small[...] = jnp.zeros_like(small)
    for i in range(4):
        small[i : i + 1, :] = sums[i]
    small[4:5, :] = jnp.sum(shift_rows(slopes, False), axis=0, keepdims=True)


def smooth_back_body(
    update_grad,
    shared_grad,
    reset_grad,
    out_grad,
    value_grad,
    mix_weight,
    value_weight,
    slope_pre,
    normed,
    omega,
    smooth_grad,
    norm_grad,
    omega_grad,
):
    width = update_grad.shape[1]
    base = width + shared_grad.shape[1]
    top = base + reset_grad.shape[1]
    rise = mm_nt(reset_grad[...], mix_weight[:, base:top])
    rise = rise + mm_nt(update_grad[...], mix_weight[:, :width])
    rise = rise + mm_nt(out_grad[...], mix_weight[:, top:])
    rise = rise + mm_nt(shared_grad[...], mix_weight[:, width:base])
    grad = rise * slope_pre[...]
    put_tiled(smooth_grad, grad)
    put_tiled(norm_grad, mm_nt(value_grad[...], value_weight[...]) + omega[...] * grad)
    omega_grad[...] = jnp.sum(grad * tiled(normed), axis=0, keepdims=True)


def rise_body(meta, smooth_grad, logk, keep, enter, end):
    tiles, tokens, _ = smooth_grad.shape
    hidden = keep.shape[0]
    chunks = tokens // CHUNK
    free = chunk_masks(meta, meta[0] * tokens, chunks)
    edge = edge_masks(free, chunks, True)
    masks, shifts = doubling_masks(edge, chunks, True)
    for tile in range(tiles):
        lanes = lanes_of(tile)
        keeps = [keep[h : h + 1, lanes] for h in range(hidden)]

        def step(t, state):
            value = smooth_grad[tile, pl.ds(CHUNK - 1 - t, chunks, stride=CHUNK), :]
            return tuple(k * u + value for k, u in zip(keeps, state))

        zero = jnp.zeros((chunks, 128), F32)
        state = lax.fori_loop(0, CHUNK, step, (zero,) * hidden, unroll=8)
        for h in range(hidden):
            decay = jnp.exp(CHUNK * logk[h : h + 1, lanes])
            reached = scan_step(masks, state[h], decay, shifts, chunks)
            enter[h, :, lanes] = edge * pltpu.roll(reached, chunks - 1, 0)
            end[h : h + 1, lanes] = reached[0:1]


def carry_back_body(chips, meta, other, *rest):
    arrived = rest[:chips]
    logk, enter, later = rest[chips:]
    hidden, chunks, width = enter.shape
    tokens = chunks * CHUNK
    carry = carry_of(True, tokens, meta, other, arrived, logk)
    free = chunk_masks(meta, meta[0] * tokens, chunks)
    reach = prefix_mask(free, chunks, True)
    offset = ((chunks - 1 - lax.broadcasted_iota(jnp.int32, (chunks, 128), 0)) * CHUNK).astype(F32)
    for tile in range(width // 128):
        lanes = lanes_of(tile)
        for h in range(hidden):
            entry = jnp.exp(offset * logk[h : h + 1, lanes]) * reach
            later[h, :, lanes] = enter[h, :, lanes] + carry[h : h + 1, tile * 128 : (tile + 1) * 128] * entry


def state_back_body(tile, normed, smooth_grad, norm_grad, states, later, keep, mix, total, sums, history):
    hidden = keep.shape[0]
    chunks = states.shape[1]
    lanes = lanes_of(tile)
    heads = range(hidden)
    keeps = [keep[h : h + 1, lanes] for h in heads]
    mixes = [mix[h : h + 1, lanes] for h in heads]

    def rise(t, state):
        value = normed[tile, pl.ds(t, chunks, stride=CHUNK), :]
        state = tuple(k * u + value for k, u in zip(keeps, state))
        for i in heads:
            history[t, i] = state[i]
        return state

    lax.fori_loop(0, CHUNK, rise, tuple(states[h, :, lanes] for h in heads), unroll=4)

    def fall(i, held):
        state, reads, marks = held
        t = CHUNK - 1 - i
        place = pl.ds(t, chunks, stride=CHUNK)
        value = smooth_grad[tile, place, :]
        row = normed[tile, place, :]
        state = tuple(k * w + value for k, w in zip(keeps, state))
        reads = tuple(r + w * row for r, w in zip(reads, state))
        marks = tuple(m + w * history[t, j] for j, (m, w) in enumerate(zip(marks, state)))
        total[place, :] = norm_grad[tile, place, :] + add_up([c * w for c, w in zip(mixes, state)])
        return state, reads, marks

    zeros = (jnp.zeros((chunks, 128), F32),) * hidden
    first = tuple(later[h, :, lanes] for h in heads)
    _, reads, marks = lax.fori_loop(0, CHUNK, fall, (first, zeros, zeros), unroll=4)
    for h in heads:
        sums[h : h + 1, :] = jnp.sum(reads[h], axis=0, keepdims=True)
        sums[hidden + h : hidden + h + 1, :] = jnp.sum(marks[h], axis=0, keepdims=True)


def close_body(count, *refs):
    totals = refs[:count]
    sums = refs[count : 2 * count]
    tok, gain, input_part, omega_grad, gain2_grad, small, input_grad, packed = refs[2 * count :]
    x = tok[...].astype(F32)
    centered = x - jnp.mean(x, axis=1, keepdims=True)
    inverse = lax.rsqrt(jnp.mean(centered * centered, axis=1, keepdims=True) + EPS)
    normal = centered * inverse
    upstream = jnp.concatenate([t[...] for t in totals], axis=1)
    input_grad[...] = input_part[...] + layer_grad(upstream * gain[...], normal, inverse)
    at = sums[0].shape[0]
    for i in range(count):
        packed[0:at, i * 128 : (i + 1) * 128] = sums[i][...]
    packed[at : at + 8, :] = jnp.zeros((8, x.shape[1]), F32)
    packed[at : at + 1, :] = jnp.sum(upstream * normal, axis=0, keepdims=True)
    packed[at + 1 : at + 2, :] = gain2_grad[...]
    packed[at + 2 : at + 3, :] = omega_grad[...]
    for i in range(5):
        packed[at + 3 + i : at + 4 + i, 0 : small.shape[1]] = small[i : i + 1, :]


def finish_body(packed, delta, alpha, beta, eta, delta_grad, alpha_grad, beta_grad, eta_grad):
    hidden = delta.shape[0]
    scale = 1.0 / math.sqrt(hidden)
    read = packed[0:hidden, :]
    mark = packed[hidden : 2 * hidden, :]
    share = jax.nn.sigmoid(delta[...])
    damp = jax.nn.sigmoid(alpha[...])
    inflow = share * beta[...]
    outflow = eta[...] * scale
    eta_grad[...] = inflow * read * scale
    inflow_grad = outflow * read
    beta_grad[...] = share * inflow_grad
    rate = inflow * outflow * (mark - read) / (share * damp - 1.0)
    share_grad = beta[...] * inflow_grad + damp * rate
    delta_grad[...] = share_grad * share * (1.0 - share)
    alpha_grad[...] = share * rate * damp * (1.0 - damp)


def swap(a, axis, bit):
    count = lax.axis_size(axis)
    return lax.ppermute(a, axis, [(i, i ^ bit) for i in range(count)])


def chip_parts(state, backward):
    count = lax.axis_size("seq")
    parts = []
    for k in range(1, count // 2):
        if backward:
            moves = [(i, i - 2 * k) for i in range(2 * k, count)]
        else:
            moves = [(i, i + 2 * k) for i in range(count - 2 * k)]
        parts.append(lax.ppermute(state, "seq", moves))
    return parts


def axis_bits(axis, least):
    bits = []
    bit = least
    while bit < lax.axis_size(axis):
        bits.append((axis, bit))
        bit *= 2
    return bits


def cross(a, step):
    seq = lax.axis_size("seq")
    moves = []
    for i in range(lax.axis_size("dp") * seq):
        axis, bit = step[i % 2]
        moves.append((i, i ^ (bit * seq if axis == "dp" else bit)))
    return lax.ppermute(a, ("dp", "seq"), moves)


ROUTES = (
    (("xy1", "yx1"), "2"),
    (("xy1", "yx1"), "2"),
    (("1xy", "1yx"), "2"),
    (("xy1", "yx1"), "2"),
    (("xy1", "yx1"), "2"),
)
ORDER = "0KK3014K0231KK0412034201K3K04K21032413K24K3KK41K312K34K24"
BITS = {"x": ("dp", 1), "y": ("dp", 2), "1": ("seq", 2), "2": ("seq", 4)}


def route(halving, doubling):
    named = lambda pair: all(BITS[c][1] < lax.axis_size(BITS[c][0]) for c in pair)
    halves = [tuple(BITS[c] for c in pair) for pair in zip(*halving) if named(pair)]
    wholes = [(BITS[c], BITS[c]) for c in doubling if named(c)]
    for bit in axis_bits("dp", 1) + axis_bits("seq", 2):
        if bit not in BITS.values():
            halves.append((bit, bit))
    return halves, wholes


def masks_body(steps, meta, out):
    for i, step in enumerate(steps):
        place = [(meta[0] if axis == "seq" else meta[meta.shape[0] - 1]) // bit % 2 for axis, bit in step]
        side = jnp.where(meta[0] % 2 == 0, place[0], place[1])
        out[i] = jnp.full((8, 128), side.astype(F32))


def split_body(index, masks, kept, arrived, keep, send):
    half = keep.shape[0]
    upper = masks[index, 0:1, 0:1] > 0.5
    low = kept[:half, :] + arrived[:half, :]
    high = kept[half:, :] + arrived[half:, :]
    keep[...] = jnp.where(upper, high, low)
    send[...] = jnp.where(upper, low, high)


def sum_body(kept, arrived, out):
    out[...] = kept[...] + arrived[...]


def join_body(index, masks, own, other, out):
    half = own.shape[0]
    upper = masks[index, 0:1, 0:1] > 0.5
    out[:half, :] = jnp.where(upper, other[...], own[...])
    out[half:, :] = jnp.where(upper, own[...], other[...])


class Piece:
    def __init__(self, line, masks, steps, kept, sent, routes, outputs, name):
        self.line, self.masks, self.steps, self.name = line, masks, steps, name
        self.outputs = outputs
        self.work = self.run(kept, sent, *routes)
        self.done = False
        self.advance()

    def advance(self):
        if not self.done:
            self.done = next(self.work, "end") == "end"

    def run(self, kept, sent, halves, wholes):
        line, masks = self.line, self.masks
        arrived = swap(sent, "seq", 1)
        yield
        for step in halves:
            rows, cols = kept.shape
            kept, send = line(
                lambda *refs, index=self.steps.index(step): split_body(index, *refs),
                (masks, kept, arrived),
                [((rows // 2, cols), F32)] * 2,
                name=self.name + "_split",
            )
            arrived = cross(send, step)
            yield
        for step in wholes:
            kept = line(sum_body, (kept, arrived), [(kept.shape, F32)], name=self.name + "_sum")[0]
            arrived = cross(kept, step)
            yield
        part = line(sum_body, (kept, arrived), [(kept.shape, F32)], name=self.name + "_sum")[0]
        for i, step in enumerate(reversed(halves)):
            other = cross(part, step)
            yield
            rows, cols = part.shape
            part = line(
                lambda *refs, index=self.steps.index(step): join_body(index, *refs),
                (masks, part, other),
                [((2 * rows, cols), F32)],
                name=self.name + "_join",
            )[0]
        other = swap(part, "seq", 1)
        self.outputs(part, False)
        yield
        self.outputs(other, True)


def place_body(plans, far, count, meta, part, *refs):
    outs = refs[count : count + len(plans)]
    sems = refs[-1]
    side = meta[0] % 2
    side = 1 - side if far else side
    rows = part.shape[0]
    copies = []
    for out, plan in zip(outs, plans):
        for column, width, row, place in plan:
            begin = pl.multiple_of(side * rows + row, 8)
            copies.append(
                pltpu.make_async_copy(
                    part.at[:, pl.ds(column, width)],
                    out.at[pl.ds(begin, rows), pl.ds(place, width)],
                    sems.at[len(copies)],
                )
            )
            copies[-1].start()
    for copy in copies:
        copy.wait()


class Outputs:
    def __init__(self, line, meta, shapes):
        self.line, self.meta, self.shapes, self.arrays = line, meta, shapes, {}

    def placer(self, plans, name):
        def place(part, far):
            names = list(plans)
            held = [n for n in names if n in self.arrays]
            alias = {2 + i: names.index(n) for i, n in enumerate(held)}
            results = self.line(
                lambda *refs: place_body(list(plans.values()), far, len(held), *refs),
                (self.meta, part, *[self.arrays[n] for n in held]),
                [(self.shapes[n], F32) for n in names],
                name=name + "_out",
                held=part.size * 4,
                alias=alias,
                dma=sum(len(p) for p in plans.values()),
            )
            self.arrays.update(zip(names, results))

        return place


def shards(
    tokens,
    cotangent,
    seq_lengths,
    norm1_gain,
    value_weight,
    ema_delta,
    ema_alpha,
    ema_beta,
    ema_eta,
    ema_omega,
    mix_weight,
    qk_gain,
    qk_bias,
    rel_bias,
    out_weight,
    norm2_gain,
    ffn_in,
    ffn_out,
):
    rows, width = tokens.shape
    hidden = ema_delta.shape[1]
    chunks = rows // CHUNK
    value_width = value_weight.shape[1]
    inner = ffn_in.shape[1]
    mixed = mix_weight.shape[1]
    shared_width = qk_gain.shape[1]
    places = jnp.stack([lax.axis_index("seq"), lax.axis_index("dp")]).astype(jnp.int32)
    meta = jnp.concatenate([places[:1], seq_lengths[0], places[1:]])
    gain1 = norm1_gain[None]
    gain2 = norm2_gain[None]
    omega = ema_omega[None]
    rel_rev = jnp.roll(rel_bias[::-1], 1)[None]
    ema = (ema_delta.T, ema_alpha.T, ema_beta.T, ema_eta.T)
    full = (rows, width)
    wide = (rows, value_width)
    thin = (rows, shared_width)
    tiles = (width // 128, rows, 128)
    state = (hidden, width)
    states = (hidden, chunks, width)
    line = Line()

    normed, low_normed, enter, end, logk, keep, mix = line(
        start_body,
        (meta, tokens, gain1, *ema),
        [(tiles, F32), (full, BF16), (states, F32), (state, F32), (state, F32), (state, F32), (state, F32)],
        name="norm_and_states",
    )
    other = swap(end, "seq", 1)
    chip_end = line(
        lambda *refs: pair_body(False, rows, *refs), (meta, end, other, logk), [(state, F32)], name="chip_state"
    )[0]
    arrived = chip_parts(chip_end, False)
    routes = [route(halving, doubling) for halving, doubling in ROUTES]
    steps = sorted({step for halves, wholes in routes for step in halves})
    masks = line(lambda *refs: masks_body(steps, *refs), (meta,), [((len(steps), 8, 128), F32)], name="masks")[0]
    values, values_slope = line(values_body, (low_normed, value_weight), [(wide, BF16), (wide, F32)], name="values")
    smooth = line(local_body, (normed, enter, keep, mix), [(tiles, F32)], name="local_average")[0]
    low_smoothed, slope_pre, entering = line(
        lambda *refs: carried_body(len(arrived), *refs),
        (meta, other, *arrived, logk, keep, mix, omega, normed, smooth, enter),
        [(full, BF16), (full, F32), (states, F32)],
        scratch=[(state, F32), ((rows, 128), F32)],
        name="carried_average",
    )
    update, candidate, reset, queries, keys, shared, shared_slope = line(
        mix_body,
        (low_smoothed, mix_weight, qk_gain, qk_bias),
        [(full, F32), (full, F32), (wide, F32), (thin, BF16), (thin, BF16), (thin, F32), (thin, F32)],
        name="mix",
    )
    weights, attended, gated = line(
        attend_body,
        (queries, keys, values, rel_rev, reset),
        [((rows, SPAN), F32), (wide, F32), (wide, BF16)],
        name="attention",
    )
    residual, change, slope_hidden, normal2, inverse2, low2 = line(
        hidden_body,
        (gated, out_weight, candidate, update, tokens, gain2),
        [(full, F32), (full, F32), (full, F32), (full, F32), ((rows, 128), F32), (full, BF16)],
        name="hidden",
    )
    expanded, slope_exp = line(
        expand_body, (low2, ffn_in), [((rows, inner), BF16), ((rows, inner), F32)], name="expand"
    )
    half = width // 2
    outputs = Outputs(
        line,
        meta,
        {
            "ffn_out": (inner, width),
            "ffn_in": (width, inner),
            "out": (value_width, width),
            "mix": (width, mixed),
            "value": (width, value_width),
        },
    )
    pieces = []

    def start_piece(parts, pairs, height, cols, plans, name):
        kept, sent = line(
            lambda *refs: weights_body(parts, *refs),
            (meta, *[a for pair in pairs for a in pair]),
            [((height, cols), F32)] * 2,
            name=name + "_grad",
        )
        pieces.append(
            Piece(line, masks, steps, kept, sent, routes[len(pieces)], outputs.placer(plans, name), name)
        )

    def step(*which):
        for i in which:
            pieces[i].advance()

    start_piece(
        [(0, 0)], [(expanded, cotangent)], inner // 2, width, {"ffn_out": [(0, width, 0, 0)]}, "ffn_out"
    )
    expand_grad = line(
        expand_back_body, (cotangent, ffn_out, slope_exp), [((rows, inner), BF16)], name="expand_back"
    )[0]
    step(0)
    input_part, update_grad, out_grad, gain2_grad = line(
        hidden_back_body,
        (expand_grad, ffn_in, normal2, inverse2, gain2, cotangent, update, change, slope_hidden),
        [(full, F32), (full, BF16), (full, BF16), ((1, width), F32)],
        name="hidden_back",
    )
    start_piece(
        [(0, 0), (inner, 0)],
        [(low2, expand_grad), (low_smoothed, update_grad)],
        half,
        inner + width,
        {"ffn_in": [(0, inner, 0, 0)], "mix": [(inner, width, 0, 0)]},
        "ffn_in",
    )
    start_piece(
        [(0, 0), (width, width), (2 * width, 0)],
        [(gated, out_grad), (gated, out_grad), (low_smoothed, out_grad)],
        half,
        3 * width,
        {
            "out": [(0, width, 0, 0), (width, width, width, 0)],
            "mix": [(2 * width, width, 0, width + shared_width + value_width)],
        },
        "out",
    )
    step(1)
    reset_grad, attend_grad = line(
        reset_back_body, (out_grad, out_weight, reset, attended), [(wide, BF16)] * 2, name="reset_back"
    )
    step(2)
    value_grad, shared_grad, small = line(
        attend_back_body,
        (attend_grad, weights, queries, keys, shared, shared_slope, values, values_slope, qk_gain),
        [(wide, BF16), (thin, BF16), ((8, shared_width), F32)],
        name="attention_back",
    )
    start_piece(
        [(0, 0)],
        [(low_smoothed, reset_grad)],
        half,
        value_width,
        {"mix": [(0, value_width, 0, width + shared_width)]},
        "reset",
    )
    start_piece(
        [(0, 0), (value_width, 0)],
        [(low_normed, value_grad), (low_smoothed, shared_grad)],
        half,
        value_width + shared_width,
        {"value": [(0, value_width, 0, 0)], "mix": [(value_width, shared_width, 0, width)]},
        "value",
    )

    def rest():
        smooth_grad, norm_grad, omega_grad = line(
            smooth_back_body,
            (update_grad, shared_grad, reset_grad, out_grad, value_grad, mix_weight, value_weight, slope_pre)
            + (normed, omega),
            [(tiles, F32), (tiles, F32), ((1, width), F32)],
            name="smooth_back",
        )
        yield
        later, begin = line(
            rise_body, (meta, smooth_grad, logk, keep), [(states, F32), (state, F32)], name="states_back"
        )
        other_begin = swap(begin, "seq", 1)
        yield
        chip_begin = line(
            lambda *refs: pair_body(True, rows, *refs),
            (meta, begin, other_begin, logk),
            [(state, F32)],
            name="chip_grad",
        )[0]
        returned = chip_parts(chip_begin, True)
        yield
        later = line(
            lambda *refs: carry_back_body(len(returned), *refs),
            (meta, other_begin, *returned, logk, later),
            [(states, F32)],
            name="carry_back",
        )[0]
        yield
        backs = []
        for tile in range(width // 128):
            backs.append(
                line(
                    lambda *refs, tile=tile: state_back_body(tile, *refs),
                    (normed, smooth_grad, norm_grad, entering, later, keep, mix),
                    [((rows, 128), F32), ((2 * hidden, 128), F32)],
                    scratch=[((CHUNK, hidden, chunks, 128), F32)],
                    name="state_back",
                )
            )
            yield
        input_grad, packed = line(
            lambda *refs: close_body(len(backs), *refs),
            (*[b[0] for b in backs], *[b[1] for b in backs], tokens, gain1, input_part, omega_grad, gain2_grad, small),
            [(full, F32), ((2 * hidden + 8, width), F32)],
            name="norm_back",
        )
        results["input_grad"] = input_grad
        for axis, bit in axis_bits("seq", 1) + axis_bits("dp", 1):
            moved = swap(packed, axis, bit)
            yield
            packed = line(sum_body, (packed, moved), [(packed.shape, F32)], name="small_sum")[0]
        results["packed"] = packed
        results["ema"] = line(finish_body, (packed, *ema), [(state, F32)] * 4, name="state_parameters")
        yield
        results["block_out"] = line(block_body, (residual, expanded, ffn_out), [(full, F32)], name="block_out")[0]

    results = {}
    work = rest()
    for item in ORDER:
        if item == "K":
            next(work, None)
        else:
            step(int(item))
    for _ in work:
        pass
    while not all(p.done for p in pieces):
        step(*range(len(pieces)))
    packed = results["packed"]
    at = 2 * hidden
    tail = packed[at + 3 :, :shared_width]
    sums = outputs.arrays
    return (
        results["block_out"],
        results["input_grad"],
        packed[at],
        sums["value"],
        *[g.T for g in results["ema"]],
        packed[at + 2],
        sums["mix"],
        tail[0:2],
        tail[2:4],
        jnp.roll(tail[4][::-1], 1),
        sums["out"],
        packed[at + 1],
        sums["ffn_in"],
        sums["ffn_out"],
    )


def solution(mesh):
    rows = P(("dp", "seq"), None)
    in_specs = (rows, rows, P("dp", None)) + (P(),) * 15
    out_specs = (rows, rows) + (P(),) * 15
    return jax.shard_map(shards, mesh=mesh, in_specs=in_specs, out_specs=out_specs, check_vma=False)
```

```python
import math

import jax
import jax.numpy as jnp
from jax import lax
from jax.experimental import pallas as pl
from jax.experimental.pallas import tpu as pltpu
from jax.sharding import PartitionSpec as P

SPAN = 128
CHUNK = 64
EPS = 1e-05
BF16 = jnp.bfloat16
F32 = jnp.float32
ROOM = 2 * 1024 * 1024
SWAPS = 1
SMALL_ROWS = 24


def sigmoid(a):
    return 0.5 * jnp.tanh(0.5 * a) + 0.5


def mm(a, b):
    return lax.dot_general(a, b, (((1,), (0,)), ((), ())), preferred_element_type=F32)


def mm_nt(a, b):
    return lax.dot_general(a, b, (((1,), (1,)), ((), ())), preferred_element_type=F32)


def mm_tn(a, b):
    return lax.dot_general(a, b, (((0,), (0,)), ((), ())), preferred_element_type=F32)


class Place:
    def __init__(self, lengths):
        self.lengths = lengths
        self.shape = (lengths.shape[1] + 2,)

    def __getitem__(self, i):
        if i == 0:
            return lax.axis_index("seq")
        return self.lengths[0, i - 1]


class Line:
    def __init__(self, paces):
        self.token = None
        self.paces = paces
        self.count = 0

    def __call__(self, body, ins, outs, scratch=(), name=None, held=None, left=(), alias=None, out_left=0, dma=0):
        count = len(ins)
        before = () if self.token is None else (self.token,)
        alias = alias or {}
        specs = []
        for i, a in enumerate(ins):
            if i in left:
                specs.append(pl.BlockSpec(memory_space=pltpu.HBM))
            elif i in alias:
                specs.append(pl.BlockSpec(memory_space=pl.ANY))
            else:
                specs.append(pl.BlockSpec(memory_space=pltpu.SMEM if a.dtype == jnp.int32 else pltpu.VMEM))
        specs += [pl.BlockSpec(memory_space=pl.ANY)] * len(before)
        if held is None:
            held = sum(a.size * a.dtype.itemsize for a in ins if a.dtype != jnp.int32)
            held += sum(math.prod(s) * jnp.dtype(d).itemsize for s, d in tuple(outs) + tuple(scratch))
        first = count + len(before)

        def run(*refs):
            body(*refs[:count], *refs[first : first + len(outs)], *refs[first + len(outs) + 1 :])
            refs[first + len(outs)][...] = jnp.zeros((8, 128), F32)

        places = [pl.ANY if i < out_left else pltpu.VMEM for i in range(len(outs))]
        scratches = [pltpu.VMEM(s, d) for s, d in scratch]
        if dma:
            scratches.append(pltpu.SemaphoreType.DMA((dma,)))
        pace = self.paces[self.count] if self.count < len(self.paces) else 0
        self.count += 1
        result = pl.pallas_call(
            run,
            in_specs=specs,
            out_specs=[pl.BlockSpec(memory_space=m) for m in places + [pltpu.VMEM]],
            out_shape=[jax.ShapeDtypeStruct(s, d) for s, d in outs] + [jax.ShapeDtypeStruct((8, 128), F32)],
            scratch_shapes=scratches,
            input_output_aliases=alias,
            compiler_params=pltpu.CompilerParams(vmem_limit_bytes=int(held * 1.05) + ROOM),
            cost_estimate=pl.CostEstimate(flops=int(pace * 1e9), bytes_accessed=0, transcendentals=0),
            name=name,
        )(*ins, *before)
        self.token = result[-1]
        return result[:-1]


def clear_range(meta, low, high):
    count = meta.shape[0] - 2
    begin = jnp.int32(0)
    hit = jnp.bool_(False)
    for i in range(count):
        length = meta[1 + i]
        hit = hit | ((length > 0) & (begin >= low) & (begin < high))
        begin = begin + length
    return jnp.where(hit, 0.0, 1.0).astype(F32)


def chunk_masks(meta, first, chunks):
    rows = lax.broadcasted_iota(jnp.int32, (chunks, 128), 0)
    free = jnp.ones((chunks, 128), F32)
    for s in range(0, chunks, SPAN // CHUNK):
        position = first + s * CHUNK
        free = jnp.where(rows == s, clear_range(meta, position, position + 1), free)
    return free


def lanes_of(tile):
    return pl.ds(tile * 128, 128)


def tiled(ref):
    return jnp.concatenate([ref[i] for i in range(ref.shape[0])], axis=1)


def put_tiled(ref, value):
    for i in range(ref.shape[0]):
        ref[i] = value[:, i * 128 : (i + 1) * 128]


def scan_step(masks, values, decay_row, shifts, chunks):
    power = decay_row
    for i, mask in enumerate(masks):
        values = values + power * (mask * pltpu.roll(values, shifts[i], 0))
        power = power * power
    return values


def doubling_masks(mask, chunks, backward):
    masks = []
    distance = 1
    while distance < chunks:
        masks.append(mask)
        shift = chunks - distance if backward else distance
        mask = mask * pltpu.roll(mask, shift, 0)
        distance *= 2
    shifts = []
    distance = 1
    while distance < chunks:
        shifts.append(chunks - distance if backward else distance)
        distance *= 2
    return masks, shifts


def edge_masks(free, chunks, backward):
    rows = lax.broadcasted_iota(jnp.int32, (chunks, 128), 0)
    if backward:
        return jnp.where(rows == chunks - 1, 0.0, pltpu.roll(free, chunks - 1, 0))
    return jnp.where(rows == 0, 0.0, free)


def prefix_mask(free, chunks, backward):
    rows = lax.broadcasted_iota(jnp.int32, (chunks, 128), 0)
    if backward:
        reach = jnp.where(rows == chunks - 1, 1.0, pltpu.roll(free, chunks - 1, 0))
    else:
        reach = free
    distance = 1
    while distance < chunks:
        if backward:
            moved = jnp.where(rows >= chunks - distance, 1.0, pltpu.roll(reach, chunks - distance, 0))
        else:
            moved = jnp.where(rows < distance, 1.0, pltpu.roll(reach, distance, 0))
        reach = reach * moved
        distance *= 2
    return reach


def start_body(lengths, tok, gain, logk, keep, normed, low, enter, end):
    meta = Place(lengths)
    tokens, width = tok.shape
    hidden = end.shape[0]
    chunks = tokens // CHUNK
    x = tok[...].astype(F32)
    centered = x - jnp.mean(x, axis=1, keepdims=True)
    spread = jnp.mean(centered * centered, axis=1, keepdims=True)
    rows = centered * lax.rsqrt(spread + EPS) * gain[0:1, :]
    put_tiled(normed, rows)
    low[...] = rows.astype(BF16)
    free = chunk_masks(meta, meta[0] * tokens, chunks)
    edge = edge_masks(free, chunks, False)
    masks, shifts = doubling_masks(edge, chunks, False)
    for tile in range(width // 128):
        lanes = lanes_of(tile)
        keeps = [keep[h : h + 1, lanes] for h in range(hidden)]

        def step(t, state):
            value = normed[tile, pl.ds(t, chunks, stride=CHUNK), :]
            return tuple(k * u + value for k, u in zip(keeps, state))

        zero = jnp.zeros((chunks, 128), F32)
        state = lax.fori_loop(0, CHUNK, step, (zero,) * hidden, unroll=8)
        for h in range(hidden):
            decay = jnp.exp(CHUNK * logk[h : h + 1, lanes])
            reached = scan_step(masks, state[h], decay, shifts, chunks)
            enter[h, :, lanes] = edge * pltpu.roll(reached, 1, 0)
            end[h : h + 1, lanes] = reached[chunks - 1 : chunks]


def values_body(low, weight, values, slope):
    for b in range(weight.shape[1] // 256):
        cols = pl.ds(b * 256, 256)
        raw = mm(low[...], weight[:, cols])
        gate = sigmoid(raw)
        out = raw * gate
        values[:, cols] = out.astype(BF16)
        slope[:, cols] = gate + out * (1.0 - gate)


def add_up(parts):
    while len(parts) > 1:
        parts = [a + b for a, b in zip(parts[::2], parts[1::2])]
    return parts[0]


def local_body(normed, enter, keep, mix, smooth):
    chunks = enter.shape[1]
    hidden = keep.shape[0]
    for tile in range(normed.shape[0]):
        lanes = lanes_of(tile)
        keeps = [keep[h : h + 1, lanes] for h in range(hidden)]
        mixes = [mix[h : h + 1, lanes] for h in range(hidden)]

        def step(t, state):
            place = (tile, pl.ds(t, chunks, stride=CHUNK), slice(None))
            value = normed[place]
            state = tuple(k * u + value for k, u in zip(keeps, state))
            smooth[place] = add_up([c * u for c, u in zip(mixes, state)])
            return state

        lax.fori_loop(0, CHUNK, step, tuple(enter[h, :, lanes] for h in range(hidden)), unroll=8)


def pair_body(backward, tokens, meta, own, other, logk, out):
    core = meta[0] % 2
    first = (meta[0] - core) * tokens
    middle = first + tokens
    decay = jnp.exp(tokens * logk[...])
    if backward:
        reach = clear_range(meta, first + 1, middle + 1)
        near = jnp.where(core == 0, own[...], other[...])
        far = jnp.where(core == 0, other[...], own[...])
    else:
        reach = clear_range(meta, middle, middle + tokens)
        near = jnp.where(core == 0, other[...], own[...])
        far = jnp.where(core == 0, own[...], other[...])
    out[...] = near + (reach * decay) * far


def window_body(count, tokens, meta, near, far, logk, out):
    span = 2 * tokens
    first = (meta[0] - meta[0] % 2) * tokens
    reach = clear_range(meta, first + 1, first + count * span + 1)
    out[...] = near[...] + (reach * jnp.exp((count * span) * logk[...])) * far[...]


def carry_of(backward, tokens, meta, other, arrived, logk):
    core = meta[0] % 2
    first = (meta[0] - core) * tokens
    span = 2 * tokens
    total = None
    for k, part in arrived:
        if backward:
            reach = clear_range(meta, first + span, first + (k + 1) * span + 1)
        else:
            reach = clear_range(meta, first - k * span, first)
        term = part[...] * reach
        if k:
            term = term * jnp.exp((k * span) * logk[...])
        total = term if total is None else total + term
    decay = jnp.exp(tokens * logk[...])
    middle = first + tokens
    if backward:
        crossing = clear_range(meta, middle, middle + 1)
        through = clear_range(meta, middle + 1, middle + tokens)
        passed = crossing * (other[...] + (through * decay) * total)
        return jnp.where(core == 0, passed, total)
    through = clear_range(meta, first, middle)
    return jnp.where(core == 0, total, other[...] + (through * decay) * total)


def reversed_lanes(row):
    size = row.shape[1]
    down = lax.broadcasted_iota(jnp.int32, (size, size), 0)
    across = lax.broadcasted_iota(jnp.int32, (size, size), 1)
    turn = jnp.where((down + across) % size == 0, 1.0, 0.0).astype(F32)
    return jnp.dot(row, turn, precision=lax.Precision.HIGHEST, preferred_element_type=F32)


def carried_body(chips, meta, other, *rest):
    arrived = rest[:chips]
    logk, keep, mix, omega, normed, smooth, enter, low, slope, states, carry, extra = rest[chips:]
    tiles, tokens, _ = normed.shape
    hidden = keep.shape[0]
    chunks = tokens // CHUNK
    carry[...] = carry_of(False, tokens, meta, other, list(enumerate(arrived)), logk)
    free = chunk_masks(meta, meta[0] * tokens, chunks)
    reach = prefix_mask(free, chunks, False)
    offset = (lax.broadcasted_iota(jnp.int32, (chunks, 128), 0) * CHUNK).astype(F32)
    for tile in range(tiles):
        lanes = lanes_of(tile)
        state = []
        for h in range(hidden):
            entry = jnp.exp(offset * logk[h : h + 1, lanes]) * reach
            first = carry[h : h + 1, lanes] * entry
            states[h, :, lanes] = enter[h, :, lanes] + first
            state.append(mix[h : h + 1, lanes] * first)
        keeps = [keep[h : h + 1, lanes] for h in range(hidden)]

        def step(t, state):
            place = pl.ds(t, chunks, stride=CHUNK)
            state = tuple(k * u for k, u in zip(keeps, state))
            extra[place, :] = add_up(list(state))
            return state

        lax.fori_loop(0, CHUNK, step, tuple(state), unroll=8)
        pre = smooth[tile] + extra[...] + omega[:, lanes] * normed[tile]
        gate = sigmoid(pre)
        smoothed = pre * gate
        low[:, lanes] = smoothed.astype(BF16)
        slope[:, lanes] = gate + smoothed * (1.0 - gate)


def layer_grad(weighted, normal, inverse):
    mean_one = jnp.mean(weighted, axis=1, keepdims=True)
    mean_two = jnp.mean(weighted * normal, axis=1, keepdims=True)
    return (weighted - mean_one - normal * mean_two) * inverse


def shift_rows(table, down):
    size = table.shape[0]
    rows = lax.broadcasted_iota(jnp.int32, table.shape, 0)
    bit = 1
    while bit < size:
        moved = pltpu.roll(table, bit if down else size - bit, 1)
        table = jnp.where((rows & bit) != 0, moved, table)
        bit *= 2
    return table


def mix_body(low, mix_weight, qk_gain, qk_bias, update, candidate, reset, queries, keys, shared, shared_slope):
    width = update.shape[1]
    base = width + shared.shape[1]
    top = base + reset.shape[1]
    raw = mm(low[...], mix_weight[:, width:base])
    gate = sigmoid(raw)
    silu = raw * gate
    shared[...] = silu
    shared_slope[...] = gate + silu * (1.0 - gate)
    queries[...] = (silu * qk_gain[0:1] + qk_bias[0:1]).astype(BF16)
    keys[...] = (silu * qk_gain[1:2] + qk_bias[1:2]).astype(BF16)
    for b in range(width // 256):
        update[:, b * 256 : (b + 1) * 256] = sigmoid(mm(low[...], mix_weight[:, b * 256 : (b + 1) * 256]))
    for b in range(reset.shape[1] // 256):
        reset[:, b * 256 : (b + 1) * 256] = mm(low[...], mix_weight[:, base + b * 256 : base + (b + 1) * 256])
    for b in range(width // 256):
        candidate[:, b * 256 : (b + 1) * 256] = mm(low[...], mix_weight[:, top + b * 256 : top + (b + 1) * 256])


def attend_body(queries, keys, values, rel_bias, reset, weights, attended, gated):
    tokens, shared_width = queries.shape
    place = lax.broadcasted_iota(jnp.int32, (SPAN, SPAN), 0)
    causal = place >= lax.broadcasted_iota(jnp.int32, (SPAN, SPAN), 1)
    turned = jnp.broadcast_to(reversed_lanes(jnp.broadcast_to(rel_bias[...], (8, SPAN)))[0:1], (SPAN, SPAN))
    bias = shift_rows(turned, True)
    scale = 1.0 / math.sqrt(shared_width)
    for s in range(tokens // SPAN):
        rows = pl.ds(s * SPAN, SPAN)
        scores = mm_nt(queries[rows, :], keys[rows, :]) * scale + bias
        scores = jnp.where(causal, scores, -1e30)
        powers = jnp.exp(scores - jnp.max(scores, axis=1, keepdims=True))
        share = powers / jnp.sum(powers, axis=1, keepdims=True)
        weights[rows, :] = share
        rise = mm(share.astype(BF16), values[rows, :])
        attended[rows, :] = rise
        raw = reset[rows, :]
        gated[rows, :] = (raw * sigmoid(raw) * rise).astype(BF16)


def hidden_body(
    gated, out_weight, candidate, update, tok, gain2, residual, change, slope_hidden, normal2, inverse2, low2
):
    total = candidate[...] + mm(gated[...], out_weight[...])
    gate = sigmoid(total)
    hidden_rows = total * gate
    slope_hidden[...] = gate + hidden_rows * (1.0 - gate)
    x = tok[...].astype(F32)
    moved = hidden_rows - x
    change[...] = moved
    rows = x + update[...] * moved
    residual[...] = rows
    centered = rows - jnp.mean(rows, axis=1, keepdims=True)
    inverse = lax.rsqrt(jnp.mean(centered * centered, axis=1, keepdims=True) + EPS)
    normal = centered * inverse
    normal2[...] = normal
    inverse2[...] = jnp.broadcast_to(inverse, inverse2.shape)
    low2[...] = (normal * gain2[...]).astype(BF16)


def expand_body(low2, ffn_in, expanded, slope_exp):
    for b in range(ffn_in.shape[1] // 256):
        cols = pl.ds(b * 256, 256)
        raw = mm(low2[...], ffn_in[:, cols])
        gate = sigmoid(raw)
        silu = raw * gate
        expanded[:, cols] = silu.astype(BF16)
        slope_exp[:, cols] = gate + silu * (1.0 - gate)


def weights_body(parts, meta, *refs):
    kept, sent = refs[-SWAPS - 1], refs[-SWAPS:]
    pairs = refs[: -SWAPS - 1]
    half = kept.shape[0]
    core = meta[0] % 2
    for mine, side in ((False, 1 - core), (True, core)):
        for i, (column, block) in enumerate(parts):
            left, right = pairs[2 * i], pairs[2 * i + 1]
            begin = pl.multiple_of(side * half + block, 128)
            cols = slice(column, column + right.shape[1])
            value = mm_tn(left[:, pl.ds(begin, half)], right[...])
            if mine:
                kept[:, cols] = value
            else:
                for j, target in enumerate(sent):
                    target[:, cols] = value[j * half // SWAPS : (j + 1) * half // SWAPS]


def block_body(residual, expanded, ffn_out, out):
    out[...] = residual[...] + mm(expanded[...], ffn_out[...])


def expand_back_body(cot, ffn_out, slope_exp, expand_grad):
    for b in range(ffn_out.shape[0] // 256):
        cols = pl.ds(b * 256, 256)
        expand_grad[:, cols] = (mm_nt(cot[...], ffn_out[cols, :]) * slope_exp[:, cols]).astype(BF16)


def hidden_back_body(
    expand_grad,
    ffn_in,
    normal2,
    inverse2,
    gain2,
    cot,
    update,
    change,
    slope_hidden,
    input_part,
    update_grad,
    out_grad,
    gain2_grad,
):
    norm_out = mm_nt(expand_grad[...], ffn_in[...])
    normal = normal2[...]
    gain2_grad[...] = jnp.sum(norm_out * normal, axis=0, keepdims=True)
    upstream = cot[...].astype(F32) + layer_grad(norm_out * gain2[...], normal, inverse2[:, 0:1])
    gates = update[...]
    input_part[...] = upstream * (1.0 - gates)
    update_grad[...] = (upstream * change[...] * gates * (1.0 - gates)).astype(BF16)
    out_grad[...] = (upstream * gates * slope_hidden[...]).astype(BF16)


def reset_back_body(out_grad, out_weight, reset, attended, reset_grad, attend_grad):
    for b in range(reset.shape[1] // 256):
        cols = pl.ds(b * 256, 256)
        rise = mm_nt(out_grad[...], out_weight[cols, :])
        raw = reset[:, cols]
        gate = sigmoid(raw)
        silu = raw * gate
        reset_grad[:, cols] = (rise * attended[:, cols] * (gate + silu * (1.0 - gate))).astype(BF16)
        attend_grad[:, cols] = (rise * silu).astype(BF16)


def attend_back_body(
    attend_grad,
    weights,
    queries,
    keys,
    shared,
    shared_slope,
    values,
    values_slope,
    qk_gain,
    value_grad,
    shared_grad,
    small,
):
    tokens, shared_width = queries.shape
    scale = 1.0 / math.sqrt(shared_width)
    slopes = jnp.zeros((SPAN, SPAN), F32)
    for s in range(tokens // SPAN):
        rows = pl.ds(s * SPAN, SPAN)
        upstream = attend_grad[rows, :]
        share = weights[rows, :]
        rise = mm_nt(upstream, values[rows, :])
        value_rise = mm_tn(share.astype(BF16), upstream)
        value_grad[rows, :] = (value_rise * values_slope[rows, :]).astype(BF16)
        score_grad = share * (rise - jnp.sum(share * rise, axis=1, keepdims=True))
        slopes = slopes + score_grad
        low = (score_grad * scale).astype(BF16)
        query_grad = mm(low, keys[rows, :])
        key_grad = mm_tn(low, queries[rows, :])
        silu = shared[rows, :]
        pieces = (
            jnp.sum(query_grad * silu, axis=0, keepdims=True),
            jnp.sum(key_grad * silu, axis=0, keepdims=True),
            jnp.sum(query_grad, axis=0, keepdims=True),
            jnp.sum(key_grad, axis=0, keepdims=True),
        )
        sums = pieces if s == 0 else tuple(a + b for a, b in zip(sums, pieces))
        back = query_grad * qk_gain[0:1] + key_grad * qk_gain[1:2]
        shared_grad[rows, :] = (back * shared_slope[rows, :]).astype(BF16)
    small[...] = jnp.zeros_like(small)
    for i in range(4):
        small[i : i + 1, :] = sums[i]
    turned = jnp.sum(shift_rows(slopes, False), axis=0, keepdims=True)
    small[4:5, :] = reversed_lanes(jnp.broadcast_to(turned, (8, SPAN)))[0:1]


def smooth_back_body(
    update_grad,
    shared_grad,
    reset_grad,
    out_grad,
    value_grad,
    mix_weight,
    value_weight,
    slope_pre,
    normed,
    omega,
    smooth_grad,
    norm_grad,
    omega_grad,
):
    width = update_grad.shape[1]
    base = width + shared_grad.shape[1]
    top = base + reset_grad.shape[1]
    rise = mm_nt(reset_grad[...], mix_weight[:, base:top])
    rise = rise + mm_nt(update_grad[...], mix_weight[:, :width])
    rise = rise + mm_nt(out_grad[...], mix_weight[:, top:])
    rise = rise + mm_nt(shared_grad[...], mix_weight[:, width:base])
    grad = rise * slope_pre[...]
    put_tiled(smooth_grad, grad)
    put_tiled(norm_grad, mm_nt(value_grad[...], value_weight[...]) + omega[...] * grad)
    omega_grad[...] = jnp.sum(grad * tiled(normed), axis=0, keepdims=True)


def rise_body(meta, smooth_grad, logk, keep, enter, end):
    tiles, tokens, _ = smooth_grad.shape
    hidden = keep.shape[0]
    chunks = tokens // CHUNK
    free = chunk_masks(meta, meta[0] * tokens, chunks)
    edge = edge_masks(free, chunks, True)
    masks, shifts = doubling_masks(edge, chunks, True)
    for tile in range(tiles):
        lanes = lanes_of(tile)
        keeps = [keep[h : h + 1, lanes] for h in range(hidden)]

        def step(t, state):
            value = smooth_grad[tile, pl.ds(CHUNK - 1 - t, chunks, stride=CHUNK), :]
            return tuple(k * u + value for k, u in zip(keeps, state))

        zero = jnp.zeros((chunks, 128), F32)
        state = lax.fori_loop(0, CHUNK, step, (zero,) * hidden, unroll=8)
        for h in range(hidden):
            decay = jnp.exp(CHUNK * logk[h : h + 1, lanes])
            reached = scan_step(masks, state[h], decay, shifts, chunks)
            enter[h, :, lanes] = edge * pltpu.roll(reached, chunks - 1, 0)
            end[h : h + 1, lanes] = reached[0:1]


def carry_back_body(chips, meta, other, *rest):
    arrived = rest[:chips]
    logk, enter, later = rest[chips:]
    hidden, chunks, width = enter.shape
    tokens = chunks * CHUNK
    carry = carry_of(True, tokens, meta, other, [(2**j - 1, part) for j, part in enumerate(arrived)], logk)
    free = chunk_masks(meta, meta[0] * tokens, chunks)
    reach = prefix_mask(free, chunks, True)
    offset = ((chunks - 1 - lax.broadcasted_iota(jnp.int32, (chunks, 128), 0)) * CHUNK).astype(F32)
    for tile in range(width // 128):
        lanes = lanes_of(tile)
        for h in range(hidden):
            entry = jnp.exp(offset * logk[h : h + 1, lanes]) * reach
            later[h, :, lanes] = enter[h, :, lanes] + carry[h : h + 1, tile * 128 : (tile + 1) * 128] * entry


def state_back_body(tile, normed, smooth_grad, norm_grad, states, later, keep, mix, total, sums, history):
    hidden = keep.shape[0]
    chunks = states.shape[1]
    lanes = lanes_of(tile)
    heads = range(hidden)
    keeps = [keep[h : h + 1, lanes] for h in heads]
    mixes = [mix[h : h + 1, lanes] for h in heads]

    def rise(t, state):
        value = normed[tile, pl.ds(t, chunks, stride=CHUNK), :]
        state = tuple(k * u + value for k, u in zip(keeps, state))
        for i in heads:
            history[t, i] = state[i]
        return state

    lax.fori_loop(0, CHUNK, rise, tuple(states[h, :, lanes] for h in heads), unroll=4)

    def fall(i, held):
        state, reads, marks = held
        t = CHUNK - 1 - i
        place = pl.ds(t, chunks, stride=CHUNK)
        value = smooth_grad[tile, place, :]
        row = normed[tile, place, :]
        state = tuple(k * w + value for k, w in zip(keeps, state))
        reads = tuple(r + w * row for r, w in zip(reads, state))
        marks = tuple(m + w * history[t, j] for j, (m, w) in enumerate(zip(marks, state)))
        total[place, :] = norm_grad[tile, place, :] + add_up([c * w for c, w in zip(mixes, state)])
        return state, reads, marks

    zeros = (jnp.zeros((chunks, 128), F32),) * hidden
    first = tuple(later[h, :, lanes] for h in heads)
    _, reads, marks = lax.fori_loop(0, CHUNK, fall, (first, zeros, zeros), unroll=4)
    for h in heads:
        sums[h : h + 1, :] = jnp.sum(reads[h], axis=0, keepdims=True)
        sums[hidden + h : hidden + h + 1, :] = jnp.sum(marks[h], axis=0, keepdims=True)


def close_body(count, *refs):
    totals = refs[:count]
    sums = refs[count : 2 * count]
    tok, gain, input_part, omega_grad, gain2_grad, small, input_grad, packed = refs[2 * count :]
    x = tok[...].astype(F32)
    width = x.shape[1]
    centered = x - jnp.mean(x, axis=1, keepdims=True)
    inverse = lax.rsqrt(jnp.mean(centered * centered, axis=1, keepdims=True) + EPS)
    normal = centered * inverse
    upstream = jnp.concatenate([t[...] for t in totals], axis=1)
    input_grad[...] = input_part[...] + layer_grad(upstream * gain[...], normal, inverse)
    at = sums[0].shape[0] // 2
    packed[...] = jnp.zeros_like(packed)
    for i in range(count):
        packed[0:at, i * 128 : (i + 1) * 128] = sums[i][0:at, :]
        packed[0:at, width + i * 128 : width + (i + 1) * 128] = sums[i][at : 2 * at, :]
    packed[at : at + 1, :width] = jnp.sum(upstream * normal, axis=0, keepdims=True)
    packed[at : at + 1, width : 2 * width] = gain2_grad[...]
    packed[at + 1 : at + 2, :width] = omega_grad[...]
    packed[0:8, 2 * width : 2 * width + small.shape[1]] = small[...]


def finish_body(own, other, delta, alpha, beta, eta, *outs):
    delta_grad, alpha_grad, beta_grad, eta_grad, gain1_grad, gain2_grad, omega_grad, qk_gain_grad, qk_bias_grad, rel_grad = outs
    hidden, width = delta_grad.shape
    scale = 1.0 / math.sqrt(hidden)
    low = own.shape[0] - SMALL_ROWS
    packed = own[low:, :] + other[low:, :]
    read = packed[0:hidden, :width]
    mark = packed[0:hidden, width : 2 * width]
    share = jax.nn.sigmoid(delta[...])
    damp = jax.nn.sigmoid(alpha[...])
    inflow = share * beta[...]
    outflow = eta[...] * scale
    eta_grad[...] = inflow * read * scale
    inflow_grad = outflow * read
    beta_grad[...] = share * inflow_grad
    rate = inflow * outflow * (mark - read) / (share * damp - 1.0)
    share_grad = beta[...] * inflow_grad + damp * rate
    delta_grad[...] = share_grad * share * (1.0 - share)
    alpha_grad[...] = share * rate * damp * (1.0 - damp)
    gain1_grad[...] = packed[hidden : hidden + 1, :width]
    gain2_grad[...] = packed[hidden : hidden + 1, width : 2 * width]
    omega_grad[...] = packed[hidden + 1 : hidden + 2, :width]
    tail = slice(2 * width, 2 * width + rel_grad.shape[1])
    qk_gain_grad[...] = packed[0:2, tail]
    qk_bias_grad[...] = packed[2:4, tail]
    rel_grad[...] = packed[4:5, tail]


def swap(a, axis, bit):
    count = lax.axis_size(axis)
    return lax.ppermute(a, axis, [(i, i ^ bit) for i in range(count)])


def chip_before(state, chips):
    count = lax.axis_size("seq")
    return lax.ppermute(state, "seq", [(i, i + 2 * chips) for i in range(count - 2 * chips)])


def chip_after(state, chips):
    count = lax.axis_size("seq")
    return lax.ppermute(state, "seq", [(i, i - 2 * chips) for i in range(2 * chips, count)])


def axis_bits(axis, least):
    bits = []
    bit = least
    while bit < lax.axis_size(axis):
        bits.append((axis, bit))
        bit *= 2
    return bits


def cross(a, step):
    seq = lax.axis_size("seq")
    moves = []
    for i in range(lax.axis_size("dp") * seq):
        axis, bit = step[i % 2]
        moves.append((i, i ^ (bit * seq if axis == "dp" else bit)))
    return lax.ppermute(a, ("dp", "seq"), moves)


ROUTES = (
    (("xy1", "yx1"), "2"),
    (("1xy", "yx1"), "2"),
    (("xy1", "1yx"), "2"),
    (("xy12", "yx12"), ""),
    (("xy1", "yx1"), "2"),
)
ORDER = (
    "C0CC10C231KC02SK01K3042K",
    "KK0132041K32KK04K1324301",
    "2340312344313241424",
)
PACES = (
    2, 2, 2, 2, 2, 2, 2, 2, 2, 8, 12, 12, 12, 12, 2, 12, 12, 12, 3, 12, 0, 2, 2, 2, 2, 2, 2, 2, 2,
    2, 2, 2, 2, 2, 2, 12, 2, 2, 2, 2, 3, 0.5, 0.5, 12, 12, 12, 0, 12, 12, 12, 12, 2, 8, 8, 8, 8, 1,
    6, 1, 12, 2, 2, 2, 2, 2, 2, 2, 2, 12, 12, 12, 12, 12, 6, 6, 6, 6, 6, 6, 6,
)
BITS = {"x": ("dp", 1), "y": ("dp", 2), "1": ("seq", 2), "2": ("seq", 4)}


def route(halving, doubling):
    named = lambda pair: all(BITS[c][1] < lax.axis_size(BITS[c][0]) for c in pair)
    halves = [tuple(BITS[c] for c in pair) for pair in zip(*halving) if named(pair)]
    wholes = [(BITS[c], BITS[c]) for c in doubling if named(c)]
    for bit in axis_bits("dp", 1) + axis_bits("seq", 2):
        if bit not in BITS.values():
            halves.append((bit, bit))
    return halves, wholes


def masks_body(steps, meta, out):
    for i, step in enumerate(steps):
        place = [(meta[0] if axis == "seq" else meta[meta.shape[0] - 1]) // bit % 2 for axis, bit in step]
        side = jnp.where(meta[0] % 2 == 0, place[0], place[1])
        out[i] = jnp.full((8, 128), side.astype(F32))


def split_body(index, masks, kept, *refs):
    arrived, (keep, send) = refs[:-2], refs[-2:]
    half = keep.shape[0]
    upper = masks[index, 0:1, 0:1] > 0.5
    came = jnp.concatenate([a[...] for a in arrived], axis=0) if len(arrived) > 1 else arrived[0][...]
    total = kept[...] + came
    low, high = total[:half], total[half:]
    keep[...] = jnp.where(upper, high, low)
    send[...] = jnp.where(upper, low, high)


def sum_body(kept, arrived, out):
    out[...] = kept[...] + arrived[...]


def sum_more_body(kept, arrived, more, out):
    rows = kept.shape[0]
    out[:rows, :] = kept[...] + arrived[...]
    out[rows:, :] = more[...]


def join_body(index, extra, masks, own, other, out):
    half = own.shape[0] - extra
    upper = masks[index, 0:1, 0:1] > 0.5
    out[:half, :] = jnp.where(upper, other[:half, :], own[:half, :])
    out[half : 2 * half, :] = jnp.where(upper, own[:half, :], other[:half, :])
    if extra:
        out[2 * half :, :] = own[half:, :] + other[half:, :]


class Piece:
    def __init__(self, line, made, steps, kept, sent, routes, outputs, name, more=None):
        self.line, self.made, self.steps, self.name = line, made, steps, name
        self.outputs, self.more = outputs, more
        self.work = self.run(kept, sent, *routes)
        self.done = False
        self.advance()

    def advance(self):
        if not self.done:
            self.done = next(self.work, "end") == "end"

    def run(self, kept, sent, halves, wholes):
        line = self.line
        arrived = [swap(a, "seq", 1) for a in sent]
        yield
        masks = self.made["masks"]
        for step in halves:
            rows, cols = kept.shape
            kept, send = line(
                lambda *refs, index=self.steps.index(step): split_body(index, *refs),
                (masks, kept, *arrived),
                [((rows // 2, cols), F32)] * 2,
                name=self.name + "_split",
            )
            arrived = [cross(send, step)]
            yield
        extra = 0
        for step in list(wholes) + [None]:
            rows, cols = kept.shape
            if self.more is not None and not extra:
                extra = SMALL_ROWS
                kept = line(
                    sum_more_body,
                    (kept, arrived[0], self.more()),
                    [((rows + extra, cols), F32)],
                    name=self.name + "_sum",
                )[0]
            else:
                kept = line(sum_body, (kept, arrived[0]), [(kept.shape, F32)], name=self.name + "_sum")[0]
            if step is not None:
                arrived = [cross(kept, step)]
                yield
        part = kept
        for step in reversed(halves):
            other = cross(part, step)
            yield
            rows, cols = part.shape
            part = line(
                lambda *refs, index=self.steps.index(step): join_body(index, extra, *refs),
                (masks, part, other),
                [((2 * rows - extra, cols), F32)],
                name=self.name + "_join",
            )[0]
        other = swap(part, "seq", 1)
        yield
        self.outputs(part, other, part.shape[0] - extra)


def place_body(plans, rows, extra, count, more, meta, own, other, *refs):
    outs = refs[count : count + len(plans)]
    sems = refs[-1]
    core = meta[0] % 2
    copies = []
    for part, side in ((own, core), (other, 1 - core)):
        for out, plan in zip(outs, plans):
            for column, width, row, place in plan:
                begin = pl.multiple_of(side * rows + row, 8)
                copies.append(
                    pltpu.make_async_copy(
                        part.at[pl.ds(0, rows), pl.ds(column, width)],
                        out.at[pl.ds(begin, rows), pl.ds(place, width)],
                        sems.at[len(copies)],
                    )
                )
                copies[-1].start()
    if more is not None:
        more(own, other, *refs[:extra], *refs[count + len(plans) : -1])
    for copy in copies:
        copy.wait()


class Outputs:
    def __init__(self, line, meta, shapes):
        self.line, self.meta, self.shapes, self.arrays = line, meta, shapes, {}

    def placer(self, plans, name, more=None):
        def place(own, other, rows):
            names = list(plans)
            held = [n for n in names if n in self.arrays]
            body, extra, shapes = (more[0], more[1], more[2]) if more else (None, (), [])
            at = 3 + len(extra)
            alias = {at + i: names.index(n) for i, n in enumerate(held)}
            results = self.line(
                lambda *refs: place_body(
                    list(plans.values()), rows, len(extra), len(extra) + len(held), body, *refs
                ),
                (self.meta, own, other, *extra, *[self.arrays[n] for n in held]),
                [(self.shapes[n], F32) for n in names] + shapes,
                name=name + "_out",
                held=own.size * 8 + 2**20 * len(shapes) // 8,
                alias=alias,
                out_left=len(names),
                dma=2 * sum(len(p) for p in plans.values()),
            )
            self.arrays.update(zip(names, results))
            if more:
                more[3](results[len(names) :])

        return place


def shards(
    tokens,
    cotangent,
    seq_lengths,
    norm1_gain,
    value_weight,
    ema_delta,
    ema_alpha,
    ema_beta,
    ema_eta,
    ema_omega,
    mix_weight,
    qk_gain,
    qk_bias,
    rel_bias,
    out_weight,
    norm2_gain,
    ffn_in,
    ffn_out,
):
    rows, width = tokens.shape
    hidden = ema_delta.shape[1]
    chunks = rows // CHUNK
    value_width = value_weight.shape[1]
    inner = ffn_in.shape[1]
    mixed = mix_weight.shape[1]
    shared_width = qk_gain.shape[1]
    places = jnp.stack([lax.axis_index("seq"), lax.axis_index("dp")]).astype(jnp.int32)
    meta = jnp.concatenate([places[:1], seq_lengths[0], places[1:]])
    gain1 = norm1_gain[None]
    gain2 = norm2_gain[None]
    omega = ema_omega[None]
    ema = (ema_delta.T, ema_alpha.T, ema_beta.T, ema_eta.T)
    full = (rows, width)
    wide = (rows, value_width)
    thin = (rows, shared_width)
    tiles = (width // 128, rows, 128)
    state = (hidden, width)
    states = (hidden, chunks, width)
    line = Line(PACES)

    share = jax.nn.sigmoid(ema_delta.T)
    logk = jnp.log1p(-share * jax.nn.sigmoid(ema_alpha.T))
    keep = jnp.exp(logk)
    mix = share * ema_beta.T * (ema_eta.T * (1.0 / math.sqrt(hidden)))
    gain_rows = jnp.where(share > -1.0, gain1, 0.0)
    normed, low_normed, enter, end = line(
        start_body,
        (seq_lengths, tokens, gain_rows, logk, keep),
        [(tiles, F32), (full, BF16), (states, F32), (state, F32)],
        name="norm_and_states",
    )
    other = swap(end, "seq", 1)
    chip_end = line(
        lambda *refs: pair_body(False, rows, *refs), (meta, end, other, logk), [(state, F32)], name="chip_state"
    )[0]
    arrived = [chip_before(chip_end, k) for k in range(1, lax.axis_size("seq") // 2)]
    routes = [route(halving, doubling) for halving, doubling in ROUTES]
    steps = sorted({step for halves, wholes in routes for step in halves})
    smooth = line(local_body, (normed, enter, keep, mix), [(tiles, F32)], name="local_average")[0]
    values, values_slope = line(values_body, (low_normed, value_weight), [(wide, BF16), (wide, F32)], name="values")
    low_smoothed, slope_pre, entering = line(
        lambda *refs: carried_body(len(arrived), *refs),
        (meta, other, *arrived, logk, keep, mix, omega, normed, smooth, enter),
        [(full, BF16), (full, F32), (states, F32)],
        scratch=[(state, F32), ((rows, 128), F32)],
        name="carried_average",
    )
    update, candidate, reset, queries, keys, shared, shared_slope = line(
        mix_body,
        (low_smoothed, mix_weight, qk_gain, qk_bias),
        [(full, F32), (full, F32), (wide, F32), (thin, BF16), (thin, BF16), (thin, F32), (thin, F32)],
        name="mix",
    )
    weights, attended, gated = line(
        attend_body,
        (queries, keys, values, rel_bias[None], reset),
        [((rows, SPAN), F32), (wide, F32), (wide, BF16)],
        name="attention",
    )
    residual, change, slope_hidden, normal2, inverse2, low2 = line(
        hidden_body,
        (gated, out_weight, candidate, update, tokens, gain2),
        [(full, F32), (full, F32), (full, F32), (full, F32), ((rows, 128), F32), (full, BF16)],
        name="hidden",
    )
    expanded, slope_exp = line(
        expand_body, (low2, ffn_in), [((rows, inner), BF16), ((rows, inner), F32)], name="expand"
    )
    half = width // 2
    outputs = Outputs(
        line,
        meta,
        {
            "ffn_out": (inner, width),
            "ffn_in": (width, inner),
            "out": (value_width, width),
            "mix": (width, mixed),
            "value": (width, value_width),
        },
    )
    made = {}
    results = {}

    def more():
        while "packed" not in results:
            next(work)
        return results["packed"]

    def take(values):
        results["small"] = values

    last = (
        finish_body,
        ema,
        [(state, F32)] * 4 + [((1, width), F32)] * 3 + [((2, shared_width), F32)] * 2 + [((1, shared_width), F32)],
        take,
    )

    def start_piece(number, parts, pairs, height, cols, plans, name):
        kept, *sent = line(
            lambda *refs: weights_body(parts, *refs),
            (meta, *[a for pair in pairs for a in pair]),
            [((height, cols), F32)] + [((height // SWAPS, cols), F32)] * SWAPS,
            name=name + "_grad",
        )
        end = name == "value"
        placer = outputs.placer(plans, name, last if end else None)
        return Piece(line, made, steps, kept, sent, routes[number], placer, name, more if end else None)

    def ffn_out_piece():
        return start_piece(
            0,
            [(0, 0)], [(expanded, cotangent)], inner // 2, width, {"ffn_out": [(0, width, 0, 0)]}, "ffn_out"
        )

    def ffn_in_piece():
        return start_piece(
            1,
            [(0, 0), (inner, 0)],
            [(low2, made["expand_grad"]), (low_smoothed, made["update_grad"])],
            half,
            inner + width,
            {"ffn_in": [(0, inner, 0, 0)], "mix": [(inner, width, 0, 0)]},
            "ffn_in",
        )

    def out_piece():
        return start_piece(
            2,
            [(0, 0), (width, width), (2 * width, 0)],
            [(gated, made["out_grad"]), (gated, made["out_grad"]), (low_smoothed, made["out_grad"])],
            half,
            3 * width,
            {
                "out": [(0, width, 0, 0), (width, width, width, 0)],
                "mix": [(2 * width, width, 0, width + shared_width + value_width)],
            },
            "out",
        )

    def reset_piece():
        return start_piece(
            3,
            [(0, 0)],
            [(low_smoothed, made["reset_grad"])],
            half,
            value_width,
            {"mix": [(0, value_width, 0, width + shared_width)]},
            "reset",
        )

    def value_piece():
        return start_piece(
            4,
            [(0, 0), (value_width, 0)],
            [(low_normed, made["value_grad"]), (low_smoothed, made["shared_grad"])],
            half,
            value_width + shared_width,
            {"value": [(0, value_width, 0, 0)], "mix": [(value_width, shared_width, 0, width)]},
            "value",
        )

    makers = (ffn_out_piece, ffn_in_piece, out_piece, reset_piece, value_piece)
    pieces = []

    def advance(i):
        if i < len(pieces) and pieces[i] is not None:
            pieces[i].advance()
        else:
            pieces.extend([None] * (i + 1 - len(pieces)))
            pieces[i] = makers[i]()

    def compute():
        yield
        made["masks"] = line(
            lambda *refs: masks_body(steps, *refs), (meta,), [((len(steps), 8, 128), F32)], name="masks"
        )[0]
        made["expand_grad"] = line(
            expand_back_body, (cotangent, ffn_out, slope_exp), [((rows, inner), BF16)], name="expand_back"
        )[0]
        yield
        input_part, update_grad, out_grad, gain2_grad = line(
            hidden_back_body,
            (made["expand_grad"], ffn_in, normal2, inverse2, gain2, cotangent, update, change, slope_hidden),
            [(full, F32), (full, BF16), (full, BF16), ((1, width), F32)],
            name="hidden_back",
        )
        made["update_grad"], made["out_grad"] = update_grad, out_grad
        yield
        reset_grad, attend_grad = line(
            reset_back_body, (out_grad, out_weight, reset, attended), [(wide, BF16)] * 2, name="reset_back"
        )
        made["reset_grad"] = reset_grad
        yield
        value_grad, shared_grad, small = line(
            attend_back_body,
            (attend_grad, weights, queries, keys, shared, shared_slope, values, values_slope, qk_gain),
            [(wide, BF16), (thin, BF16), ((8, shared_width), F32)],
            name="attention_back",
        )
        made["value_grad"], made["shared_grad"] = value_grad, shared_grad
        yield
        smooth_grad, norm_grad, omega_grad = line(
            smooth_back_body,
            (update_grad, shared_grad, reset_grad, out_grad, value_grad, mix_weight, value_weight, slope_pre)
            + (normed, omega),
            [(tiles, F32), (tiles, F32), ((1, width), F32)],
            name="smooth_back",
        )
        yield
        later, begin = line(
            rise_body, (meta, smooth_grad, logk, keep), [(states, F32), (state, F32)], name="states_back"
        )
        other_begin = swap(begin, "seq", 1)
        yield
        window = line(
            lambda *refs: pair_body(True, rows, *refs),
            (meta, begin, other_begin, logk),
            [(state, F32)],
            name="chip_grad",
        )[0]
        returned = [chip_after(window, 1)]
        yield
        chips = 1
        while 4 * chips < lax.axis_size("seq"):
            window = line(
                lambda *refs, chips=chips: window_body(chips, rows, *refs),
                (meta, window, returned[-1], logk),
                [(state, F32)],
                name="window_grad",
            )[0]
            chips *= 2
            returned.append(chip_after(window, chips))
            yield
        later = line(
            lambda *refs: carry_back_body(len(returned), *refs),
            (meta, other_begin, *returned, logk, later),
            [(states, F32)],
            name="carry_back",
        )[0]
        yield
        backs = []
        for tile in range(width // 128):
            backs.append(
                line(
                    lambda *refs, tile=tile: state_back_body(tile, *refs),
                    (normed, smooth_grad, norm_grad, entering, later, keep, mix),
                    [((rows, 128), F32), ((2 * hidden, 128), F32)],
                    scratch=[((CHUNK, hidden, chunks, 128), F32)],
                    name="state_back",
                )
            )
            yield
        results["input_grad"], results["packed"] = line(
            lambda *refs: close_body(len(backs), *refs),
            (*[b[0] for b in backs], *[b[1] for b in backs], tokens, gain1, input_part, omega_grad, gain2_grad, small),
            [(full, F32), ((SMALL_ROWS, value_width + shared_width), F32)],
            name="norm_back",
        )
        yield
        results["block_out"] = line(block_body, (residual, expanded, ffn_out), [(full, F32)], name="block_out")[0]

    work = compute()
    for item in "".join(ORDER):
        if item.isdigit():
            advance(int(item))
        else:
            next(work, None)
    for _ in work:
        pass
    while not all(p.done for p in pieces):
        for i in range(len(pieces)):
            advance(i)
    sums = outputs.arrays
    small = results["small"]
    return (
        results["block_out"],
        results["input_grad"],
        small[4][0],
        sums["value"],
        *[g.T for g in small[:4]],
        small[6][0],
        sums["mix"],
        small[7],
        small[8],
        small[9][0],
        sums["out"],
        small[5][0],
        sums["ffn_in"],
        sums["ffn_out"],
    )


def solution(mesh):
    rows = P(("dp", "seq"), None)
    in_specs = (rows, rows, P("dp", None)) + (P(),) * 15
    out_specs = (rows, rows) + (P(),) * 15
    return jax.shard_map(shards, mesh=mesh, in_specs=in_specs, out_specs=out_specs, check_vma=False)
```

```python
import math

import jax
import jax.numpy as jnp
from jax import lax
from jax.experimental import pallas as pl
from jax.experimental.pallas import tpu as pltpu
from jax.sharding import PartitionSpec as P

SPAN = 128
CHUNK = 64
EPS = 1e-05
BF16 = jnp.bfloat16
F32 = jnp.float32
ROOM = 2 * 1024 * 1024
SWAPS = 1
SMALL_ROWS = 24


def sigmoid(a):
    return 0.5 * jnp.tanh(0.5 * a) + 0.5


def mm(a, b):
    return lax.dot_general(a, b, (((1,), (0,)), ((), ())), preferred_element_type=F32)


def mm_nt(a, b):
    return lax.dot_general(a, b, (((1,), (1,)), ((), ())), preferred_element_type=F32)


def mm_tn(a, b):
    return lax.dot_general(a, b, (((0,), (0,)), ((), ())), preferred_element_type=F32)


class Place:
    def __init__(self, lengths):
        self.lengths = lengths
        self.shape = (lengths.shape[1] + 2,)

    def __getitem__(self, i):
        if i == 0:
            return lax.axis_index("seq")
        return self.lengths[0, i - 1]


class Line:
    def __init__(self, paces):
        self.token = None
        self.paces = paces
        self.count = 0

    def __call__(self, body, ins, outs, scratch=(), name=None, held=None, left=(), alias=None, out_left=0, dma=0):
        count = len(ins)
        before = () if self.token is None else (self.token,)
        alias = alias or {}
        specs = []
        for i, a in enumerate(ins):
            if i in left:
                specs.append(pl.BlockSpec(memory_space=pltpu.HBM))
            elif i in alias:
                specs.append(pl.BlockSpec(memory_space=pl.ANY))
            else:
                specs.append(pl.BlockSpec(memory_space=pltpu.SMEM if a.dtype == jnp.int32 else pltpu.VMEM))
        specs += [pl.BlockSpec(memory_space=pl.ANY)] * len(before)
        if held is None:
            held = sum(a.size * a.dtype.itemsize for a in ins if a.dtype != jnp.int32)
            held += sum(math.prod(s) * jnp.dtype(d).itemsize for s, d in tuple(outs) + tuple(scratch))
        first = count + len(before)

        def run(*refs):
            body(*refs[:count], *refs[first : first + len(outs)], *refs[first + len(outs) + 1 :])
            refs[first + len(outs)][...] = jnp.zeros((8, 128), F32)

        places = [pl.ANY if i < out_left else pltpu.VMEM for i in range(len(outs))]
        scratches = [pltpu.VMEM(s, d) for s, d in scratch]
        if dma:
            scratches.append(pltpu.SemaphoreType.DMA((dma,)))
        pace = self.paces[self.count] if self.count < len(self.paces) else 0
        self.count += 1
        result = pl.pallas_call(
            run,
            in_specs=specs,
            out_specs=[pl.BlockSpec(memory_space=m) for m in places + [pltpu.VMEM]],
            out_shape=[jax.ShapeDtypeStruct(s, d) for s, d in outs] + [jax.ShapeDtypeStruct((8, 128), F32)],
            scratch_shapes=scratches,
            input_output_aliases=alias,
            compiler_params=pltpu.CompilerParams(vmem_limit_bytes=int(held * 1.05) + ROOM),
            cost_estimate=pl.CostEstimate(flops=int(pace * 1e9), bytes_accessed=0, transcendentals=0),
            name=name,
        )(*ins, *before)
        self.token = result[-1]
        return result[:-1]


def clear_range(meta, low, high):
    count = meta.shape[0] - 2
    begin = jnp.int32(0)
    hit = jnp.bool_(False)
    for i in range(count):
        length = meta[1 + i]
        hit = hit | ((length > 0) & (begin >= low) & (begin < high))
        begin = begin + length
    return jnp.where(hit, 0.0, 1.0).astype(F32)


def chunk_masks(meta, first, chunks):
    rows = lax.broadcasted_iota(jnp.int32, (chunks, 128), 0)
    free = jnp.ones((chunks, 128), F32)
    for s in range(0, chunks, SPAN // CHUNK):
        position = first + s * CHUNK
        free = jnp.where(rows == s, clear_range(meta, position, position + 1), free)
    return free


def lanes_of(tile):
    return pl.ds(tile * 128, 128)


def tiled(ref):
    return jnp.concatenate([ref[i] for i in range(ref.shape[0])], axis=1)


def put_tiled(ref, value):
    for i in range(ref.shape[0]):
        ref[i] = value[:, i * 128 : (i + 1) * 128]


def scan_step(masks, values, decay_row, shifts, chunks):
    power = decay_row
    for i, mask in enumerate(masks):
        values = values + power * (mask * pltpu.roll(values, shifts[i], 0))
        power = power * power
    return values


def doubling_masks(mask, chunks, backward):
    masks = []
    distance = 1
    while distance < chunks:
        masks.append(mask)
        shift = chunks - distance if backward else distance
        mask = mask * pltpu.roll(mask, shift, 0)
        distance *= 2
    shifts = []
    distance = 1
    while distance < chunks:
        shifts.append(chunks - distance if backward else distance)
        distance *= 2
    return masks, shifts


def edge_masks(free, chunks, backward):
    rows = lax.broadcasted_iota(jnp.int32, (chunks, 128), 0)
    if backward:
        return jnp.where(rows == chunks - 1, 0.0, pltpu.roll(free, chunks - 1, 0))
    return jnp.where(rows == 0, 0.0, free)


def prefix_mask(free, chunks, backward):
    rows = lax.broadcasted_iota(jnp.int32, (chunks, 128), 0)
    if backward:
        reach = jnp.where(rows == chunks - 1, 1.0, pltpu.roll(free, chunks - 1, 0))
    else:
        reach = free
    distance = 1
    while distance < chunks:
        if backward:
            moved = jnp.where(rows >= chunks - distance, 1.0, pltpu.roll(reach, chunks - distance, 0))
        else:
            moved = jnp.where(rows < distance, 1.0, pltpu.roll(reach, distance, 0))
        reach = reach * moved
        distance *= 2
    return reach


def start_body(lengths, tok, gain, logk, keep, normed, low, enter, end, strips):
    meta = Place(lengths)
    tokens, width = tok.shape
    hidden = end.shape[0]
    chunks = tokens // CHUNK
    x = tok[...].astype(F32)
    centered = x - jnp.mean(x, axis=1, keepdims=True)
    spread = jnp.mean(centered * centered, axis=1, keepdims=True)
    rows = centered * lax.rsqrt(spread + EPS) * gain[0:1, :]
    put_tiled(normed, rows)
    low[...] = rows.astype(BF16)
    free = chunk_masks(meta, meta[0] * tokens, chunks)
    edge = edge_masks(free, chunks, False)
    masks, shifts = doubling_masks(edge, chunks, False)
    for tile in range(width // 128):
        lanes = lanes_of(tile)
        keeps = [keep[h : h + 1, lanes] for h in range(hidden)]

        def step(t, state):
            value = normed[tile, pl.ds(t, chunks, stride=CHUNK), :]
            strips[tile, t] = value
            return tuple(k * u + value for k, u in zip(keeps, state))

        zero = jnp.zeros((chunks, 128), F32)
        state = lax.fori_loop(0, CHUNK, step, (zero,) * hidden, unroll=8)
        for h in range(hidden):
            decay = jnp.exp(CHUNK * logk[h : h + 1, lanes])
            reached = scan_step(masks, state[h], decay, shifts, chunks)
            enter[h, :, lanes] = edge * pltpu.roll(reached, 1, 0)
            end[h : h + 1, lanes] = reached[chunks - 1 : chunks]


def values_body(low, weight, values, slope):
    for b in range(weight.shape[1] // 256):
        cols = pl.ds(b * 256, 256)
        raw = mm(low[...], weight[:, cols])
        gate = sigmoid(raw)
        out = raw * gate
        values[:, cols] = out.astype(BF16)
        slope[:, cols] = gate + out * (1.0 - gate)


def add_up(parts):
    while len(parts) > 1:
        parts = [a + b for a, b in zip(parts[::2], parts[1::2])]
    return parts[0]


def local_body(strips, enter, keep, mix, smooth):
    hidden = keep.shape[0]
    for tile in range(strips.shape[0]):
        lanes = lanes_of(tile)
        keeps = [keep[h : h + 1, lanes] for h in range(hidden)]
        mixes = [mix[h : h + 1, lanes] for h in range(hidden)]

        def step(t, state):
            value = strips[tile, t]
            state = tuple(k * u + value for k, u in zip(keeps, state))
            smooth[tile, t] = add_up([c * u for c, u in zip(mixes, state)])
            return state

        lax.fori_loop(0, CHUNK, step, tuple(enter[h, :, lanes] for h in range(hidden)), unroll=8)


def pair_body(backward, tokens, meta, own, other, logk, out):
    core = meta[0] % 2
    first = (meta[0] - core) * tokens
    middle = first + tokens
    decay = jnp.exp(tokens * logk[...])
    if backward:
        reach = clear_range(meta, first + 1, middle + 1)
        near = jnp.where(core == 0, own[...], other[...])
        far = jnp.where(core == 0, other[...], own[...])
    else:
        reach = clear_range(meta, middle, middle + tokens)
        near = jnp.where(core == 0, other[...], own[...])
        far = jnp.where(core == 0, own[...], other[...])
    out[...] = near + (reach * decay) * far


def window_body(count, tokens, meta, near, far, logk, out):
    span = 2 * tokens
    first = (meta[0] - meta[0] % 2) * tokens
    reach = clear_range(meta, first + 1, first + count * span + 1)
    out[...] = near[...] + (reach * jnp.exp((count * span) * logk[...])) * far[...]


def carry_of(backward, tokens, meta, other, arrived, logk):
    core = meta[0] % 2
    first = (meta[0] - core) * tokens
    span = 2 * tokens
    total = None
    for k, part in arrived:
        if backward:
            reach = clear_range(meta, first + span, first + (k + 1) * span + 1)
        else:
            reach = clear_range(meta, first - k * span, first)
        term = part[...] * reach
        if k:
            term = term * jnp.exp((k * span) * logk[...])
        total = term if total is None else total + term
    decay = jnp.exp(tokens * logk[...])
    middle = first + tokens
    if backward:
        crossing = clear_range(meta, middle, middle + 1)
        through = clear_range(meta, middle + 1, middle + tokens)
        passed = crossing * (other[...] + (through * decay) * total)
        return jnp.where(core == 0, passed, total)
    through = clear_range(meta, first, middle)
    return jnp.where(core == 0, total, other[...] + (through * decay) * total)


def reversed_lanes(row):
    size = row.shape[1]
    down = lax.broadcasted_iota(jnp.int32, (size, size), 0)
    across = lax.broadcasted_iota(jnp.int32, (size, size), 1)
    turn = jnp.where((down + across) % size == 0, 1.0, 0.0).astype(F32)
    return jnp.dot(row, turn, precision=lax.Precision.HIGHEST, preferred_element_type=F32)


def carried_body(chips, meta, other, *rest):
    arrived = rest[:chips]
    logk, keep, mix, omega, strips, smooth, enter, low, slope, states, carry, rows = rest[chips:]
    tiles, _, chunks, _ = strips.shape
    tokens = chunks * CHUNK
    hidden = keep.shape[0]
    carry[...] = carry_of(False, tokens, meta, other, list(enumerate(arrived)), logk)
    free = chunk_masks(meta, meta[0] * tokens, chunks)
    reach = prefix_mask(free, chunks, False)
    offset = (lax.broadcasted_iota(jnp.int32, (chunks, 128), 0) * CHUNK).astype(F32)
    for tile in range(tiles):
        lanes = lanes_of(tile)
        state = []
        for h in range(hidden):
            entry = jnp.exp(offset * logk[h : h + 1, lanes]) * reach
            first = carry[h : h + 1, lanes] * entry
            states[h, :, lanes] = enter[h, :, lanes] + first
            state.append(mix[h : h + 1, lanes] * first)
        keeps = [keep[h : h + 1, lanes] for h in range(hidden)]
        skip = omega[:, lanes]

        def step(t, state):
            state = tuple(k * u for k, u in zip(keeps, state))
            pre = smooth[tile, t] + skip * strips[tile, t] + add_up(list(state))
            rows[pl.ds(t, chunks, stride=CHUNK), :] = pre
            return state

        lax.fori_loop(0, CHUNK, step, tuple(state), unroll=8)
        pre = rows[...]
        gate = sigmoid(pre)
        smoothed = pre * gate
        low[:, lanes] = smoothed.astype(BF16)
        slope[:, lanes] = gate + smoothed * (1.0 - gate)


def layer_grad(weighted, normal, inverse):
    mean_one = jnp.mean(weighted, axis=1, keepdims=True)
    mean_two = jnp.mean(weighted * normal, axis=1, keepdims=True)
    return (weighted - mean_one - normal * mean_two) * inverse


def shift_rows(table, down):
    size = table.shape[0]
    rows = lax.broadcasted_iota(jnp.int32, table.shape, 0)
    bit = 1
    while bit < size:
        moved = pltpu.roll(table, bit if down else size - bit, 1)
        table = jnp.where((rows & bit) != 0, moved, table)
        bit *= 2
    return table


def mix_body(low, mix_weight, qk_gain, qk_bias, update, candidate, reset, queries, keys, shared, shared_slope):
    width = update.shape[1]
    base = width + shared.shape[1]
    top = base + reset.shape[1]
    raw = mm(low[...], mix_weight[:, width:base])
    gate = sigmoid(raw)
    silu = raw * gate
    shared[...] = silu
    shared_slope[...] = gate + silu * (1.0 - gate)
    queries[...] = (silu * qk_gain[0:1] + qk_bias[0:1]).astype(BF16)
    keys[...] = (silu * qk_gain[1:2] + qk_bias[1:2]).astype(BF16)
    for b in range(width // 256):
        update[:, b * 256 : (b + 1) * 256] = sigmoid(mm(low[...], mix_weight[:, b * 256 : (b + 1) * 256]))
    for b in range(reset.shape[1] // 256):
        reset[:, b * 256 : (b + 1) * 256] = mm(low[...], mix_weight[:, base + b * 256 : base + (b + 1) * 256])
    for b in range(width // 256):
        candidate[:, b * 256 : (b + 1) * 256] = mm(low[...], mix_weight[:, top + b * 256 : top + (b + 1) * 256])


def attend_body(queries, keys, values, rel_bias, reset, weights, attended, gated):
    tokens, shared_width = queries.shape
    place = lax.broadcasted_iota(jnp.int32, (SPAN, SPAN), 0)
    causal = place >= lax.broadcasted_iota(jnp.int32, (SPAN, SPAN), 1)
    turned = jnp.broadcast_to(reversed_lanes(jnp.broadcast_to(rel_bias[...], (8, SPAN)))[0:1], (SPAN, SPAN))
    bias = shift_rows(turned, True)
    scale = 1.0 / math.sqrt(shared_width)
    for s in range(tokens // SPAN):
        rows = pl.ds(s * SPAN, SPAN)
        scores = mm_nt(queries[rows, :], keys[rows, :]) * scale + bias
        scores = jnp.where(causal, scores, -1e30)
        powers = jnp.exp(scores - jnp.max(scores, axis=1, keepdims=True))
        share = powers / jnp.sum(powers, axis=1, keepdims=True)
        weights[rows, :] = share
        rise = mm(share.astype(BF16), values[rows, :])
        attended[rows, :] = rise
        raw = reset[rows, :]
        gated[rows, :] = (raw * sigmoid(raw) * rise).astype(BF16)


def hidden_body(
    gated, out_weight, candidate, update, tok, gain2, residual, change, slope_hidden, normal2, inverse2, low2
):
    total = candidate[...] + mm(gated[...], out_weight[...])
    gate = sigmoid(total)
    hidden_rows = total * gate
    slope_hidden[...] = gate + hidden_rows * (1.0 - gate)
    x = tok[...].astype(F32)
    moved = hidden_rows - x
    change[...] = moved
    rows = x + update[...] * moved
    residual[...] = rows
    centered = rows - jnp.mean(rows, axis=1, keepdims=True)
    inverse = lax.rsqrt(jnp.mean(centered * centered, axis=1, keepdims=True) + EPS)
    normal = centered * inverse
    normal2[...] = normal
    inverse2[...] = jnp.broadcast_to(inverse, inverse2.shape)
    low2[...] = (normal * gain2[...]).astype(BF16)


def expand_body(low2, ffn_in, expanded, slope_exp):
    for b in range(ffn_in.shape[1] // 256):
        cols = pl.ds(b * 256, 256)
        raw = mm(low2[...], ffn_in[:, cols])
        gate = sigmoid(raw)
        silu = raw * gate
        expanded[:, cols] = silu.astype(BF16)
        slope_exp[:, cols] = gate + silu * (1.0 - gate)


def weights_body(parts, meta, *refs):
    kept, sent = refs[-SWAPS - 1], refs[-SWAPS:]
    pairs = refs[: -SWAPS - 1]
    half = kept.shape[0]
    core = meta[0] % 2
    for mine, side in ((False, 1 - core), (True, core)):
        for i, (column, block) in enumerate(parts):
            left, right = pairs[2 * i], pairs[2 * i + 1]
            begin = pl.multiple_of(side * half + block, 128)
            cols = slice(column, column + right.shape[1])
            value = mm_tn(left[:, pl.ds(begin, half)], right[...])
            if mine:
                kept[:, cols] = value
            else:
                for j, target in enumerate(sent):
                    target[:, cols] = value[j * half // SWAPS : (j + 1) * half // SWAPS]


def block_body(residual, expanded, ffn_out, out):
    out[...] = residual[...] + mm(expanded[...], ffn_out[...])


def expand_back_body(cot, ffn_out, slope_exp, expand_grad):
    for b in range(ffn_out.shape[0] // 256):
        cols = pl.ds(b * 256, 256)
        expand_grad[:, cols] = (mm_nt(cot[...], ffn_out[cols, :]) * slope_exp[:, cols]).astype(BF16)


def hidden_back_body(
    expand_grad,
    ffn_in,
    normal2,
    inverse2,
    gain2,
    cot,
    update,
    change,
    slope_hidden,
    input_part,
    update_grad,
    out_grad,
    gain2_grad,
):
    norm_out = mm_nt(expand_grad[...], ffn_in[...])
    normal = normal2[...]
    gain2_grad[...] = jnp.sum(norm_out * normal, axis=0, keepdims=True)
    upstream = cot[...].astype(F32) + layer_grad(norm_out * gain2[...], normal, inverse2[:, 0:1])
    gates = update[...]
    input_part[...] = upstream * (1.0 - gates)
    update_grad[...] = (upstream * change[...] * gates * (1.0 - gates)).astype(BF16)
    out_grad[...] = (upstream * gates * slope_hidden[...]).astype(BF16)


def reset_back_body(out_grad, out_weight, reset, attended, reset_grad, attend_grad):
    for b in range(reset.shape[1] // 256):
        cols = pl.ds(b * 256, 256)
        rise = mm_nt(out_grad[...], out_weight[cols, :])
        raw = reset[:, cols]
        gate = sigmoid(raw)
        silu = raw * gate
        reset_grad[:, cols] = (rise * attended[:, cols] * (gate + silu * (1.0 - gate))).astype(BF16)
        attend_grad[:, cols] = (rise * silu).astype(BF16)


def attend_back_body(
    attend_grad,
    weights,
    queries,
    keys,
    shared,
    shared_slope,
    values,
    values_slope,
    qk_gain,
    value_grad,
    shared_grad,
    small,
):
    tokens, shared_width = queries.shape
    scale = 1.0 / math.sqrt(shared_width)
    slopes = jnp.zeros((SPAN, SPAN), F32)
    for s in range(tokens // SPAN):
        rows = pl.ds(s * SPAN, SPAN)
        upstream = attend_grad[rows, :]
        share = weights[rows, :]
        rise = mm_nt(upstream, values[rows, :])
        value_rise = mm_tn(share.astype(BF16), upstream)
        value_grad[rows, :] = (value_rise * values_slope[rows, :]).astype(BF16)
        score_grad = share * (rise - jnp.sum(share * rise, axis=1, keepdims=True))
        slopes = slopes + score_grad
        low = (score_grad * scale).astype(BF16)
        query_grad = mm(low, keys[rows, :])
        key_grad = mm_tn(low, queries[rows, :])
        silu = shared[rows, :]
        pieces = (
            jnp.sum(query_grad * silu, axis=0, keepdims=True),
            jnp.sum(key_grad * silu, axis=0, keepdims=True),
            jnp.sum(query_grad, axis=0, keepdims=True),
            jnp.sum(key_grad, axis=0, keepdims=True),
        )
        sums = pieces if s == 0 else tuple(a + b for a, b in zip(sums, pieces))
        back = query_grad * qk_gain[0:1] + key_grad * qk_gain[1:2]
        shared_grad[rows, :] = (back * shared_slope[rows, :]).astype(BF16)
    small[...] = jnp.zeros_like(small)
    for i in range(4):
        small[i : i + 1, :] = sums[i]
    turned = jnp.sum(shift_rows(slopes, False), axis=0, keepdims=True)
    small[4:5, :] = reversed_lanes(jnp.broadcast_to(turned, (8, SPAN)))[0:1]


def smooth_back_body(
    update_grad,
    shared_grad,
    reset_grad,
    out_grad,
    value_grad,
    mix_weight,
    value_weight,
    slope_pre,
    normed,
    omega,
    smooth_grad,
    norm_grad,
    omega_grad,
):
    width = update_grad.shape[1]
    base = width + shared_grad.shape[1]
    top = base + reset_grad.shape[1]
    rise = mm_nt(reset_grad[...], mix_weight[:, base:top])
    rise = rise + mm_nt(update_grad[...], mix_weight[:, :width])
    rise = rise + mm_nt(out_grad[...], mix_weight[:, top:])
    rise = rise + mm_nt(shared_grad[...], mix_weight[:, width:base])
    grad = rise * slope_pre[...]
    put_tiled(smooth_grad, grad)
    put_tiled(norm_grad, mm_nt(value_grad[...], value_weight[...]) + omega[...] * grad)
    omega_grad[...] = jnp.sum(grad * tiled(normed), axis=0, keepdims=True)


def rise_body(meta, smooth_grad, logk, keep, enter, end, strips):
    tiles, tokens, _ = smooth_grad.shape
    hidden = keep.shape[0]
    chunks = tokens // CHUNK
    free = chunk_masks(meta, meta[0] * tokens, chunks)
    edge = edge_masks(free, chunks, True)
    masks, shifts = doubling_masks(edge, chunks, True)
    for tile in range(tiles):
        lanes = lanes_of(tile)
        keeps = [keep[h : h + 1, lanes] for h in range(hidden)]

        def step(t, state):
            value = smooth_grad[tile, pl.ds(CHUNK - 1 - t, chunks, stride=CHUNK), :]
            strips[tile, CHUNK - 1 - t] = value
            return tuple(k * u + value for k, u in zip(keeps, state))

        zero = jnp.zeros((chunks, 128), F32)
        state = lax.fori_loop(0, CHUNK, step, (zero,) * hidden, unroll=8)
        for h in range(hidden):
            decay = jnp.exp(CHUNK * logk[h : h + 1, lanes])
            reached = scan_step(masks, state[h], decay, shifts, chunks)
            enter[h, :, lanes] = edge * pltpu.roll(reached, chunks - 1, 0)
            end[h : h + 1, lanes] = reached[0:1]


def carry_back_body(chips, meta, other, *rest):
    arrived = rest[:chips]
    logk, enter, later = rest[chips:]
    hidden, chunks, width = enter.shape
    tokens = chunks * CHUNK
    carry = carry_of(True, tokens, meta, other, [(2**j - 1, part) for j, part in enumerate(arrived)], logk)
    free = chunk_masks(meta, meta[0] * tokens, chunks)
    reach = prefix_mask(free, chunks, True)
    offset = ((chunks - 1 - lax.broadcasted_iota(jnp.int32, (chunks, 128), 0)) * CHUNK).astype(F32)
    for tile in range(width // 128):
        lanes = lanes_of(tile)
        for h in range(hidden):
            entry = jnp.exp(offset * logk[h : h + 1, lanes]) * reach
            later[h, :, lanes] = enter[h, :, lanes] + carry[h : h + 1, tile * 128 : (tile + 1) * 128] * entry


def state_back_body(tile, strips, grads, states, later, keep, mix, part, sums, history):
    hidden = keep.shape[0]
    chunks = states.shape[1]
    lanes = lanes_of(tile)
    heads = range(hidden)
    keeps = [keep[h : h + 1, lanes] for h in heads]
    mixes = [mix[h : h + 1, lanes] for h in heads]
    zeros = (jnp.zeros((chunks, 128), F32),) * hidden

    def rise(t, held):
        state, reads = held
        value = strips[tile, t]
        grad = grads[tile, t]
        state = tuple(k * u + value for k, u in zip(keeps, state))
        reads = tuple(r + u * grad for r, u in zip(reads, state))
        for i in heads:
            history[t, i] = state[i]
        return state, reads

    first = tuple(states[h, :, lanes] for h in heads)
    _, reads = lax.fori_loop(0, CHUNK, rise, (first, zeros), unroll=4)
    for h in heads:
        sums[h : h + 1, :] = jnp.sum(reads[h], axis=0, keepdims=True)

    def fall(i, held):
        state, marks = held
        t = CHUNK - 1 - i
        grad = grads[tile, t]
        state = tuple(k * w + grad for k, w in zip(keeps, state))
        marks = tuple(m + w * history[t, j] for j, (m, w) in enumerate(zip(marks, state)))
        part[pl.ds(t, chunks, stride=CHUNK), :] = add_up([c * w for c, w in zip(mixes, state)])
        return state, marks

    first = tuple(later[h, :, lanes] for h in heads)
    _, marks = lax.fori_loop(0, CHUNK, fall, (first, zeros), unroll=4)
    for h in heads:
        sums[hidden + h : hidden + h + 1, :] = jnp.sum(marks[h], axis=0, keepdims=True)


def close_body(count, *refs):
    totals = refs[:count]
    sums = refs[count : 2 * count]
    tok, gain, norm_grad, input_part, omega_grad, gain2_grad, small, input_grad, packed = refs[2 * count :]
    x = tok[...].astype(F32)
    width = x.shape[1]
    centered = x - jnp.mean(x, axis=1, keepdims=True)
    inverse = lax.rsqrt(jnp.mean(centered * centered, axis=1, keepdims=True) + EPS)
    normal = centered * inverse
    upstream = tiled(norm_grad) + jnp.concatenate([t[...] for t in totals], axis=1)
    input_grad[...] = input_part[...] + layer_grad(upstream * gain[...], normal, inverse)
    at = sums[0].shape[0] // 2
    packed[...] = jnp.zeros_like(packed)
    for i in range(count):
        packed[0:at, i * 128 : (i + 1) * 128] = sums[i][0:at, :]
        packed[0:at, width + i * 128 : width + (i + 1) * 128] = sums[i][at : 2 * at, :]
    packed[at : at + 1, :width] = jnp.sum(upstream * normal, axis=0, keepdims=True)
    packed[at : at + 1, width : 2 * width] = gain2_grad[...]
    packed[at + 1 : at + 2, :width] = omega_grad[...]
    packed[0:8, 2 * width : 2 * width + small.shape[1]] = small[...]


def finish_body(own, other, delta, alpha, beta, eta, *outs):
    delta_grad, alpha_grad, beta_grad, eta_grad, gain1_grad, gain2_grad, omega_grad, qk_gain_grad, qk_bias_grad, rel_grad = outs
    hidden, width = delta_grad.shape
    scale = 1.0 / math.sqrt(hidden)
    packed = own[...] + other[...]
    read = packed[0:hidden, :width]
    mark = packed[0:hidden, width : 2 * width]
    share = jax.nn.sigmoid(delta[...])
    damp = jax.nn.sigmoid(alpha[...])
    inflow = share * beta[...]
    outflow = eta[...] * scale
    eta_grad[...] = inflow * read * scale
    inflow_grad = outflow * read
    beta_grad[...] = share * inflow_grad
    rate = inflow * outflow * (mark - read) / (share * damp - 1.0)
    share_grad = beta[...] * inflow_grad + damp * rate
    delta_grad[...] = share_grad * share * (1.0 - share)
    alpha_grad[...] = share * rate * damp * (1.0 - damp)
    gain1_grad[...] = packed[hidden : hidden + 1, :width]
    gain2_grad[...] = packed[hidden : hidden + 1, width : 2 * width]
    omega_grad[...] = packed[hidden + 1 : hidden + 2, :width]
    tail = slice(2 * width, 2 * width + rel_grad.shape[1])
    qk_gain_grad[...] = packed[0:2, tail]
    qk_bias_grad[...] = packed[2:4, tail]
    rel_grad[...] = packed[4:5, tail]


def swap(a, axis, bit):
    count = lax.axis_size(axis)
    return lax.ppermute(a, axis, [(i, i ^ bit) for i in range(count)])


def chip_before(state, chips):
    count = lax.axis_size("seq")
    return lax.ppermute(state, "seq", [(i, i + 2 * chips) for i in range(count - 2 * chips)])


def chip_after(state, chips):
    count = lax.axis_size("seq")
    return lax.ppermute(state, "seq", [(i, i - 2 * chips) for i in range(2 * chips, count)])


def axis_bits(axis, least):
    bits = []
    bit = least
    while bit < lax.axis_size(axis):
        bits.append((axis, bit))
        bit *= 2
    return bits


def cross(a, step):
    seq = lax.axis_size("seq")
    moves = []
    for i in range(lax.axis_size("dp") * seq):
        axis, bit = step[i % 2]
        moves.append((i, i ^ (bit * seq if axis == "dp" else bit)))
    return lax.ppermute(a, ("dp", "seq"), moves)


ROUTES = (
    (("xy", "yx"), "12"),
    (("xy1", "yx1"), "2"),
    (("xy1", "yx1"), "2"),
    (("xy1", "yx1"), "2"),
    (("1xy", "1yx"), "2"),
)
ORDER = (
    "CCKC1C410C40KK1K21042K13",
    "K03K12041K321432K1K03402",
    "143502435250S35425304235",
    "3",
)
PACES = (
    8, 8, 8, 8, 8, 8, 8, 8, 8, 8, 8, 8, 0, 0, 0, 0, 8, 8, 8, 8, 8, 8, 8, 12, 12, 12, 12, 8, 8, 8,
    12, 4, 4, 10, 2, 2, 2, 2, 10, 10, 10, 8, 8, 8, 8, 8, 8, 8, 8, 8, 8, 8, 8, 8, 8, 8, 8, 8, 8, 8,
    8, 8, 8, 8, 8, 8, 8, 8, 8, 8, 8, 8, 8, 12, 12, 12, 12, 8, 2, 0, 8, 8, 8, 12, 8, 0, 0, 0, 0, 8,
)
BITS = {"x": ("dp", 1), "y": ("dp", 2), "1": ("seq", 2), "2": ("seq", 4)}


def route(halving, doubling):
    named = lambda pair: all(BITS[c][1] < lax.axis_size(BITS[c][0]) for c in pair)
    halves = [tuple(BITS[c] for c in pair) for pair in zip(*halving) if named(pair)]
    wholes = [(BITS[c], BITS[c]) for c in doubling if named(c)]
    for bit in axis_bits("dp", 1) + axis_bits("seq", 2):
        if bit not in BITS.values():
            halves.append((bit, bit))
    return halves, wholes


def masks_body(steps, meta, out):
    for i, step in enumerate(steps):
        place = [(meta[0] if axis == "seq" else meta[meta.shape[0] - 1]) // bit % 2 for axis, bit in step]
        side = jnp.where(meta[0] % 2 == 0, place[0], place[1])
        out[i] = jnp.full((8, 128), side.astype(F32))


def split_body(index, masks, kept, *refs):
    arrived, (keep, send) = refs[:-2], refs[-2:]
    half = keep.shape[0]
    upper = masks[index, 0:1, 0:1] > 0.5
    came = jnp.concatenate([a[...] for a in arrived], axis=0) if len(arrived) > 1 else arrived[0][...]
    total = kept[...] + came
    low, high = total[:half], total[half:]
    keep[...] = jnp.where(upper, high, low)
    send[...] = jnp.where(upper, low, high)


def sum_body(kept, arrived, out):
    out[...] = kept[...] + arrived[...]


def join_body(index, masks, own, other, out):
    half = own.shape[0]
    upper = masks[index, 0:1, 0:1] > 0.5
    out[:half, :] = jnp.where(upper, other[...], own[...])
    out[half:, :] = jnp.where(upper, own[...], other[...])


class Piece:
    def __init__(self, line, made, steps, kept, sent, routes, outputs, name):
        self.line, self.made, self.steps, self.name = line, made, steps, name
        self.outputs = outputs
        self.work = self.run(kept, sent, *routes)
        self.done = False
        self.advance()

    def advance(self):
        if not self.done:
            self.done = next(self.work, "end") == "end"

    def run(self, kept, sent, halves, wholes):
        line = self.line
        arrived = [swap(a, "seq", 1) for a in sent]
        yield
        masks = self.made["masks"]
        for step in halves:
            rows, cols = kept.shape
            kept, send = line(
                lambda *refs, index=self.steps.index(step): split_body(index, *refs),
                (masks, kept, *arrived),
                [((rows // 2, cols), F32)] * 2,
                name=self.name + "_split",
            )
            arrived = [cross(send, step)]
            yield
        for step in list(wholes) + [None]:
            kept = line(sum_body, (kept, arrived[0]), [(kept.shape, F32)], name=self.name + "_sum")[0]
            if step is not None:
                arrived = [cross(kept, step)]
                yield
        part = kept
        for step in reversed(halves):
            other = cross(part, step)
            yield
            rows, cols = part.shape
            part = line(
                lambda *refs, index=self.steps.index(step): join_body(index, *refs),
                (masks, part, other),
                [((2 * rows, cols), F32)],
                name=self.name + "_join",
            )[0]
        other = swap(part, "seq", 1)
        yield
        self.outputs(part, other, part.shape[0])


class Small:
    def __init__(self, line, part, last):
        self.work = self.run(line, part, last)
        self.done = False
        self.advance()

    def advance(self):
        if not self.done:
            self.done = next(self.work, "end") == "end"

    def run(self, line, part, last):
        flat = axis_bits("dp", 1)
        steps = list(zip(flat, flat[::-1])) + [(bit, bit) for bit in axis_bits("seq", 2)]
        other = swap(part, "seq", 1)
        yield
        for step in steps:
            part = line(sum_body, (part, other), [(part.shape, F32)], name="small_sum")[0]
            other = cross(part, step)
            yield
        last(part, other)


def place_body(plans, rows, count, meta, own, other, *refs):
    outs = refs[count : count + len(plans)]
    sems = refs[-1]
    core = meta[0] % 2
    copies = []
    for part, side in ((own, core), (other, 1 - core)):
        for out, plan in zip(outs, plans):
            for column, width, row, place in plan:
                begin = pl.multiple_of(side * rows + row, 8)
                copies.append(
                    pltpu.make_async_copy(
                        part.at[pl.ds(0, rows), pl.ds(column, width)],
                        out.at[pl.ds(begin, rows), pl.ds(place, width)],
                        sems.at[len(copies)],
                    )
                )
                copies[-1].start()
    for copy in copies:
        copy.wait()


class Outputs:
    def __init__(self, line, meta, shapes):
        self.line, self.meta, self.shapes, self.arrays = line, meta, shapes, {}

    def placer(self, plans, name):
        def place(own, other, rows):
            names = list(plans)
            held = [n for n in names if n in self.arrays]
            results = self.line(
                lambda *refs: place_body(list(plans.values()), rows, len(held), *refs),
                (self.meta, own, other, *[self.arrays[n] for n in held]),
                [(self.shapes[n], F32) for n in names],
                name=name + "_out",
                held=own.size * 8,
                alias={3 + i: names.index(n) for i, n in enumerate(held)},
                out_left=len(names),
                dma=2 * sum(len(p) for p in plans.values()),
            )
            self.arrays.update(zip(names, results))

        return place


def shards(
    tokens,
    cotangent,
    seq_lengths,
    norm1_gain,
    value_weight,
    ema_delta,
    ema_alpha,
    ema_beta,
    ema_eta,
    ema_omega,
    mix_weight,
    qk_gain,
    qk_bias,
    rel_bias,
    out_weight,
    norm2_gain,
    ffn_in,
    ffn_out,
):
    rows, width = tokens.shape
    hidden = ema_delta.shape[1]
    chunks = rows // CHUNK
    value_width = value_weight.shape[1]
    inner = ffn_in.shape[1]
    mixed = mix_weight.shape[1]
    shared_width = qk_gain.shape[1]
    places = jnp.stack([lax.axis_index("seq"), lax.axis_index("dp")]).astype(jnp.int32)
    meta = jnp.concatenate([places[:1], seq_lengths[0], places[1:]])
    gain1 = norm1_gain[None]
    gain2 = norm2_gain[None]
    omega = ema_omega[None]
    ema = (ema_delta.T, ema_alpha.T, ema_beta.T, ema_eta.T)
    full = (rows, width)
    wide = (rows, value_width)
    thin = (rows, shared_width)
    tiles = (width // 128, rows, 128)
    state = (hidden, width)
    states = (hidden, chunks, width)
    line = Line(PACES)

    share = jax.nn.sigmoid(ema_delta.T)
    logk = jnp.log1p(-share * jax.nn.sigmoid(ema_alpha.T))
    keep = jnp.exp(logk)
    mix = share * ema_beta.T * (ema_eta.T * (1.0 / math.sqrt(hidden)))
    gain_rows = jnp.where(share > -1.0, gain1, 0.0)
    strip = (width // 128, CHUNK, chunks, 128)
    normed, low_normed, enter, end, strips = line(
        start_body,
        (seq_lengths, tokens, gain_rows, logk, keep),
        [(tiles, F32), (full, BF16), (states, F32), (state, F32), (strip, F32)],
        name="norm_and_states",
    )
    other = swap(end, "seq", 1)
    chip_end = line(
        lambda *refs: pair_body(False, rows, *refs), (meta, end, other, logk), [(state, F32)], name="chip_state"
    )[0]
    arrived = [chip_before(chip_end, k) for k in range(1, lax.axis_size("seq") // 2)]
    routes = [route(halving, doubling) for halving, doubling in ROUTES]
    steps = sorted({step for halves, wholes in routes for step in halves})
    smooth = line(local_body, (strips, enter, keep, mix), [(strip, F32)], name="local_average")[0]
    values, values_slope = line(values_body, (low_normed, value_weight), [(wide, BF16), (wide, F32)], name="values")
    low_smoothed, slope_pre, entering = line(
        lambda *refs: carried_body(len(arrived), *refs),
        (meta, other, *arrived, logk, keep, mix, omega, strips, smooth, enter),
        [(full, BF16), (full, F32), (states, F32)],
        scratch=[(state, F32), ((rows, 128), F32)],
        name="carried_average",
    )
    update, candidate, reset, queries, keys, shared, shared_slope = line(
        mix_body,
        (low_smoothed, mix_weight, qk_gain, qk_bias),
        [(full, F32), (full, F32), (wide, F32), (thin, BF16), (thin, BF16), (thin, F32), (thin, F32)],
        name="mix",
    )
    weights, attended, gated = line(
        attend_body,
        (queries, keys, values, rel_bias[None], reset),
        [((rows, SPAN), F32), (wide, F32), (wide, BF16)],
        name="attention",
    )
    residual, change, slope_hidden, normal2, inverse2, low2 = line(
        hidden_body,
        (gated, out_weight, candidate, update, tokens, gain2),
        [(full, F32), (full, F32), (full, F32), (full, F32), ((rows, 128), F32), (full, BF16)],
        name="hidden",
    )
    expanded, slope_exp = line(
        expand_body, (low2, ffn_in), [((rows, inner), BF16), ((rows, inner), F32)], name="expand"
    )
    half = width // 2
    outputs = Outputs(
        line,
        meta,
        {
            "ffn_out": (inner, width),
            "ffn_in": (width, inner),
            "out": (value_width, width),
            "mix": (width, mixed),
            "value": (width, value_width),
        },
    )
    made = {}
    results = {}

    def more():
        while "packed" not in results:
            next(work)
        return results["packed"]

    def last(own, other):
        results["small"] = line(
            finish_body,
            (own, other, *ema),
            [(state, F32)] * 4 + [((1, width), F32)] * 3 + [((2, shared_width), F32)] * 2 + [((1, shared_width), F32)],
            name="parameters",
        )

    def small_piece():
        return Small(line, more(), last)

    def start_piece(number, parts, pairs, height, cols, plans, name):
        kept, *sent = line(
            lambda *refs: weights_body(parts, *refs),
            (meta, *[a for pair in pairs for a in pair]),
            [((height, cols), F32)] + [((height // SWAPS, cols), F32)] * SWAPS,
            name=name + "_grad",
        )
        placer = outputs.placer(plans, name)
        return Piece(line, made, steps, kept, sent, routes[number], placer, name)

    def ffn_out_piece():
        return start_piece(
            0,
            [(0, 0)], [(expanded, cotangent)], inner // 2, width, {"ffn_out": [(0, width, 0, 0)]}, "ffn_out"
        )

    def ffn_in_piece():
        return start_piece(
            1,
            [(0, 0), (inner, 0)],
            [(low2, made["expand_grad"]), (low_smoothed, made["update_grad"])],
            half,
            inner + width,
            {"ffn_in": [(0, inner, 0, 0)], "mix": [(inner, width, 0, 0)]},
            "ffn_in",
        )

    def out_piece():
        return start_piece(
            2,
            [(0, 0), (width, width), (2 * width, 0)],
            [(gated, made["out_grad"]), (gated, made["out_grad"]), (low_smoothed, made["out_grad"])],
            half,
            3 * width,
            {
                "out": [(0, width, 0, 0), (width, width, width, 0)],
                "mix": [(2 * width, width, 0, width + shared_width + value_width)],
            },
            "out",
        )

    def reset_piece():
        return start_piece(
            3,
            [(0, 0)],
            [(low_smoothed, made["reset_grad"])],
            half,
            value_width,
            {"mix": [(0, value_width, 0, width + shared_width)]},
            "reset",
        )

    def value_piece():
        return start_piece(
            4,
            [(0, 0), (value_width, 0)],
            [(low_normed, made["value_grad"]), (low_smoothed, made["shared_grad"])],
            half,
            value_width + shared_width,
            {"value": [(0, value_width, 0, 0)], "mix": [(value_width, shared_width, 0, width)]},
            "value",
        )

    makers = (ffn_out_piece, ffn_in_piece, out_piece, reset_piece, value_piece, small_piece)
    pieces = []

    def advance(i):
        if i < len(pieces) and pieces[i] is not None:
            pieces[i].advance()
        else:
            pieces.extend([None] * (i + 1 - len(pieces)))
            pieces[i] = makers[i]()

    def compute():
        yield
        made["masks"] = line(
            lambda *refs: masks_body(steps, *refs), (meta,), [((len(steps), 8, 128), F32)], name="masks"
        )[0]
        made["expand_grad"] = line(
            expand_back_body, (cotangent, ffn_out, slope_exp), [((rows, inner), BF16)], name="expand_back"
        )[0]
        yield
        input_part, update_grad, out_grad, gain2_grad = line(
            hidden_back_body,
            (made["expand_grad"], ffn_in, normal2, inverse2, gain2, cotangent, update, change, slope_hidden),
            [(full, F32), (full, BF16), (full, BF16), ((1, width), F32)],
            name="hidden_back",
        )
        made["update_grad"], made["out_grad"] = update_grad, out_grad
        yield
        reset_grad, attend_grad = line(
            reset_back_body, (out_grad, out_weight, reset, attended), [(wide, BF16)] * 2, name="reset_back"
        )
        made["reset_grad"] = reset_grad
        yield
        value_grad, shared_grad, small = line(
            attend_back_body,
            (attend_grad, weights, queries, keys, shared, shared_slope, values, values_slope, qk_gain),
            [(wide, BF16), (thin, BF16), ((8, shared_width), F32)],
            name="attention_back",
        )
        made["value_grad"], made["shared_grad"] = value_grad, shared_grad
        yield
        smooth_grad, norm_grad, omega_grad = line(
            smooth_back_body,
            (update_grad, shared_grad, reset_grad, out_grad, value_grad, mix_weight, value_weight, slope_pre)
            + (normed, omega),
            [(tiles, F32), (tiles, F32), ((1, width), F32)],
            name="smooth_back",
        )
        yield
        later, begin, grad_strips = line(
            rise_body,
            (meta, smooth_grad, logk, keep),
            [(states, F32), (state, F32), (strip, F32)],
            name="states_back",
        )
        other_begin = swap(begin, "seq", 1)
        yield
        window = line(
            lambda *refs: pair_body(True, rows, *refs),
            (meta, begin, other_begin, logk),
            [(state, F32)],
            name="chip_grad",
        )[0]
        returned = [chip_after(window, 1)]
        yield
        chips = 1
        while 4 * chips < lax.axis_size("seq"):
            window = line(
                lambda *refs, chips=chips: window_body(chips, rows, *refs),
                (meta, window, returned[-1], logk),
                [(state, F32)],
                name="window_grad",
            )[0]
            chips *= 2
            returned.append(chip_after(window, chips))
            yield
        later = line(
            lambda *refs: carry_back_body(len(returned), *refs),
            (meta, other_begin, *returned, logk, later),
            [(states, F32)],
            name="carry_back",
        )[0]
        yield
        backs = []
        for tile in range(width // 128):
            backs.append(
                line(
                    lambda *refs, tile=tile: state_back_body(tile, *refs),
                    (strips, grad_strips, entering, later, keep, mix),
                    [((rows, 128), F32), ((2 * hidden, 128), F32)],
                    scratch=[((CHUNK, hidden, chunks, 128), F32)],
                    name="state_back",
                )
            )
            yield
        results["input_grad"], results["packed"] = line(
            lambda *refs: close_body(len(backs), *refs),
            (*[b[0] for b in backs], *[b[1] for b in backs], tokens, gain1, norm_grad, input_part)
            + (omega_grad, gain2_grad, small),
            [(full, F32), ((SMALL_ROWS, value_width + shared_width), F32)],
            name="norm_back",
        )
        yield
        results["block_out"] = line(block_body, (residual, expanded, ffn_out), [(full, F32)], name="block_out")[0]

    work = compute()
    for item in "".join(ORDER):
        if item.isdigit():
            advance(int(item))
        else:
            next(work, None)
    for _ in work:
        pass
    for i in range(len(pieces), len(makers)):
        advance(i)
    while not all(p.done for p in pieces):
        for i in range(len(pieces)):
            advance(i)
    sums = outputs.arrays
    small = results["small"]
    return (
        results["block_out"],
        results["input_grad"],
        small[4][0],
        sums["value"],
        *[g.T for g in small[:4]],
        small[6][0],
        sums["mix"],
        small[7],
        small[8],
        small[9][0],
        sums["out"],
        small[5][0],
        sums["ffn_in"],
        sums["ffn_out"],
    )


def solution(mesh):
    rows = P(("dp", "seq"), None)
    in_specs = (rows, rows, P("dp", None)) + (P(),) * 15
    out_specs = (rows, rows) + (P(),) * 15
    return jax.shard_map(shards, mesh=mesh, in_specs=in_specs, out_specs=out_specs, check_vma=False)
```

```python
import math

import jax
import jax.numpy as jnp
from jax import lax
from jax.experimental import pallas as pl
from jax.experimental.pallas import tpu as pltpu
from jax.sharding import PartitionSpec as P

SPAN = 128
CHUNK = 64
EPS = 1e-05
BF16 = jnp.bfloat16
F32 = jnp.float32
ROOM = 2 * 1024 * 1024
SWAPS = 1
SMALL_ROWS = 24


def sigmoid(a):
    return 0.5 * jnp.tanh(0.5 * a) + 0.5


def mm(a, b):
    return lax.dot_general(a, b, (((1,), (0,)), ((), ())), preferred_element_type=F32)


def mm_nt(a, b):
    return lax.dot_general(a, b, (((1,), (1,)), ((), ())), preferred_element_type=F32)


def mm_tn(a, b):
    return lax.dot_general(a, b, (((0,), (0,)), ((), ())), preferred_element_type=F32)


class Place:
    def __init__(self, lengths):
        self.lengths = lengths
        self.shape = (lengths.shape[1] + 2,)

    def __getitem__(self, i):
        if i == 0:
            return lax.axis_index("seq")
        return self.lengths[0, i - 1]


class Line:
    def __init__(self, paces):
        self.token = None
        self.paces = paces
        self.count = 0

    def __call__(self, body, ins, outs, scratch=(), name=None, held=None, left=(), alias=None, out_left=0, dma=0):
        count = len(ins)
        before = () if self.token is None else (self.token,)
        alias = alias or {}
        specs = []
        for i, a in enumerate(ins):
            if i in left:
                specs.append(pl.BlockSpec(memory_space=pltpu.HBM))
            elif i in alias:
                specs.append(pl.BlockSpec(memory_space=pl.ANY))
            else:
                specs.append(pl.BlockSpec(memory_space=pltpu.SMEM if a.dtype == jnp.int32 else pltpu.VMEM))
        specs += [pl.BlockSpec(memory_space=pl.ANY)] * len(before)
        if held is None:
            held = sum(a.size * a.dtype.itemsize for a in ins if a.dtype != jnp.int32)
            held += sum(math.prod(s) * jnp.dtype(d).itemsize for s, d in tuple(outs) + tuple(scratch))
        first = count + len(before)

        def run(*refs):
            body(*refs[:count], *refs[first : first + len(outs)], *refs[first + len(outs) + 1 :])
            refs[first + len(outs)][...] = jnp.zeros((8, 128), F32)

        places = [pl.ANY if i < out_left else pltpu.VMEM for i in range(len(outs))]
        scratches = [pltpu.VMEM(s, d) for s, d in scratch]
        if dma:
            scratches.append(pltpu.SemaphoreType.DMA((dma,)))
        pace = self.paces[self.count] if self.count < len(self.paces) else 0
        self.count += 1
        result = pl.pallas_call(
            run,
            in_specs=specs,
            out_specs=[pl.BlockSpec(memory_space=m) for m in places + [pltpu.VMEM]],
            out_shape=[jax.ShapeDtypeStruct(s, d) for s, d in outs] + [jax.ShapeDtypeStruct((8, 128), F32)],
            scratch_shapes=scratches,
            input_output_aliases=alias,
            compiler_params=pltpu.CompilerParams(vmem_limit_bytes=int(held * 1.05) + ROOM),
            cost_estimate=pl.CostEstimate(flops=int(pace * 1e9), bytes_accessed=0, transcendentals=0),
            name=name,
        )(*ins, *before)
        self.token = result[-1]
        return result[:-1]


def clear_range(meta, low, high):
    count = meta.shape[0] - 2
    begin = jnp.int32(0)
    hit = jnp.bool_(False)
    for i in range(count):
        length = meta[1 + i]
        hit = hit | ((length > 0) & (begin >= low) & (begin < high))
        begin = begin + length
    return jnp.where(hit, 0.0, 1.0).astype(F32)


def chunk_masks(meta, first, chunks):
    rows = lax.broadcasted_iota(jnp.int32, (chunks, 128), 0)
    free = jnp.ones((chunks, 128), F32)
    for s in range(0, chunks, SPAN // CHUNK):
        position = first + s * CHUNK
        free = jnp.where(rows == s, clear_range(meta, position, position + 1), free)
    return free


def lanes_of(tile):
    return pl.ds(tile * 128, 128)


def tiled(ref):
    return jnp.concatenate([ref[i] for i in range(ref.shape[0])], axis=1)


def put_tiled(ref, value):
    for i in range(ref.shape[0]):
        ref[i] = value[:, i * 128 : (i + 1) * 128]


def scan_step(masks, values, decay_row, shifts, chunks):
    power = decay_row
    for i, mask in enumerate(masks):
        values = values + power * (mask * pltpu.roll(values, shifts[i], 0))
        power = power * power
    return values


def doubling_masks(mask, chunks, backward):
    masks = []
    distance = 1
    while distance < chunks:
        masks.append(mask)
        shift = chunks - distance if backward else distance
        mask = mask * pltpu.roll(mask, shift, 0)
        distance *= 2
    shifts = []
    distance = 1
    while distance < chunks:
        shifts.append(chunks - distance if backward else distance)
        distance *= 2
    return masks, shifts


def edge_masks(free, chunks, backward):
    rows = lax.broadcasted_iota(jnp.int32, (chunks, 128), 0)
    if backward:
        return jnp.where(rows == chunks - 1, 0.0, pltpu.roll(free, chunks - 1, 0))
    return jnp.where(rows == 0, 0.0, free)


def prefix_mask(free, chunks, backward):
    rows = lax.broadcasted_iota(jnp.int32, (chunks, 128), 0)
    if backward:
        reach = jnp.where(rows == chunks - 1, 1.0, pltpu.roll(free, chunks - 1, 0))
    else:
        reach = free
    distance = 1
    while distance < chunks:
        if backward:
            moved = jnp.where(rows >= chunks - distance, 1.0, pltpu.roll(reach, chunks - distance, 0))
        else:
            moved = jnp.where(rows < distance, 1.0, pltpu.roll(reach, distance, 0))
        reach = reach * moved
        distance *= 2
    return reach


def start_body(lengths, tok, gain, logk, keep, normed, low, enter, end, strips):
    meta = Place(lengths)
    tokens, width = tok.shape
    hidden = end.shape[0]
    chunks = tokens // CHUNK
    x = tok[...].astype(F32)
    centered = x - jnp.mean(x, axis=1, keepdims=True)
    spread = jnp.mean(centered * centered, axis=1, keepdims=True)
    rows = centered * lax.rsqrt(spread + EPS) * gain[0:1, :]
    put_tiled(normed, rows)
    low[...] = rows.astype(BF16)
    free = chunk_masks(meta, meta[0] * tokens, chunks)
    edge = edge_masks(free, chunks, False)
    masks, shifts = doubling_masks(edge, chunks, False)
    for tile in range(width // 128):
        lanes = lanes_of(tile)
        keeps = [keep[h : h + 1, lanes] for h in range(hidden)]

        def step(t, state):
            value = normed[tile, pl.ds(t, chunks, stride=CHUNK), :]
            strips[tile, t] = value
            return tuple(k * u + value for k, u in zip(keeps, state))

        zero = jnp.zeros((chunks, 128), F32)
        state = lax.fori_loop(0, CHUNK, step, (zero,) * hidden, unroll=8)
        for h in range(hidden):
            decay = jnp.exp(CHUNK * logk[h : h + 1, lanes])
            reached = scan_step(masks, state[h], decay, shifts, chunks)
            enter[h, :, lanes] = edge * pltpu.roll(reached, 1, 0)
            end[h : h + 1, lanes] = reached[chunks - 1 : chunks]


def values_body(low, weight, values, slope):
    for b in range(weight.shape[1] // 256):
        cols = pl.ds(b * 256, 256)
        raw = mm(low[...], weight[:, cols])
        gate = sigmoid(raw)
        out = raw * gate
        values[:, cols] = out.astype(BF16)
        slope[:, cols] = gate + out * (1.0 - gate)


def add_up(parts):
    while len(parts) > 1:
        parts = [a + b for a, b in zip(parts[::2], parts[1::2])]
    return parts[0]


def local_body(strips, enter, keep, mix, smooth):
    hidden = keep.shape[0]
    for tile in range(strips.shape[0]):
        lanes = lanes_of(tile)
        keeps = [keep[h : h + 1, lanes] for h in range(hidden)]
        mixes = [mix[h : h + 1, lanes] for h in range(hidden)]

        def step(t, state):
            value = strips[tile, t]
            state = tuple(k * u + value for k, u in zip(keeps, state))
            smooth[tile, t] = add_up([c * u for c, u in zip(mixes, state)])
            return state

        lax.fori_loop(0, CHUNK, step, tuple(enter[h, :, lanes] for h in range(hidden)), unroll=8)


def pair_body(backward, tokens, meta, own, other, logk, out):
    core = meta[0] % 2
    first = (meta[0] - core) * tokens
    middle = first + tokens
    decay = jnp.exp(tokens * logk[...])
    if backward:
        reach = clear_range(meta, first + 1, middle + 1)
        near = jnp.where(core == 0, own[...], other[...])
        far = jnp.where(core == 0, other[...], own[...])
    else:
        reach = clear_range(meta, middle, middle + tokens)
        near = jnp.where(core == 0, other[...], own[...])
        far = jnp.where(core == 0, own[...], other[...])
    out[...] = near + (reach * decay) * far


def window_body(count, tokens, meta, near, far, logk, out):
    span = 2 * tokens
    first = (meta[0] - meta[0] % 2) * tokens
    reach = clear_range(meta, first + 1, first + count * span + 1)
    out[...] = near[...] + (reach * jnp.exp((count * span) * logk[...])) * far[...]


def carry_of(backward, tokens, meta, other, arrived, logk):
    core = meta[0] % 2
    first = (meta[0] - core) * tokens
    span = 2 * tokens
    total = None
    for k, part in arrived:
        if backward:
            reach = clear_range(meta, first + span, first + (k + 1) * span + 1)
        else:
            reach = clear_range(meta, first - k * span, first)
        term = part[...] * reach
        if k:
            term = term * jnp.exp((k * span) * logk[...])
        total = term if total is None else total + term
    decay = jnp.exp(tokens * logk[...])
    middle = first + tokens
    if backward:
        crossing = clear_range(meta, middle, middle + 1)
        through = clear_range(meta, middle + 1, middle + tokens)
        passed = crossing * (other[...] + (through * decay) * total)
        return jnp.where(core == 0, passed, total)
    through = clear_range(meta, first, middle)
    return jnp.where(core == 0, total, other[...] + (through * decay) * total)


def reversed_lanes(row):
    size = row.shape[1]
    down = lax.broadcasted_iota(jnp.int32, (size, size), 0)
    across = lax.broadcasted_iota(jnp.int32, (size, size), 1)
    turn = jnp.where((down + across) % size == 0, 1.0, 0.0).astype(F32)
    return jnp.dot(row, turn, precision=lax.Precision.HIGHEST, preferred_element_type=F32)


def carried_body(chips, meta, other, *rest):
    arrived = rest[:chips]
    logk, keep, mix, omega, strips, smooth, enter, low, slope, states, carry, rows = rest[chips:]
    tiles, _, chunks, _ = strips.shape
    tokens = chunks * CHUNK
    hidden = keep.shape[0]
    carry[...] = carry_of(False, tokens, meta, other, list(enumerate(arrived)), logk)
    free = chunk_masks(meta, meta[0] * tokens, chunks)
    reach = prefix_mask(free, chunks, False)
    offset = (lax.broadcasted_iota(jnp.int32, (chunks, 128), 0) * CHUNK).astype(F32)
    for tile in range(tiles):
        lanes = lanes_of(tile)
        state = []
        for h in range(hidden):
            entry = jnp.exp(offset * logk[h : h + 1, lanes]) * reach
            first = carry[h : h + 1, lanes] * entry
            states[h, :, lanes] = enter[h, :, lanes] + first
            state.append(mix[h : h + 1, lanes] * first)
        keeps = [keep[h : h + 1, lanes] for h in range(hidden)]
        skip = omega[:, lanes]

        def step(t, state):
            state = tuple(k * u for k, u in zip(keeps, state))
            pre = smooth[tile, t] + skip * strips[tile, t] + add_up(list(state))
            rows[pl.ds(t, chunks, stride=CHUNK), :] = pre
            return state

        lax.fori_loop(0, CHUNK, step, tuple(state), unroll=8)
        pre = rows[...]
        gate = sigmoid(pre)
        smoothed = pre * gate
        low[:, lanes] = smoothed.astype(BF16)
        slope[:, lanes] = gate + smoothed * (1.0 - gate)


def layer_grad(weighted, normal, inverse):
    mean_one = jnp.mean(weighted, axis=1, keepdims=True)
    mean_two = jnp.mean(weighted * normal, axis=1, keepdims=True)
    return (weighted - mean_one - normal * mean_two) * inverse


def shift_rows(table, down):
    size = table.shape[0]
    rows = lax.broadcasted_iota(jnp.int32, table.shape, 0)
    bit = 1
    while bit < size:
        moved = pltpu.roll(table, bit if down else size - bit, 1)
        table = jnp.where((rows & bit) != 0, moved, table)
        bit *= 2
    return table


def mix_body(low, mix_weight, qk_gain, qk_bias, update, candidate, reset, queries, keys, shared, shared_slope):
    width = update.shape[1]
    base = width + shared.shape[1]
    top = base + reset.shape[1]
    raw = mm(low[...], mix_weight[:, width:base])
    gate = sigmoid(raw)
    silu = raw * gate
    shared[...] = silu
    shared_slope[...] = gate + silu * (1.0 - gate)
    queries[...] = (silu * qk_gain[0:1] + qk_bias[0:1]).astype(BF16)
    keys[...] = (silu * qk_gain[1:2] + qk_bias[1:2]).astype(BF16)
    for b in range(width // 256):
        update[:, b * 256 : (b + 1) * 256] = sigmoid(mm(low[...], mix_weight[:, b * 256 : (b + 1) * 256]))
    for b in range(reset.shape[1] // 256):
        reset[:, b * 256 : (b + 1) * 256] = mm(low[...], mix_weight[:, base + b * 256 : base + (b + 1) * 256])
    for b in range(width // 256):
        candidate[:, b * 256 : (b + 1) * 256] = mm(low[...], mix_weight[:, top + b * 256 : top + (b + 1) * 256])


def attend_body(queries, keys, values, rel_bias, reset, weights, attended, gated):
    tokens, shared_width = queries.shape
    place = lax.broadcasted_iota(jnp.int32, (SPAN, SPAN), 0)
    causal = place >= lax.broadcasted_iota(jnp.int32, (SPAN, SPAN), 1)
    turned = jnp.broadcast_to(reversed_lanes(jnp.broadcast_to(rel_bias[...], (8, SPAN)))[0:1], (SPAN, SPAN))
    bias = shift_rows(turned, True)
    scale = 1.0 / math.sqrt(shared_width)
    for s in range(tokens // SPAN):
        rows = pl.ds(s * SPAN, SPAN)
        scores = mm_nt(queries[rows, :], keys[rows, :]) * scale + bias
        scores = jnp.where(causal, scores, -1e30)
        powers = jnp.exp(scores - jnp.max(scores, axis=1, keepdims=True))
        share = powers / jnp.sum(powers, axis=1, keepdims=True)
        weights[rows, :] = share
        rise = mm(share.astype(BF16), values[rows, :])
        attended[rows, :] = rise
        raw = reset[rows, :]
        gated[rows, :] = (raw * sigmoid(raw) * rise).astype(BF16)


def hidden_body(
    gated, out_weight, candidate, update, tok, gain2, residual, change, slope_hidden, normal2, inverse2, low2
):
    total = candidate[...] + mm(gated[...], out_weight[...])
    gate = sigmoid(total)
    hidden_rows = total * gate
    slope_hidden[...] = gate + hidden_rows * (1.0 - gate)
    x = tok[...].astype(F32)
    moved = hidden_rows - x
    change[...] = moved
    rows = x + update[...] * moved
    residual[...] = rows
    centered = rows - jnp.mean(rows, axis=1, keepdims=True)
    inverse = lax.rsqrt(jnp.mean(centered * centered, axis=1, keepdims=True) + EPS)
    normal = centered * inverse
    normal2[...] = normal
    inverse2[...] = jnp.broadcast_to(inverse, inverse2.shape)
    low2[...] = (normal * gain2[...]).astype(BF16)


def expand_body(low2, ffn_in, expanded, slope_exp):
    for b in range(ffn_in.shape[1] // 256):
        cols = pl.ds(b * 256, 256)
        raw = mm(low2[...], ffn_in[:, cols])
        gate = sigmoid(raw)
        silu = raw * gate
        expanded[:, cols] = silu.astype(BF16)
        slope_exp[:, cols] = gate + silu * (1.0 - gate)


def weights_body(parts, meta, *refs):
    kept, sent = refs[-SWAPS - 1], refs[-SWAPS:]
    pairs = refs[: -SWAPS - 1]
    half = kept.shape[0]
    core = meta[0] % 2
    for mine, side in ((False, 1 - core), (True, core)):
        for i, (column, block) in enumerate(parts):
            left, right = pairs[2 * i], pairs[2 * i + 1]
            begin = pl.multiple_of(side * half + block, 128)
            cols = slice(column, column + right.shape[1])
            value = mm_tn(left[:, pl.ds(begin, half)], right[...])
            if mine:
                kept[:, cols] = value
            else:
                for j, target in enumerate(sent):
                    target[:, cols] = value[j * half // SWAPS : (j + 1) * half // SWAPS]


def block_body(residual, expanded, ffn_out, out):
    out[...] = residual[...] + mm(expanded[...], ffn_out[...])


def expand_back_body(cot, ffn_out, slope_exp, expand_grad):
    for b in range(ffn_out.shape[0] // 256):
        cols = pl.ds(b * 256, 256)
        expand_grad[:, cols] = (mm_nt(cot[...], ffn_out[cols, :]) * slope_exp[:, cols]).astype(BF16)


def hidden_back_body(
    expand_grad,
    ffn_in,
    normal2,
    inverse2,
    gain2,
    cot,
    update,
    change,
    slope_hidden,
    input_part,
    update_grad,
    out_grad,
    gain2_grad,
):
    norm_out = mm_nt(expand_grad[...], ffn_in[...])
    normal = normal2[...]
    gain2_grad[...] = jnp.sum(norm_out * normal, axis=0, keepdims=True)
    upstream = cot[...].astype(F32) + layer_grad(norm_out * gain2[...], normal, inverse2[:, 0:1])
    gates = update[...]
    input_part[...] = upstream * (1.0 - gates)
    update_grad[...] = (upstream * change[...] * gates * (1.0 - gates)).astype(BF16)
    out_grad[...] = (upstream * gates * slope_hidden[...]).astype(BF16)


def reset_back_body(out_grad, out_weight, reset, attended, reset_grad, attend_grad):
    for b in range(reset.shape[1] // 256):
        cols = pl.ds(b * 256, 256)
        rise = mm_nt(out_grad[...], out_weight[cols, :])
        raw = reset[:, cols]
        gate = sigmoid(raw)
        silu = raw * gate
        reset_grad[:, cols] = (rise * attended[:, cols] * (gate + silu * (1.0 - gate))).astype(BF16)
        attend_grad[:, cols] = (rise * silu).astype(BF16)


def attend_back_body(
    attend_grad,
    weights,
    queries,
    keys,
    shared,
    shared_slope,
    values,
    values_slope,
    qk_gain,
    value_grad,
    shared_grad,
    small,
):
    tokens, shared_width = queries.shape
    scale = 1.0 / math.sqrt(shared_width)
    slopes = jnp.zeros((SPAN, SPAN), F32)
    for s in range(tokens // SPAN):
        rows = pl.ds(s * SPAN, SPAN)
        upstream = attend_grad[rows, :]
        share = weights[rows, :]
        rise = mm_nt(upstream, values[rows, :])
        value_rise = mm_tn(share.astype(BF16), upstream)
        value_grad[rows, :] = (value_rise * values_slope[rows, :]).astype(BF16)
        score_grad = share * (rise - jnp.sum(share * rise, axis=1, keepdims=True))
        slopes = slopes + score_grad
        low = (score_grad * scale).astype(BF16)
        query_grad = mm(low, keys[rows, :])
        key_grad = mm_tn(low, queries[rows, :])
        silu = shared[rows, :]
        pieces = (
            jnp.sum(query_grad * silu, axis=0, keepdims=True),
            jnp.sum(key_grad * silu, axis=0, keepdims=True),
            jnp.sum(query_grad, axis=0, keepdims=True),
            jnp.sum(key_grad, axis=0, keepdims=True),
        )
        sums = pieces if s == 0 else tuple(a + b for a, b in zip(sums, pieces))
        back = query_grad * qk_gain[0:1] + key_grad * qk_gain[1:2]
        shared_grad[rows, :] = (back * shared_slope[rows, :]).astype(BF16)
    small[...] = jnp.zeros_like(small)
    for i in range(4):
        small[i : i + 1, :] = sums[i]
    turned = jnp.sum(shift_rows(slopes, False), axis=0, keepdims=True)
    small[4:5, :] = reversed_lanes(jnp.broadcast_to(turned, (8, SPAN)))[0:1]


def smooth_back_body(
    update_grad,
    shared_grad,
    reset_grad,
    out_grad,
    value_grad,
    mix_weight,
    value_weight,
    slope_pre,
    normed,
    omega,
    smooth_grad,
    norm_grad,
    omega_grad,
):
    width = update_grad.shape[1]
    base = width + shared_grad.shape[1]
    top = base + reset_grad.shape[1]
    rise = mm_nt(reset_grad[...], mix_weight[:, base:top])
    rise = rise + mm_nt(update_grad[...], mix_weight[:, :width])
    rise = rise + mm_nt(out_grad[...], mix_weight[:, top:])
    rise = rise + mm_nt(shared_grad[...], mix_weight[:, width:base])
    grad = rise * slope_pre[...]
    put_tiled(smooth_grad, grad)
    put_tiled(norm_grad, mm_nt(value_grad[...], value_weight[...]) + omega[...] * grad)
    omega_grad[...] = jnp.sum(grad * tiled(normed), axis=0, keepdims=True)


def rise_body(meta, smooth_grad, logk, keep, enter, end, strips):
    tiles, tokens, _ = smooth_grad.shape
    hidden = keep.shape[0]
    chunks = tokens // CHUNK
    free = chunk_masks(meta, meta[0] * tokens, chunks)
    edge = edge_masks(free, chunks, True)
    masks, shifts = doubling_masks(edge, chunks, True)
    for tile in range(tiles):
        lanes = lanes_of(tile)
        keeps = [keep[h : h + 1, lanes] for h in range(hidden)]

        def step(t, state):
            value = smooth_grad[tile, pl.ds(CHUNK - 1 - t, chunks, stride=CHUNK), :]
            strips[tile, CHUNK - 1 - t] = value
            return tuple(k * u + value for k, u in zip(keeps, state))

        zero = jnp.zeros((chunks, 128), F32)
        state = lax.fori_loop(0, CHUNK, step, (zero,) * hidden, unroll=8)
        for h in range(hidden):
            decay = jnp.exp(CHUNK * logk[h : h + 1, lanes])
            reached = scan_step(masks, state[h], decay, shifts, chunks)
            enter[h, :, lanes] = edge * pltpu.roll(reached, chunks - 1, 0)
            end[h : h + 1, lanes] = reached[0:1]


def carry_back_body(chips, meta, other, *rest):
    arrived = rest[:chips]
    logk, enter, later = rest[chips:]
    hidden, chunks, width = enter.shape
    tokens = chunks * CHUNK
    carry = carry_of(True, tokens, meta, other, [(2**j - 1, part) for j, part in enumerate(arrived)], logk)
    free = chunk_masks(meta, meta[0] * tokens, chunks)
    reach = prefix_mask(free, chunks, True)
    offset = ((chunks - 1 - lax.broadcasted_iota(jnp.int32, (chunks, 128), 0)) * CHUNK).astype(F32)
    for tile in range(width // 128):
        lanes = lanes_of(tile)
        for h in range(hidden):
            entry = jnp.exp(offset * logk[h : h + 1, lanes]) * reach
            later[h, :, lanes] = enter[h, :, lanes] + carry[h : h + 1, tile * 128 : (tile + 1) * 128] * entry


def state_back_body(tile, strips, grads, states, later, keep, mix, part, sums, history):
    hidden = keep.shape[0]
    chunks = states.shape[1]
    lanes = lanes_of(tile)
    heads = range(hidden)
    keeps = [keep[h : h + 1, lanes] for h in heads]
    mixes = [mix[h : h + 1, lanes] for h in heads]
    zeros = (jnp.zeros((chunks, 128), F32),) * hidden

    def rise(t, held):
        state, reads = held
        value = strips[tile, t]
        grad = grads[tile, t]
        state = tuple(k * u + value for k, u in zip(keeps, state))
        reads = tuple(r + u * grad for r, u in zip(reads, state))
        for i in heads:
            history[t, i] = state[i]
        return state, reads

    first = tuple(states[h, :, lanes] for h in heads)
    _, reads = lax.fori_loop(0, CHUNK, rise, (first, zeros), unroll=4)
    for h in heads:
        sums[h : h + 1, :] = jnp.sum(reads[h], axis=0, keepdims=True)

    def fall(i, held):
        state, marks = held
        t = CHUNK - 1 - i
        grad = grads[tile, t]
        state = tuple(k * w + grad for k, w in zip(keeps, state))
        marks = tuple(m + w * history[t, j] for j, (m, w) in enumerate(zip(marks, state)))
        part[pl.ds(t, chunks, stride=CHUNK), :] = add_up([c * w for c, w in zip(mixes, state)])
        return state, marks

    first = tuple(later[h, :, lanes] for h in heads)
    _, marks = lax.fori_loop(0, CHUNK, fall, (first, zeros), unroll=4)
    for h in heads:
        sums[hidden + h : hidden + h + 1, :] = jnp.sum(marks[h], axis=0, keepdims=True)


def close_body(count, *refs):
    totals = refs[:count]
    sums = refs[count : 2 * count]
    tok, gain, norm_grad, input_part, omega_grad, gain2_grad, small, input_grad, packed = refs[2 * count :]
    x = tok[...].astype(F32)
    width = x.shape[1]
    centered = x - jnp.mean(x, axis=1, keepdims=True)
    inverse = lax.rsqrt(jnp.mean(centered * centered, axis=1, keepdims=True) + EPS)
    normal = centered * inverse
    upstream = tiled(norm_grad) + jnp.concatenate([t[...] for t in totals], axis=1)
    input_grad[...] = input_part[...] + layer_grad(upstream * gain[...], normal, inverse)
    at = sums[0].shape[0] // 2
    packed[...] = jnp.zeros_like(packed)
    for i in range(count):
        packed[0:at, i * 128 : (i + 1) * 128] = sums[i][0:at, :]
        packed[0:at, width + i * 128 : width + (i + 1) * 128] = sums[i][at : 2 * at, :]
    packed[at : at + 1, :width] = jnp.sum(upstream * normal, axis=0, keepdims=True)
    packed[at : at + 1, width : 2 * width] = gain2_grad[...]
    packed[at + 1 : at + 2, :width] = omega_grad[...]
    packed[0:8, 2 * width : 2 * width + small.shape[1]] = small[...]


def finish_body(own, other, delta, alpha, beta, eta, *outs):
    delta_grad, alpha_grad, beta_grad, eta_grad, gain1_grad, gain2_grad, omega_grad, qk_gain_grad, qk_bias_grad, rel_grad = outs
    hidden, width = delta_grad.shape
    scale = 1.0 / math.sqrt(hidden)
    packed = own[...] + other[...]
    read = packed[0:hidden, :width]
    mark = packed[0:hidden, width : 2 * width]
    share = jax.nn.sigmoid(delta[...])
    damp = jax.nn.sigmoid(alpha[...])
    inflow = share * beta[...]
    outflow = eta[...] * scale
    eta_grad[...] = inflow * read * scale
    inflow_grad = outflow * read
    beta_grad[...] = share * inflow_grad
    rate = inflow * outflow * (mark - read) / (share * damp - 1.0)
    share_grad = beta[...] * inflow_grad + damp * rate
    delta_grad[...] = share_grad * share * (1.0 - share)
    alpha_grad[...] = share * rate * damp * (1.0 - damp)
    gain1_grad[...] = packed[hidden : hidden + 1, :width]
    gain2_grad[...] = packed[hidden : hidden + 1, width : 2 * width]
    omega_grad[...] = packed[hidden + 1 : hidden + 2, :width]
    tail = slice(2 * width, 2 * width + rel_grad.shape[1])
    qk_gain_grad[...] = packed[0:2, tail]
    qk_bias_grad[...] = packed[2:4, tail]
    rel_grad[...] = packed[4:5, tail]


def swap(a, axis, bit):
    count = lax.axis_size(axis)
    return lax.ppermute(a, axis, [(i, i ^ bit) for i in range(count)])


def chip_before(state, chips):
    count = lax.axis_size("seq")
    return lax.ppermute(state, "seq", [(i, i + 2 * chips) for i in range(count - 2 * chips)])


def chip_after(state, chips):
    count = lax.axis_size("seq")
    return lax.ppermute(state, "seq", [(i, i - 2 * chips) for i in range(2 * chips, count)])


def axis_bits(axis, least):
    bits = []
    bit = least
    while bit < lax.axis_size(axis):
        bits.append((axis, bit))
        bit *= 2
    return bits


def cross(a, step):
    seq = lax.axis_size("seq")
    moves = []
    for i in range(lax.axis_size("dp") * seq):
        axis, bit = step[i % 2]
        moves.append((i, i ^ (bit * seq if axis == "dp" else bit)))
    return lax.ppermute(a, ("dp", "seq"), moves)


ROUTES = (
    (("xy", "yx"), "12"),
    (("xy1", "yx1"), "2"),
    (("xy1", "yx1"), "2"),
    (("xy1", "yx1"), "2"),
    (("1xy", "1yx"), "2"),
)
ORDER = (
    "CCKC1C410C40KK1K2104231K",
    "KK0431201K32143K2K103405",
    "214302435250S35425304235",
    "3",
)
PACES = (
    8, 8, 8, 8, 8, 8, 8, 8, 8, 8, 8, 8, 0, 0, 0, 0, 8, 8, 12, 12, 12, 12, 8, 3, 12, 12, 12, 8, 12,
    12, 10, 10, 10, 10, 2, 1, 1, 1, 1, 10, 10, 8, 8, 8, 8, 1.5, 0.6, 3, 8, 8, 8, 8, 8, 8, 12, 8, 4,
    2, 8, 8, 8, 0.3, 0.3, 12, 12, 12, 8, 8, 0, 3, 8, 8, 8, 12, 12, 6, 10, 8, 12, 0, 8, 8, 8, 12, 8,
    0, 0, 0, 0, 8,
)
BITS = {"x": ("dp", 1), "y": ("dp", 2), "1": ("seq", 2), "2": ("seq", 4)}


def route(halving, doubling):
    named = lambda pair: all(BITS[c][1] < lax.axis_size(BITS[c][0]) for c in pair)
    halves = [tuple(BITS[c] for c in pair) for pair in zip(*halving) if named(pair)]
    wholes = [(BITS[c], BITS[c]) for c in doubling if named(c)]
    for bit in axis_bits("dp", 1) + axis_bits("seq", 2):
        if bit not in BITS.values():
            halves.append((bit, bit))
    return halves, wholes


def masks_body(steps, meta, out):
    for i, step in enumerate(steps):
        place = [(meta[0] if axis == "seq" else meta[meta.shape[0] - 1]) // bit % 2 for axis, bit in step]
        side = jnp.where(meta[0] % 2 == 0, place[0], place[1])
        out[i] = jnp.full((8, 128), side.astype(F32))


def split_body(index, masks, kept, *refs):
    arrived, (keep, send) = refs[:-2], refs[-2:]
    half = keep.shape[0]
    upper = masks[index, 0:1, 0:1] > 0.5
    came = jnp.concatenate([a[...] for a in arrived], axis=0) if len(arrived) > 1 else arrived[0][...]
    total = kept[...] + came
    low, high = total[:half], total[half:]
    keep[...] = jnp.where(upper, high, low)
    send[...] = jnp.where(upper, low, high)


def sum_body(kept, arrived, out):
    out[...] = kept[...] + arrived[...]


def join_body(index, masks, own, other, out):
    half = own.shape[0]
    upper = masks[index, 0:1, 0:1] > 0.5
    out[:half, :] = jnp.where(upper, other[...], own[...])
    out[half:, :] = jnp.where(upper, own[...], other[...])


class Piece:
    def __init__(self, line, made, steps, kept, sent, routes, outputs, name):
        self.line, self.made, self.steps, self.name = line, made, steps, name
        self.outputs = outputs
        self.work = self.run(kept, sent, *routes)
        self.done = False
        self.advance()

    def advance(self):
        if not self.done:
            self.done = next(self.work, "end") == "end"

    def run(self, kept, sent, halves, wholes):
        line = self.line
        arrived = [swap(a, "seq", 1) for a in sent]
        yield
        masks = self.made["masks"]
        for step in halves:
            rows, cols = kept.shape
            kept, send = line(
                lambda *refs, index=self.steps.index(step): split_body(index, *refs),
                (masks, kept, *arrived),
                [((rows // 2, cols), F32)] * 2,
                name=self.name + "_split",
            )
            arrived = [cross(send, step)]
            yield
        for step in list(wholes) + [None]:
            kept = line(sum_body, (kept, arrived[0]), [(kept.shape, F32)], name=self.name + "_sum")[0]
            if step is not None:
                arrived = [cross(kept, step)]
                yield
        part = kept
        for step in reversed(halves):
            other = cross(part, step)
            yield
            rows, cols = part.shape
            part = line(
                lambda *refs, index=self.steps.index(step): join_body(index, *refs),
                (masks, part, other),
                [((2 * rows, cols), F32)],
                name=self.name + "_join",
            )[0]
        other = swap(part, "seq", 1)
        yield
        self.outputs(part, other, part.shape[0])


class Small:
    def __init__(self, line, part, last):
        self.work = self.run(line, part, last)
        self.done = False
        self.advance()

    def advance(self):
        if not self.done:
            self.done = next(self.work, "end") == "end"

    def run(self, line, part, last):
        flat = axis_bits("dp", 1)
        steps = list(zip(flat, flat[::-1])) + [(bit, bit) for bit in axis_bits("seq", 2)]
        other = swap(part, "seq", 1)
        yield
        for step in steps:
            part = line(sum_body, (part, other), [(part.shape, F32)], name="small_sum")[0]
            other = cross(part, step)
            yield
        last(part, other)


def place_body(plans, rows, count, meta, own, other, *refs):
    outs = refs[count : count + len(plans)]
    sems = refs[-1]
    core = meta[0] % 2
    copies = []
    for part, side in ((own, core), (other, 1 - core)):
        for out, plan in zip(outs, plans):
            for column, width, row, place in plan:
                begin = pl.multiple_of(side * rows + row, 8)
                copies.append(
                    pltpu.make_async_copy(
                        part.at[pl.ds(0, rows), pl.ds(column, width)],
                        out.at[pl.ds(begin, rows), pl.ds(place, width)],
                        sems.at[len(copies)],
                    )
                )
                copies[-1].start()
    for copy in copies:
        copy.wait()


class Outputs:
    def __init__(self, line, meta, shapes):
        self.line, self.meta, self.shapes, self.arrays = line, meta, shapes, {}

    def placer(self, plans, name):
        def place(own, other, rows):
            names = list(plans)
            held = [n for n in names if n in self.arrays]
            results = self.line(
                lambda *refs: place_body(list(plans.values()), rows, len(held), *refs),
                (self.meta, own, other, *[self.arrays[n] for n in held]),
                [(self.shapes[n], F32) for n in names],
                name=name + "_out",
                held=own.size * 8,
                alias={3 + i: names.index(n) for i, n in enumerate(held)},
                out_left=len(names),
                dma=2 * sum(len(p) for p in plans.values()),
            )
            self.arrays.update(zip(names, results))

        return place


def shards(
    tokens,
    cotangent,
    seq_lengths,
    norm1_gain,
    value_weight,
    ema_delta,
    ema_alpha,
    ema_beta,
    ema_eta,
    ema_omega,
    mix_weight,
    qk_gain,
    qk_bias,
    rel_bias,
    out_weight,
    norm2_gain,
    ffn_in,
    ffn_out,
):
    rows, width = tokens.shape
    hidden = ema_delta.shape[1]
    chunks = rows // CHUNK
    value_width = value_weight.shape[1]
    inner = ffn_in.shape[1]
    mixed = mix_weight.shape[1]
    shared_width = qk_gain.shape[1]
    places = jnp.stack([lax.axis_index("seq"), lax.axis_index("dp")]).astype(jnp.int32)
    meta = jnp.concatenate([places[:1], seq_lengths[0], places[1:]])
    gain1 = norm1_gain[None]
    gain2 = norm2_gain[None]
    omega = ema_omega[None]
    ema = (ema_delta.T, ema_alpha.T, ema_beta.T, ema_eta.T)
    full = (rows, width)
    wide = (rows, value_width)
    thin = (rows, shared_width)
    tiles = (width // 128, rows, 128)
    state = (hidden, width)
    states = (hidden, chunks, width)
    line = Line(PACES)

    share = jax.nn.sigmoid(ema_delta.T)
    logk = jnp.log1p(-share * jax.nn.sigmoid(ema_alpha.T))
    keep = jnp.exp(logk)
    mix = share * ema_beta.T * (ema_eta.T * (1.0 / math.sqrt(hidden)))
    gain_rows = jnp.where(share > -1.0, gain1, 0.0)
    strip = (width // 128, CHUNK, chunks, 128)
    normed, low_normed, enter, end, strips = line(
        start_body,
        (seq_lengths, tokens, gain_rows, logk, keep),
        [(tiles, F32), (full, BF16), (states, F32), (state, F32), (strip, F32)],
        name="norm_and_states",
    )
    other = swap(end, "seq", 1)
    chip_end = line(
        lambda *refs: pair_body(False, rows, *refs), (meta, end, other, logk), [(state, F32)], name="chip_state"
    )[0]
    arrived = [chip_before(chip_end, k) for k in range(1, lax.axis_size("seq") // 2)]
    routes = [route(halving, doubling) for halving, doubling in ROUTES]
    steps = sorted({step for halves, wholes in routes for step in halves})
    smooth = line(local_body, (strips, enter, keep, mix), [(strip, F32)], name="local_average")[0]
    values, values_slope = line(values_body, (low_normed, value_weight), [(wide, BF16), (wide, F32)], name="values")
    low_smoothed, slope_pre, entering = line(
        lambda *refs: carried_body(len(arrived), *refs),
        (meta, other, *arrived, logk, keep, mix, omega, strips, smooth, enter),
        [(full, BF16), (full, F32), (states, F32)],
        scratch=[(state, F32), ((rows, 128), F32)],
        name="carried_average",
    )
    update, candidate, reset, queries, keys, shared, shared_slope = line(
        mix_body,
        (low_smoothed, mix_weight, qk_gain, qk_bias),
        [(full, F32), (full, F32), (wide, F32), (thin, BF16), (thin, BF16), (thin, F32), (thin, F32)],
        name="mix",
    )
    weights, attended, gated = line(
        attend_body,
        (queries, keys, values, rel_bias[None], reset),
        [((rows, SPAN), F32), (wide, F32), (wide, BF16)],
        name="attention",
    )
    residual, change, slope_hidden, normal2, inverse2, low2 = line(
        hidden_body,
        (gated, out_weight, candidate, update, tokens, gain2),
        [(full, F32), (full, F32), (full, F32), (full, F32), ((rows, 128), F32), (full, BF16)],
        name="hidden",
    )
    expanded, slope_exp = line(
        expand_body, (low2, ffn_in), [((rows, inner), BF16), ((rows, inner), F32)], name="expand"
    )
    half = width // 2
    outputs = Outputs(
        line,
        meta,
        {
            "ffn_out": (inner, width),
            "ffn_in": (width, inner),
            "out": (value_width, width),
            "mix": (width, mixed),
            "value": (width, value_width),
        },
    )
    made = {}
    results = {}

    def more():
        while "packed" not in results:
            next(work)
        return results["packed"]

    def last(own, other):
        results["small"] = line(
            finish_body,
            (own, other, *ema),
            [(state, F32)] * 4 + [((1, width), F32)] * 3 + [((2, shared_width), F32)] * 2 + [((1, shared_width), F32)],
            name="parameters",
        )

    def small_piece():
        return Small(line, more(), last)

    def start_piece(number, parts, pairs, height, cols, plans, name):
        kept, *sent = line(
            lambda *refs: weights_body(parts, *refs),
            (meta, *[a for pair in pairs for a in pair]),
            [((height, cols), F32)] + [((height // SWAPS, cols), F32)] * SWAPS,
            name=name + "_grad",
        )
        placer = outputs.placer(plans, name)
        return Piece(line, made, steps, kept, sent, routes[number], placer, name)

    def ffn_out_piece():
        return start_piece(
            0,
            [(0, 0)], [(expanded, cotangent)], inner // 2, width, {"ffn_out": [(0, width, 0, 0)]}, "ffn_out"
        )

    def ffn_in_piece():
        return start_piece(
            1,
            [(0, 0), (inner, 0)],
            [(low2, made["expand_grad"]), (low_smoothed, made["update_grad"])],
            half,
            inner + width,
            {"ffn_in": [(0, inner, 0, 0)], "mix": [(inner, width, 0, 0)]},
            "ffn_in",
        )

    def out_piece():
        return start_piece(
            2,
            [(0, 0), (width, width), (2 * width, 0)],
            [(gated, made["out_grad"]), (gated, made["out_grad"]), (low_smoothed, made["out_grad"])],
            half,
            3 * width,
            {
                "out": [(0, width, 0, 0), (width, width, width, 0)],
                "mix": [(2 * width, width, 0, width + shared_width + value_width)],
            },
            "out",
        )

    def reset_piece():
        return start_piece(
            3,
            [(0, 0)],
            [(low_smoothed, made["reset_grad"])],
            half,
            value_width,
            {"mix": [(0, value_width, 0, width + shared_width)]},
            "reset",
        )

    def value_piece():
        return start_piece(
            4,
            [(0, 0), (value_width, 0)],
            [(low_normed, made["value_grad"]), (low_smoothed, made["shared_grad"])],
            half,
            value_width + shared_width,
            {"value": [(0, value_width, 0, 0)], "mix": [(value_width, shared_width, 0, width)]},
            "value",
        )

    makers = (ffn_out_piece, ffn_in_piece, out_piece, reset_piece, value_piece, small_piece)
    pieces = []

    def advance(i):
        if i < len(pieces) and pieces[i] is not None:
            pieces[i].advance()
        else:
            pieces.extend([None] * (i + 1 - len(pieces)))
            pieces[i] = makers[i]()

    def compute():
        yield
        made["masks"] = line(
            lambda *refs: masks_body(steps, *refs), (meta,), [((len(steps), 8, 128), F32)], name="masks"
        )[0]
        made["expand_grad"] = line(
            expand_back_body, (cotangent, ffn_out, slope_exp), [((rows, inner), BF16)], name="expand_back"
        )[0]
        yield
        input_part, update_grad, out_grad, gain2_grad = line(
            hidden_back_body,
            (made["expand_grad"], ffn_in, normal2, inverse2, gain2, cotangent, update, change, slope_hidden),
            [(full, F32), (full, BF16), (full, BF16), ((1, width), F32)],
            name="hidden_back",
        )
        made["update_grad"], made["out_grad"] = update_grad, out_grad
        yield
        reset_grad, attend_grad = line(
            reset_back_body, (out_grad, out_weight, reset, attended), [(wide, BF16)] * 2, name="reset_back"
        )
        made["reset_grad"] = reset_grad
        yield
        value_grad, shared_grad, small = line(
            attend_back_body,
            (attend_grad, weights, queries, keys, shared, shared_slope, values, values_slope, qk_gain),
            [(wide, BF16), (thin, BF16), ((8, shared_width), F32)],
            name="attention_back",
        )
        made["value_grad"], made["shared_grad"] = value_grad, shared_grad
        yield
        smooth_grad, norm_grad, omega_grad = line(
            smooth_back_body,
            (update_grad, shared_grad, reset_grad, out_grad, value_grad, mix_weight, value_weight, slope_pre)
            + (normed, omega),
            [(tiles, F32), (tiles, F32), ((1, width), F32)],
            name="smooth_back",
        )
        yield
        later, begin, grad_strips = line(
            rise_body,
            (meta, smooth_grad, logk, keep),
            [(states, F32), (state, F32), (strip, F32)],
            name="states_back",
        )
        other_begin = swap(begin, "seq", 1)
        yield
        window = line(
            lambda *refs: pair_body(True, rows, *refs),
            (meta, begin, other_begin, logk),
            [(state, F32)],
            name="chip_grad",
        )[0]
        returned = [chip_after(window, 1)]
        yield
        chips = 1
        while 4 * chips < lax.axis_size("seq"):
            window = line(
                lambda *refs, chips=chips: window_body(chips, rows, *refs),
                (meta, window, returned[-1], logk),
                [(state, F32)],
                name="window_grad",
            )[0]
            chips *= 2
            returned.append(chip_after(window, chips))
            yield
        later = line(
            lambda *refs: carry_back_body(len(returned), *refs),
            (meta, other_begin, *returned, logk, later),
            [(states, F32)],
            name="carry_back",
        )[0]
        yield
        backs = []
        for tile in range(width // 128):
            backs.append(
                line(
                    lambda *refs, tile=tile: state_back_body(tile, *refs),
                    (strips, grad_strips, entering, later, keep, mix),
                    [((rows, 128), F32), ((2 * hidden, 128), F32)],
                    scratch=[((CHUNK, hidden, chunks, 128), F32)],
                    name="state_back",
                )
            )
            yield
        results["input_grad"], results["packed"] = line(
            lambda *refs: close_body(len(backs), *refs),
            (*[b[0] for b in backs], *[b[1] for b in backs], tokens, gain1, norm_grad, input_part)
            + (omega_grad, gain2_grad, small),
            [(full, F32), ((SMALL_ROWS, value_width + shared_width), F32)],
            name="norm_back",
        )
        yield
        results["block_out"] = line(block_body, (residual, expanded, ffn_out), [(full, F32)], name="block_out")[0]

    work = compute()
    for item in "".join(ORDER):
        if item.isdigit():
            advance(int(item))
        else:
            next(work, None)
    for _ in work:
        pass
    for i in range(len(pieces), len(makers)):
        advance(i)
    while not all(p.done for p in pieces):
        for i in range(len(pieces)):
            advance(i)
    sums = outputs.arrays
    small = results["small"]
    return (
        results["block_out"],
        results["input_grad"],
        small[4][0],
        sums["value"],
        *[g.T for g in small[:4]],
        small[6][0],
        sums["mix"],
        small[7],
        small[8],
        small[9][0],
        sums["out"],
        small[5][0],
        sums["ffn_in"],
        sums["ffn_out"],
    )


def solution(mesh):
    rows = P(("dp", "seq"), None)
    in_specs = (rows, rows, P("dp", None)) + (P(),) * 15
    out_specs = (rows, rows) + (P(),) * 15
    return jax.shard_map(shards, mesh=mesh, in_specs=in_specs, out_specs=out_specs, check_vma=False)
```

```python
import math

import jax
import jax.numpy as jnp
from jax import lax
from jax.experimental import pallas as pl
from jax.experimental.pallas import tpu as pltpu
from jax.sharding import PartitionSpec as P

SPAN = 128
CHUNK = 64
EPS = 1e-05
BF16 = jnp.bfloat16
F32 = jnp.float32
ROOM = 2 * 1024 * 1024
SWAPS = 1
SMALL_ROWS = 24


def sigmoid(a):
    return 0.5 * jnp.tanh(0.5 * a) + 0.5


def mm(a, b):
    return lax.dot_general(a, b, (((1,), (0,)), ((), ())), preferred_element_type=F32)


def mm_nt(a, b):
    return lax.dot_general(a, b, (((1,), (1,)), ((), ())), preferred_element_type=F32)


def mm_tn(a, b):
    return lax.dot_general(a, b, (((0,), (0,)), ((), ())), preferred_element_type=F32)


class Place:
    def __init__(self, lengths):
        self.lengths = lengths
        self.shape = (lengths.shape[1] + 2,)

    def __getitem__(self, i):
        if i == 0:
            return lax.axis_index("seq")
        return self.lengths[0, i - 1]


class Line:
    def __init__(self, paces):
        self.token = None
        self.paces = paces
        self.count = 0

    def __call__(self, body, ins, outs, scratch=(), name=None, held=None, left=(), alias=None, out_left=0, dma=0):
        count = len(ins)
        before = () if self.token is None else (self.token,)
        alias = alias or {}
        specs = []
        for i, a in enumerate(ins):
            if i in left:
                specs.append(pl.BlockSpec(memory_space=pltpu.HBM))
            elif i in alias:
                specs.append(pl.BlockSpec(memory_space=pl.ANY))
            else:
                specs.append(pl.BlockSpec(memory_space=pltpu.SMEM if a.dtype == jnp.int32 else pltpu.VMEM))
        specs += [pl.BlockSpec(memory_space=pl.ANY)] * len(before)
        if held is None:
            held = sum(a.size * a.dtype.itemsize for a in ins if a.dtype != jnp.int32)
            held += sum(math.prod(s) * jnp.dtype(d).itemsize for s, d in tuple(outs) + tuple(scratch))
        first = count + len(before)

        def run(*refs):
            body(*refs[:count], *refs[first : first + len(outs)], *refs[first + len(outs) + 1 :])
            refs[first + len(outs)][...] = jnp.zeros((8, 128), F32)

        places = [pl.ANY if i < out_left else pltpu.VMEM for i in range(len(outs))]
        scratches = [pltpu.VMEM(s, d) for s, d in scratch]
        if dma:
            scratches.append(pltpu.SemaphoreType.DMA((dma,)))
        pace = self.paces[self.count] if self.count < len(self.paces) else 0
        self.count += 1
        result = pl.pallas_call(
            run,
            in_specs=specs,
            out_specs=[pl.BlockSpec(memory_space=m) for m in places + [pltpu.VMEM]],
            out_shape=[jax.ShapeDtypeStruct(s, d) for s, d in outs] + [jax.ShapeDtypeStruct((8, 128), F32)],
            scratch_shapes=scratches,
            input_output_aliases=alias,
            compiler_params=pltpu.CompilerParams(vmem_limit_bytes=int(held * 1.05) + ROOM),
            cost_estimate=pl.CostEstimate(flops=int(pace * 1e9), bytes_accessed=0, transcendentals=0),
            name=name,
        )(*ins, *before)
        self.token = result[-1]
        return result[:-1]


def clear_range(meta, low, high):
    count = meta.shape[0] - 2
    begin = jnp.int32(0)
    hit = jnp.bool_(False)
    for i in range(count):
        length = meta[1 + i]
        hit = hit | ((length > 0) & (begin >= low) & (begin < high))
        begin = begin + length
    return jnp.where(hit, 0.0, 1.0).astype(F32)


def chunk_masks(meta, first, chunks):
    rows = lax.broadcasted_iota(jnp.int32, (chunks, 128), 0)
    free = jnp.ones((chunks, 128), F32)
    for s in range(0, chunks, SPAN // CHUNK):
        position = first + s * CHUNK
        free = jnp.where(rows == s, clear_range(meta, position, position + 1), free)
    return free


def lanes_of(tile):
    return pl.ds(tile * 128, 128)


def tiled(ref):
    return jnp.concatenate([ref[i] for i in range(ref.shape[0])], axis=1)


def put_tiled(ref, value):
    for i in range(ref.shape[0]):
        ref[i] = value[:, i * 128 : (i + 1) * 128]


def scan_step(masks, values, decay_row, shifts, chunks):
    power = decay_row
    for i, mask in enumerate(masks):
        values = values + power * (mask * pltpu.roll(values, shifts[i], 0))
        power = power * power
    return values


def doubling_masks(mask, chunks, backward):
    masks = []
    distance = 1
    while distance < chunks:
        masks.append(mask)
        shift = chunks - distance if backward else distance
        mask = mask * pltpu.roll(mask, shift, 0)
        distance *= 2
    shifts = []
    distance = 1
    while distance < chunks:
        shifts.append(chunks - distance if backward else distance)
        distance *= 2
    return masks, shifts


def edge_masks(free, chunks, backward):
    rows = lax.broadcasted_iota(jnp.int32, (chunks, 128), 0)
    if backward:
        return jnp.where(rows == chunks - 1, 0.0, pltpu.roll(free, chunks - 1, 0))
    return jnp.where(rows == 0, 0.0, free)


def prefix_mask(free, chunks, backward):
    rows = lax.broadcasted_iota(jnp.int32, (chunks, 128), 0)
    if backward:
        reach = jnp.where(rows == chunks - 1, 1.0, pltpu.roll(free, chunks - 1, 0))
    else:
        reach = free
    distance = 1
    while distance < chunks:
        if backward:
            moved = jnp.where(rows >= chunks - distance, 1.0, pltpu.roll(reach, chunks - distance, 0))
        else:
            moved = jnp.where(rows < distance, 1.0, pltpu.roll(reach, distance, 0))
        reach = reach * moved
        distance *= 2
    return reach


def start_body(lengths, tok, gain, logk, keep, normed, low, enter, end, strips):
    meta = Place(lengths)
    tokens, width = tok.shape
    hidden = end.shape[0]
    chunks = tokens // CHUNK
    x = tok[...].astype(F32)
    centered = x - jnp.mean(x, axis=1, keepdims=True)
    spread = jnp.mean(centered * centered, axis=1, keepdims=True)
    rows = centered * lax.rsqrt(spread + EPS) * gain[0:1, :]
    put_tiled(normed, rows)
    low[...] = rows.astype(BF16)
    free = chunk_masks(meta, meta[0] * tokens, chunks)
    edge = edge_masks(free, chunks, False)
    masks, shifts = doubling_masks(edge, chunks, False)
    for tile in range(width // 128):
        lanes = lanes_of(tile)
        keeps = [keep[h : h + 1, lanes] for h in range(hidden)]

        def step(t, state):
            value = normed[tile, pl.ds(t, chunks, stride=CHUNK), :]
            strips[tile, t] = value
            return tuple(k * u + value for k, u in zip(keeps, state))

        zero = jnp.zeros((chunks, 128), F32)
        state = lax.fori_loop(0, CHUNK, step, (zero,) * hidden, unroll=16)
        for h in range(hidden):
            decay = jnp.exp(CHUNK * logk[h : h + 1, lanes])
            reached = scan_step(masks, state[h], decay, shifts, chunks)
            enter[h, :, lanes] = edge * pltpu.roll(reached, 1, 0)
            end[h : h + 1, lanes] = reached[chunks - 1 : chunks]


def values_body(low, weight, values, slope):
    for b in range(weight.shape[1] // 256):
        cols = pl.ds(b * 256, 256)
        raw = mm(low[...], weight[:, cols])
        gate = sigmoid(raw)
        out = raw * gate
        values[:, cols] = out.astype(BF16)
        slope[:, cols] = gate + out * (1.0 - gate)


def add_up(parts):
    while len(parts) > 1:
        parts = [a + b for a, b in zip(parts[::2], parts[1::2])]
    return parts[0]


def local_body(strips, enter, keep, mix, smooth):
    hidden = keep.shape[0]
    for tile in range(strips.shape[0]):
        lanes = lanes_of(tile)
        keeps = [keep[h : h + 1, lanes] for h in range(hidden)]
        mixes = [mix[h : h + 1, lanes] for h in range(hidden)]

        def step(t, state):
            value = strips[tile, t]
            state = tuple(k * u + value for k, u in zip(keeps, state))
            smooth[tile, t] = add_up([c * u for c, u in zip(mixes, state)])
            return state

        lax.fori_loop(0, CHUNK, step, tuple(enter[h, :, lanes] for h in range(hidden)), unroll=16)


def pair_body(backward, tokens, meta, own, other, logk, out):
    core = meta[0] % 2
    first = (meta[0] - core) * tokens
    middle = first + tokens
    decay = jnp.exp(tokens * logk[...])
    if backward:
        reach = clear_range(meta, first + 1, middle + 1)
        near = jnp.where(core == 0, own[...], other[...])
        far = jnp.where(core == 0, other[...], own[...])
    else:
        reach = clear_range(meta, middle, middle + tokens)
        near = jnp.where(core == 0, other[...], own[...])
        far = jnp.where(core == 0, own[...], other[...])
    out[...] = near + (reach * decay) * far


def window_body(count, tokens, meta, near, far, logk, out):
    span = 2 * tokens
    first = (meta[0] - meta[0] % 2) * tokens
    reach = clear_range(meta, first + 1, first + count * span + 1)
    out[...] = near[...] + (reach * jnp.exp((count * span) * logk[...])) * far[...]


def carry_of(backward, tokens, meta, other, arrived, logk):
    core = meta[0] % 2
    first = (meta[0] - core) * tokens
    span = 2 * tokens
    total = None
    for k, part in arrived:
        if backward:
            reach = clear_range(meta, first + span, first + (k + 1) * span + 1)
        else:
            reach = clear_range(meta, first - k * span, first)
        term = part[...] * reach
        if k:
            term = term * jnp.exp((k * span) * logk[...])
        total = term if total is None else total + term
    decay = jnp.exp(tokens * logk[...])
    middle = first + tokens
    if backward:
        crossing = clear_range(meta, middle, middle + 1)
        through = clear_range(meta, middle + 1, middle + tokens)
        passed = crossing * (other[...] + (through * decay) * total)
        return jnp.where(core == 0, passed, total)
    through = clear_range(meta, first, middle)
    return jnp.where(core == 0, total, other[...] + (through * decay) * total)


def reversed_lanes(row):
    size = row.shape[1]
    down = lax.broadcasted_iota(jnp.int32, (size, size), 0)
    across = lax.broadcasted_iota(jnp.int32, (size, size), 1)
    turn = jnp.where((down + across) % size == 0, 1.0, 0.0).astype(F32)
    return jnp.dot(row, turn, precision=lax.Precision.HIGHEST, preferred_element_type=F32)


def carried_body(chips, meta, other, *rest):
    arrived = rest[:chips]
    logk, keep, mix, omega, strips, smooth, enter, low, slope, states, carry, rows = rest[chips:]
    tiles, _, chunks, _ = strips.shape
    tokens = chunks * CHUNK
    hidden = keep.shape[0]
    carry[...] = carry_of(False, tokens, meta, other, list(enumerate(arrived)), logk)
    free = chunk_masks(meta, meta[0] * tokens, chunks)
    reach = prefix_mask(free, chunks, False)
    offset = (lax.broadcasted_iota(jnp.int32, (chunks, 128), 0) * CHUNK).astype(F32)
    for tile in range(tiles):
        lanes = lanes_of(tile)
        state = []
        for h in range(hidden):
            entry = jnp.exp(offset * logk[h : h + 1, lanes]) * reach
            first = carry[h : h + 1, lanes] * entry
            states[h, :, lanes] = enter[h, :, lanes] + first
            state.append(mix[h : h + 1, lanes] * first)
        keeps = [keep[h : h + 1, lanes] for h in range(hidden)]
        skip = omega[:, lanes]

        def step(t, state):
            state = tuple(k * u for k, u in zip(keeps, state))
            pre = smooth[tile, t] + skip * strips[tile, t] + add_up(list(state))
            rows[pl.ds(t, chunks, stride=CHUNK), :] = pre
            return state

        lax.fori_loop(0, CHUNK, step, tuple(state), unroll=16)
        pre = rows[...]
        gate = sigmoid(pre)
        smoothed = pre * gate
        low[:, lanes] = smoothed.astype(BF16)
        slope[:, lanes] = gate + smoothed * (1.0 - gate)


def layer_grad(weighted, normal, inverse):
    mean_one = jnp.mean(weighted, axis=1, keepdims=True)
    mean_two = jnp.mean(weighted * normal, axis=1, keepdims=True)
    return (weighted - mean_one - normal * mean_two) * inverse


def shift_rows(table, down):
    size = table.shape[0]
    rows = lax.broadcasted_iota(jnp.int32, table.shape, 0)
    bit = 1
    while bit < size:
        moved = pltpu.roll(table, bit if down else size - bit, 1)
        table = jnp.where((rows & bit) != 0, moved, table)
        bit *= 2
    return table


def mix_body(low, mix_weight, qk_gain, qk_bias, update, candidate, reset, queries, keys, shared, shared_slope):
    width = update.shape[1]
    base = width + shared.shape[1]
    top = base + reset.shape[1]
    raw = mm(low[...], mix_weight[:, width:base])
    gate = sigmoid(raw)
    silu = raw * gate
    shared[...] = silu
    shared_slope[...] = gate + silu * (1.0 - gate)
    queries[...] = (silu * qk_gain[0:1] + qk_bias[0:1]).astype(BF16)
    keys[...] = (silu * qk_gain[1:2] + qk_bias[1:2]).astype(BF16)
    for b in range(width // 256):
        update[:, b * 256 : (b + 1) * 256] = sigmoid(mm(low[...], mix_weight[:, b * 256 : (b + 1) * 256]))
    for b in range(reset.shape[1] // 256):
        reset[:, b * 256 : (b + 1) * 256] = mm(low[...], mix_weight[:, base + b * 256 : base + (b + 1) * 256])
    for b in range(width // 256):
        candidate[:, b * 256 : (b + 1) * 256] = mm(low[...], mix_weight[:, top + b * 256 : top + (b + 1) * 256])


def attend_body(queries, keys, values, rel_bias, reset, weights, attended, gated):
    tokens, shared_width = queries.shape
    place = lax.broadcasted_iota(jnp.int32, (SPAN, SPAN), 0)
    causal = place >= lax.broadcasted_iota(jnp.int32, (SPAN, SPAN), 1)
    turned = jnp.broadcast_to(reversed_lanes(jnp.broadcast_to(rel_bias[...], (8, SPAN)))[0:1], (SPAN, SPAN))
    bias = shift_rows(turned, True)
    scale = 1.0 / math.sqrt(shared_width)
    for s in range(tokens // SPAN):
        rows = pl.ds(s * SPAN, SPAN)
        scores = mm_nt(queries[rows, :], keys[rows, :]) * scale + bias
        scores = jnp.where(causal, scores, -1e30)
        powers = jnp.exp(scores - jnp.max(scores, axis=1, keepdims=True))
        share = powers / jnp.sum(powers, axis=1, keepdims=True)
        weights[rows, :] = share
        rise = mm(share.astype(BF16), values[rows, :])
        attended[rows, :] = rise
        raw = reset[rows, :]
        gated[rows, :] = (raw * sigmoid(raw) * rise).astype(BF16)


def hidden_body(
    gated, out_weight, candidate, update, tok, gain2, residual, change, slope_hidden, normal2, inverse2, low2
):
    total = candidate[...] + mm(gated[...], out_weight[...])
    gate = sigmoid(total)
    hidden_rows = total * gate
    slope_hidden[...] = gate + hidden_rows * (1.0 - gate)
    x = tok[...].astype(F32)
    moved = hidden_rows - x
    change[...] = moved
    rows = x + update[...] * moved
    residual[...] = rows
    centered = rows - jnp.mean(rows, axis=1, keepdims=True)
    inverse = lax.rsqrt(jnp.mean(centered * centered, axis=1, keepdims=True) + EPS)
    normal = centered * inverse
    normal2[...] = normal
    inverse2[...] = jnp.broadcast_to(inverse, inverse2.shape)
    low2[...] = (normal * gain2[...]).astype(BF16)


def expand_body(low2, ffn_in, expanded, slope_exp):
    for b in range(ffn_in.shape[1] // 256):
        cols = pl.ds(b * 256, 256)
        raw = mm(low2[...], ffn_in[:, cols])
        gate = sigmoid(raw)
        silu = raw * gate
        expanded[:, cols] = silu.astype(BF16)
        slope_exp[:, cols] = gate + silu * (1.0 - gate)


def weights_body(parts, meta, *refs):
    kept, sent = refs[-SWAPS - 1], refs[-SWAPS:]
    pairs = refs[: -SWAPS - 1]
    half = kept.shape[0]
    core = meta[0] % 2
    for mine, side in ((False, 1 - core), (True, core)):
        for i, (column, block) in enumerate(parts):
            left, right = pairs[2 * i], pairs[2 * i + 1]
            begin = pl.multiple_of(side * half + block, 128)
            cols = slice(column, column + right.shape[1])
            value = mm_tn(left[:, pl.ds(begin, half)], right[...])
            if mine:
                kept[:, cols] = value
            else:
                for j, target in enumerate(sent):
                    target[:, cols] = value[j * half // SWAPS : (j + 1) * half // SWAPS]


def block_body(residual, expanded, ffn_out, out):
    out[...] = residual[...] + mm(expanded[...], ffn_out[...])


def expand_back_body(cot, ffn_out, slope_exp, expand_grad):
    for b in range(ffn_out.shape[0] // 256):
        cols = pl.ds(b * 256, 256)
        expand_grad[:, cols] = (mm_nt(cot[...], ffn_out[cols, :]) * slope_exp[:, cols]).astype(BF16)


def hidden_back_body(
    expand_grad,
    ffn_in,
    normal2,
    inverse2,
    gain2,
    cot,
    update,
    change,
    slope_hidden,
    input_part,
    update_grad,
    out_grad,
    gain2_grad,
):
    norm_out = mm_nt(expand_grad[...], ffn_in[...])
    normal = normal2[...]
    gain2_grad[...] = jnp.sum(norm_out * normal, axis=0, keepdims=True)
    upstream = cot[...].astype(F32) + layer_grad(norm_out * gain2[...], normal, inverse2[:, 0:1])
    gates = update[...]
    input_part[...] = upstream * (1.0 - gates)
    update_grad[...] = (upstream * change[...] * gates * (1.0 - gates)).astype(BF16)
    out_grad[...] = (upstream * gates * slope_hidden[...]).astype(BF16)


def reset_back_body(out_grad, out_weight, reset, attended, reset_grad, attend_grad):
    for b in range(reset.shape[1] // 256):
        cols = pl.ds(b * 256, 256)
        rise = mm_nt(out_grad[...], out_weight[cols, :])
        raw = reset[:, cols]
        gate = sigmoid(raw)
        silu = raw * gate
        reset_grad[:, cols] = (rise * attended[:, cols] * (gate + silu * (1.0 - gate))).astype(BF16)
        attend_grad[:, cols] = (rise * silu).astype(BF16)


def attend_back_body(
    attend_grad,
    weights,
    queries,
    keys,
    shared,
    shared_slope,
    values,
    values_slope,
    qk_gain,
    value_grad,
    shared_grad,
    small,
):
    tokens, shared_width = queries.shape
    scale = 1.0 / math.sqrt(shared_width)
    slopes = jnp.zeros((SPAN, SPAN), F32)
    for s in range(tokens // SPAN):
        rows = pl.ds(s * SPAN, SPAN)
        upstream = attend_grad[rows, :]
        share = weights[rows, :]
        rise = mm_nt(upstream, values[rows, :])
        value_rise = mm_tn(share.astype(BF16), upstream)
        value_grad[rows, :] = (value_rise * values_slope[rows, :]).astype(BF16)
        score_grad = share * (rise - jnp.sum(share * rise, axis=1, keepdims=True))
        slopes = slopes + score_grad
        low = (score_grad * scale).astype(BF16)
        query_grad = mm(low, keys[rows, :])
        key_grad = mm_tn(low, queries[rows, :])
        silu = shared[rows, :]
        pieces = (
            jnp.sum(query_grad * silu, axis=0, keepdims=True),
            jnp.sum(key_grad * silu, axis=0, keepdims=True),
            jnp.sum(query_grad, axis=0, keepdims=True),
            jnp.sum(key_grad, axis=0, keepdims=True),
        )
        sums = pieces if s == 0 else tuple(a + b for a, b in zip(sums, pieces))
        back = query_grad * qk_gain[0:1] + key_grad * qk_gain[1:2]
        shared_grad[rows, :] = (back * shared_slope[rows, :]).astype(BF16)
    small[...] = jnp.zeros_like(small)
    for i in range(4):
        small[i : i + 1, :] = sums[i]
    turned = jnp.sum(shift_rows(slopes, False), axis=0, keepdims=True)
    small[4:5, :] = reversed_lanes(jnp.broadcast_to(turned, (8, SPAN)))[0:1]


def smooth_back_body(
    update_grad,
    shared_grad,
    reset_grad,
    out_grad,
    value_grad,
    mix_weight,
    value_weight,
    slope_pre,
    normed,
    omega,
    smooth_grad,
    norm_grad,
    omega_grad,
):
    width = update_grad.shape[1]
    base = width + shared_grad.shape[1]
    top = base + reset_grad.shape[1]
    rise = mm_nt(reset_grad[...], mix_weight[:, base:top])
    rise = rise + mm_nt(update_grad[...], mix_weight[:, :width])
    rise = rise + mm_nt(out_grad[...], mix_weight[:, top:])
    rise = rise + mm_nt(shared_grad[...], mix_weight[:, width:base])
    grad = rise * slope_pre[...]
    put_tiled(smooth_grad, grad)
    put_tiled(norm_grad, mm_nt(value_grad[...], value_weight[...]) + omega[...] * grad)
    omega_grad[...] = jnp.sum(grad * tiled(normed), axis=0, keepdims=True)


def rise_body(meta, smooth_grad, logk, keep, enter, end, strips):
    tiles, tokens, _ = smooth_grad.shape
    hidden = keep.shape[0]
    chunks = tokens // CHUNK
    free = chunk_masks(meta, meta[0] * tokens, chunks)
    edge = edge_masks(free, chunks, True)
    masks, shifts = doubling_masks(edge, chunks, True)
    for tile in range(tiles):
        lanes = lanes_of(tile)
        keeps = [keep[h : h + 1, lanes] for h in range(hidden)]

        def step(t, state):
            value = smooth_grad[tile, pl.ds(CHUNK - 1 - t, chunks, stride=CHUNK), :]
            strips[tile, CHUNK - 1 - t] = value
            return tuple(k * u + value for k, u in zip(keeps, state))

        zero = jnp.zeros((chunks, 128), F32)
        state = lax.fori_loop(0, CHUNK, step, (zero,) * hidden, unroll=16)
        for h in range(hidden):
            decay = jnp.exp(CHUNK * logk[h : h + 1, lanes])
            reached = scan_step(masks, state[h], decay, shifts, chunks)
            enter[h, :, lanes] = edge * pltpu.roll(reached, chunks - 1, 0)
            end[h : h + 1, lanes] = reached[0:1]


def carry_back_body(chips, meta, other, *rest):
    arrived = rest[:chips]
    logk, enter, later = rest[chips:]
    hidden, chunks, width = enter.shape
    tokens = chunks * CHUNK
    carry = carry_of(True, tokens, meta, other, [(2**j - 1, part) for j, part in enumerate(arrived)], logk)
    free = chunk_masks(meta, meta[0] * tokens, chunks)
    reach = prefix_mask(free, chunks, True)
    offset = ((chunks - 1 - lax.broadcasted_iota(jnp.int32, (chunks, 128), 0)) * CHUNK).astype(F32)
    for tile in range(width // 128):
        lanes = lanes_of(tile)
        for h in range(hidden):
            entry = jnp.exp(offset * logk[h : h + 1, lanes]) * reach
            later[h, :, lanes] = enter[h, :, lanes] + carry[h : h + 1, tile * 128 : (tile + 1) * 128] * entry


def state_back_body(tile, strips, grads, states, later, keep, mix, part, sums, history):
    hidden = keep.shape[0]
    chunks = states.shape[1]
    lanes = lanes_of(tile)
    heads = range(hidden)
    keeps = [keep[h : h + 1, lanes] for h in heads]
    mixes = [mix[h : h + 1, lanes] for h in heads]
    zeros = (jnp.zeros((chunks, 128), F32),) * hidden

    def rise(t, held):
        state, reads = held
        value = strips[tile, t]
        grad = grads[tile, t]
        state = tuple(k * u + value for k, u in zip(keeps, state))
        reads = tuple(r + u * grad for r, u in zip(reads, state))
        for i in heads:
            history[t, i] = state[i]
        return state, reads

    first = tuple(states[h, :, lanes] for h in heads)
    _, reads = lax.fori_loop(0, CHUNK, rise, (first, zeros), unroll=8)
    for h in heads:
        sums[h : h + 1, :] = jnp.sum(reads[h], axis=0, keepdims=True)

    def fall(i, held):
        state, marks = held
        t = CHUNK - 1 - i
        grad = grads[tile, t]
        state = tuple(k * w + grad for k, w in zip(keeps, state))
        marks = tuple(m + w * history[t, j] for j, (m, w) in enumerate(zip(marks, state)))
        part[pl.ds(t, chunks, stride=CHUNK), :] = add_up([c * w for c, w in zip(mixes, state)])
        return state, marks

    first = tuple(later[h, :, lanes] for h in heads)
    _, marks = lax.fori_loop(0, CHUNK, fall, (first, zeros), unroll=8)
    for h in heads:
        sums[hidden + h : hidden + h + 1, :] = jnp.sum(marks[h], axis=0, keepdims=True)


def close_body(count, *refs):
    totals = refs[:count]
    sums = refs[count : 2 * count]
    tok, gain, norm_grad, input_part, omega_grad, gain2_grad, small, input_grad, packed = refs[2 * count :]
    x = tok[...].astype(F32)
    width = x.shape[1]
    centered = x - jnp.mean(x, axis=1, keepdims=True)
    inverse = lax.rsqrt(jnp.mean(centered * centered, axis=1, keepdims=True) + EPS)
    normal = centered * inverse
    upstream = tiled(norm_grad) + jnp.concatenate([t[...] for t in totals], axis=1)
    input_grad[...] = input_part[...] + layer_grad(upstream * gain[...], normal, inverse)
    at = sums[0].shape[0] // 2
    packed[...] = jnp.zeros_like(packed)
    for i in range(count):
        packed[0:at, i * 128 : (i + 1) * 128] = sums[i][0:at, :]
        packed[0:at, width + i * 128 : width + (i + 1) * 128] = sums[i][at : 2 * at, :]
    packed[at : at + 1, :width] = jnp.sum(upstream * normal, axis=0, keepdims=True)
    packed[at : at + 1, width : 2 * width] = gain2_grad[...]
    packed[at + 1 : at + 2, :width] = omega_grad[...]
    packed[0:8, 2 * width : 2 * width + small.shape[1]] = small[...]


def finish_body(own, other, delta, alpha, beta, eta, *outs):
    delta_grad, alpha_grad, beta_grad, eta_grad, gain1_grad, gain2_grad, omega_grad, qk_gain_grad, qk_bias_grad, rel_grad = outs
    hidden, width = delta_grad.shape
    scale = 1.0 / math.sqrt(hidden)
    packed = own[...] + other[...]
    read = packed[0:hidden, :width]
    mark = packed[0:hidden, width : 2 * width]
    share = jax.nn.sigmoid(delta[...])
    damp = jax.nn.sigmoid(alpha[...])
    inflow = share * beta[...]
    outflow = eta[...] * scale
    eta_grad[...] = inflow * read * scale
    inflow_grad = outflow * read
    beta_grad[...] = share * inflow_grad
    rate = inflow * outflow * (mark - read) / (share * damp - 1.0)
    share_grad = beta[...] * inflow_grad + damp * rate
    delta_grad[...] = share_grad * share * (1.0 - share)
    alpha_grad[...] = share * rate * damp * (1.0 - damp)
    gain1_grad[...] = packed[hidden : hidden + 1, :width]
    gain2_grad[...] = packed[hidden : hidden + 1, width : 2 * width]
    omega_grad[...] = packed[hidden + 1 : hidden + 2, :width]
    tail = slice(2 * width, 2 * width + rel_grad.shape[1])
    qk_gain_grad[...] = packed[0:2, tail]
    qk_bias_grad[...] = packed[2:4, tail]
    rel_grad[...] = packed[4:5, tail]


def swap(a, axis, bit):
    count = lax.axis_size(axis)
    return lax.ppermute(a, axis, [(i, i ^ bit) for i in range(count)])


def chip_before(state, chips):
    count = lax.axis_size("seq")
    return lax.ppermute(state, "seq", [(i, i + 2 * chips) for i in range(count - 2 * chips)])


def chip_after(state, chips):
    count = lax.axis_size("seq")
    return lax.ppermute(state, "seq", [(i, i - 2 * chips) for i in range(2 * chips, count)])


def axis_bits(axis, least):
    bits = []
    bit = least
    while bit < lax.axis_size(axis):
        bits.append((axis, bit))
        bit *= 2
    return bits


def cross(a, step):
    seq = lax.axis_size("seq")
    moves = []
    for i in range(lax.axis_size("dp") * seq):
        axis, bit = step[i % 2]
        moves.append((i, i ^ (bit * seq if axis == "dp" else bit)))
    return lax.ppermute(a, ("dp", "seq"), moves)


ROUTES = (
    (("xy", "yx"), "12"),
    (("xy1", "yx1"), "2"),
    (("xy1", "yx1"), "2"),
    (("xy1", "yx1"), "2"),
    (("1xy", "1yx"), "2"),
)
ORDER = (
    "CCKC1C410C40KK1K2104231K",
    "KK0431201K32143K2K103405",
    "214302435250S35425304235",
    "3",
)
PACES = (
    8, 8, 8, 8, 8, 8, 8, 8, 8, 8, 8, 8, 0, 0, 0, 0, 8, 8, 12, 12, 12, 12, 8, 3, 12, 12, 12, 8, 12,
    12, 10, 10, 10, 10, 2, 1, 1, 1, 1, 10, 10, 8, 8, 8, 8, 1.5, 0.6, 3, 8, 8, 8, 8, 8, 8, 12, 8, 4,
    2, 8, 8, 8, 0.3, 0.3, 12, 12, 12, 8, 8, 0, 3, 8, 8, 8, 12, 12, 6, 10, 8, 12, 0, 8, 8, 8, 12, 8,
    0, 0, 0, 0, 8,
)
BITS = {"x": ("dp", 1), "y": ("dp", 2), "1": ("seq", 2), "2": ("seq", 4)}


def route(halving, doubling):
    named = lambda pair: all(BITS[c][1] < lax.axis_size(BITS[c][0]) for c in pair)
    halves = [tuple(BITS[c] for c in pair) for pair in zip(*halving) if named(pair)]
    wholes = [(BITS[c], BITS[c]) for c in doubling if named(c)]
    for bit in axis_bits("dp", 1) + axis_bits("seq", 2):
        if bit not in BITS.values():
            halves.append((bit, bit))
    return halves, wholes


def masks_body(steps, meta, out):
    for i, step in enumerate(steps):
        place = [(meta[0] if axis == "seq" else meta[meta.shape[0] - 1]) // bit % 2 for axis, bit in step]
        side = jnp.where(meta[0] % 2 == 0, place[0], place[1])
        out[i] = jnp.full((8, 128), side.astype(F32))


def split_body(index, masks, kept, *refs):
    arrived, (keep, send) = refs[:-2], refs[-2:]
    half = keep.shape[0]
    upper = masks[index, 0:1, 0:1] > 0.5
    came = jnp.concatenate([a[...] for a in arrived], axis=0) if len(arrived) > 1 else arrived[0][...]
    total = kept[...] + came
    low, high = total[:half], total[half:]
    keep[...] = jnp.where(upper, high, low)
    send[...] = jnp.where(upper, low, high)


def sum_body(kept, arrived, out):
    out[...] = kept[...] + arrived[...]


def join_body(index, masks, own, other, out):
    half = own.shape[0]
    upper = masks[index, 0:1, 0:1] > 0.5
    out[:half, :] = jnp.where(upper, other[...], own[...])
    out[half:, :] = jnp.where(upper, own[...], other[...])


class Piece:
    def __init__(self, line, made, steps, kept, sent, routes, outputs, name):
        self.line, self.made, self.steps, self.name = line, made, steps, name
        self.outputs = outputs
        self.work = self.run(kept, sent, *routes)
        self.done = False
        self.advance()

    def advance(self):
        if not self.done:
            self.done = next(self.work, "end") == "end"

    def run(self, kept, sent, halves, wholes):
        line = self.line
        arrived = [swap(a, "seq", 1) for a in sent]
        yield
        masks = self.made["masks"]
        for step in halves:
            rows, cols = kept.shape
            kept, send = line(
                lambda *refs, index=self.steps.index(step): split_body(index, *refs),
                (masks, kept, *arrived),
                [((rows // 2, cols), F32)] * 2,
                name=self.name + "_split",
            )
            arrived = [cross(send, step)]
            yield
        for step in list(wholes) + [None]:
            kept = line(sum_body, (kept, arrived[0]), [(kept.shape, F32)], name=self.name + "_sum")[0]
            if step is not None:
                arrived = [cross(kept, step)]
                yield
        part = kept
        for step in reversed(halves):
            other = cross(part, step)
            yield
            rows, cols = part.shape
            part = line(
                lambda *refs, index=self.steps.index(step): join_body(index, *refs),
                (masks, part, other),
                [((2 * rows, cols), F32)],
                name=self.name + "_join",
            )[0]
        other = swap(part, "seq", 1)
        yield
        self.outputs(part, other, part.shape[0])


class Small:
    def __init__(self, line, part, last):
        self.work = self.run(line, part, last)
        self.done = False
        self.advance()

    def advance(self):
        if not self.done:
            self.done = next(self.work, "end") == "end"

    def run(self, line, part, last):
        flat = axis_bits("dp", 1)
        steps = list(zip(flat, flat[::-1])) + [(bit, bit) for bit in axis_bits("seq", 2)]
        other = swap(part, "seq", 1)
        yield
        for step in steps:
            part = line(sum_body, (part, other), [(part.shape, F32)], name="small_sum")[0]
            other = cross(part, step)
            yield
        last(part, other)


def place_body(plans, rows, count, meta, own, other, *refs):
    outs = refs[count : count + len(plans)]
    sems = refs[-1]
    core = meta[0] % 2
    copies = []
    for part, side in ((own, core), (other, 1 - core)):
        for out, plan in zip(outs, plans):
            for column, width, row, place in plan:
                begin = pl.multiple_of(side * rows + row, 8)
                copies.append(
                    pltpu.make_async_copy(
                        part.at[pl.ds(0, rows), pl.ds(column, width)],
                        out.at[pl.ds(begin, rows), pl.ds(place, width)],
                        sems.at[len(copies)],
                    )
                )
                copies[-1].start()
    for copy in copies:
        copy.wait()


class Outputs:
    def __init__(self, line, meta, shapes):
        self.line, self.meta, self.shapes, self.arrays = line, meta, shapes, {}

    def placer(self, plans, name):
        def place(own, other, rows):
            names = list(plans)
            held = [n for n in names if n in self.arrays]
            results = self.line(
                lambda *refs: place_body(list(plans.values()), rows, len(held), *refs),
                (self.meta, own, other, *[self.arrays[n] for n in held]),
                [(self.shapes[n], F32) for n in names],
                name=name + "_out",
                held=own.size * 8,
                alias={3 + i: names.index(n) for i, n in enumerate(held)},
                out_left=len(names),
                dma=2 * sum(len(p) for p in plans.values()),
            )
            self.arrays.update(zip(names, results))

        return place


def shards(
    tokens,
    cotangent,
    seq_lengths,
    norm1_gain,
    value_weight,
    ema_delta,
    ema_alpha,
    ema_beta,
    ema_eta,
    ema_omega,
    mix_weight,
    qk_gain,
    qk_bias,
    rel_bias,
    out_weight,
    norm2_gain,
    ffn_in,
    ffn_out,
):
    rows, width = tokens.shape
    hidden = ema_delta.shape[1]
    chunks = rows // CHUNK
    value_width = value_weight.shape[1]
    inner = ffn_in.shape[1]
    mixed = mix_weight.shape[1]
    shared_width = qk_gain.shape[1]
    places = jnp.stack([lax.axis_index("seq"), lax.axis_index("dp")]).astype(jnp.int32)
    meta = jnp.concatenate([places[:1], seq_lengths[0], places[1:]])
    gain1 = norm1_gain[None]
    gain2 = norm2_gain[None]
    omega = ema_omega[None]
    ema = (ema_delta.T, ema_alpha.T, ema_beta.T, ema_eta.T)
    full = (rows, width)
    wide = (rows, value_width)
    thin = (rows, shared_width)
    tiles = (width // 128, rows, 128)
    state = (hidden, width)
    states = (hidden, chunks, width)
    line = Line(PACES)

    share = jax.nn.sigmoid(ema_delta.T)
    logk = jnp.log1p(-share * jax.nn.sigmoid(ema_alpha.T))
    keep = jnp.exp(logk)
    mix = share * ema_beta.T * (ema_eta.T * (1.0 / math.sqrt(hidden)))
    gain_rows = jnp.where(share > -1.0, gain1, 0.0)
    strip = (width // 128, CHUNK, chunks, 128)
    normed, low_normed, enter, end, strips = line(
        start_body,
        (seq_lengths, tokens, gain_rows, logk, keep),
        [(tiles, F32), (full, BF16), (states, F32), (state, F32), (strip, F32)],
        name="norm_and_states",
    )
    other = swap(end, "seq", 1)
    chip_end = line(
        lambda *refs: pair_body(False, rows, *refs), (meta, end, other, logk), [(state, F32)], name="chip_state"
    )[0]
    arrived = [chip_before(chip_end, k) for k in range(1, lax.axis_size("seq") // 2)]
    routes = [route(halving, doubling) for halving, doubling in ROUTES]
    steps = sorted({step for halves, wholes in routes for step in halves})
    smooth = line(local_body, (strips, enter, keep, mix), [(strip, F32)], name="local_average")[0]
    values, values_slope = line(values_body, (low_normed, value_weight), [(wide, BF16), (wide, F32)], name="values")
    low_smoothed, slope_pre, entering = line(
        lambda *refs: carried_body(len(arrived), *refs),
        (meta, other, *arrived, logk, keep, mix, omega, strips, smooth, enter),
        [(full, BF16), (full, F32), (states, F32)],
        scratch=[(state, F32), ((rows, 128), F32)],
        name="carried_average",
    )
    update, candidate, reset, queries, keys, shared, shared_slope = line(
        mix_body,
        (low_smoothed, mix_weight, qk_gain, qk_bias),
        [(full, F32), (full, F32), (wide, F32), (thin, BF16), (thin, BF16), (thin, F32), (thin, F32)],
        name="mix",
    )
    weights, attended, gated = line(
        attend_body,
        (queries, keys, values, rel_bias[None], reset),
        [((rows, SPAN), F32), (wide, F32), (wide, BF16)],
        name="attention",
    )
    residual, change, slope_hidden, normal2, inverse2, low2 = line(
        hidden_body,
        (gated, out_weight, candidate, update, tokens, gain2),
        [(full, F32), (full, F32), (full, F32), (full, F32), ((rows, 128), F32), (full, BF16)],
        name="hidden",
    )
    expanded, slope_exp = line(
        expand_body, (low2, ffn_in), [((rows, inner), BF16), ((rows, inner), F32)], name="expand"
    )
    half = width // 2
    outputs = Outputs(
        line,
        meta,
        {
            "ffn_out": (inner, width),
            "ffn_in": (width, inner),
            "out": (value_width, width),
            "mix": (width, mixed),
            "value": (width, value_width),
        },
    )
    made = {}
    results = {}

    def more():
        while "packed" not in results:
            next(work)
        return results["packed"]

    def last(own, other):
        results["small"] = line(
            finish_body,
            (own, other, *ema),
            [(state, F32)] * 4 + [((1, width), F32)] * 3 + [((2, shared_width), F32)] * 2 + [((1, shared_width), F32)],
            name="parameters",
        )

    def small_piece():
        return Small(line, more(), last)

    def start_piece(number, parts, pairs, height, cols, plans, name):
        kept, *sent = line(
            lambda *refs: weights_body(parts, *refs),
            (meta, *[a for pair in pairs for a in pair]),
            [((height, cols), F32)] + [((height // SWAPS, cols), F32)] * SWAPS,
            name=name + "_grad",
        )
        placer = outputs.placer(plans, name)
        return Piece(line, made, steps, kept, sent, routes[number], placer, name)

    def ffn_out_piece():
        return start_piece(
            0,
            [(0, 0)], [(expanded, cotangent)], inner // 2, width, {"ffn_out": [(0, width, 0, 0)]}, "ffn_out"
        )

    def ffn_in_piece():
        return start_piece(
            1,
            [(0, 0), (inner, 0)],
            [(low2, made["expand_grad"]), (low_smoothed, made["update_grad"])],
            half,
            inner + width,
            {"ffn_in": [(0, inner, 0, 0)], "mix": [(inner, width, 0, 0)]},
            "ffn_in",
        )

    def out_piece():
        return start_piece(
            2,
            [(0, 0), (width, width), (2 * width, 0)],
            [(gated, made["out_grad"]), (gated, made["out_grad"]), (low_smoothed, made["out_grad"])],
            half,
            3 * width,
            {
                "out": [(0, width, 0, 0), (width, width, width, 0)],
                "mix": [(2 * width, width, 0, width + shared_width + value_width)],
            },
            "out",
        )

    def reset_piece():
        return start_piece(
            3,
            [(0, 0)],
            [(low_smoothed, made["reset_grad"])],
            half,
            value_width,
            {"mix": [(0, value_width, 0, width + shared_width)]},
            "reset",
        )

    def value_piece():
        return start_piece(
            4,
            [(0, 0), (value_width, 0)],
            [(low_normed, made["value_grad"]), (low_smoothed, made["shared_grad"])],
            half,
            value_width + shared_width,
            {"value": [(0, value_width, 0, 0)], "mix": [(value_width, shared_width, 0, width)]},
            "value",
        )

    makers = (ffn_out_piece, ffn_in_piece, out_piece, reset_piece, value_piece, small_piece)
    pieces = []

    def advance(i):
        if i < len(pieces) and pieces[i] is not None:
            pieces[i].advance()
        else:
            pieces.extend([None] * (i + 1 - len(pieces)))
            pieces[i] = makers[i]()

    def compute():
        yield
        made["masks"] = line(
            lambda *refs: masks_body(steps, *refs), (meta,), [((len(steps), 8, 128), F32)], name="masks"
        )[0]
        made["expand_grad"] = line(
            expand_back_body, (cotangent, ffn_out, slope_exp), [((rows, inner), BF16)], name="expand_back"
        )[0]
        yield
        input_part, update_grad, out_grad, gain2_grad = line(
            hidden_back_body,
            (made["expand_grad"], ffn_in, normal2, inverse2, gain2, cotangent, update, change, slope_hidden),
            [(full, F32), (full, BF16), (full, BF16), ((1, width), F32)],
            name="hidden_back",
        )
        made["update_grad"], made["out_grad"] = update_grad, out_grad
        yield
        reset_grad, attend_grad = line(
            reset_back_body, (out_grad, out_weight, reset, attended), [(wide, BF16)] * 2, name="reset_back"
        )
        made["reset_grad"] = reset_grad
        yield
        value_grad, shared_grad, small = line(
            attend_back_body,
            (attend_grad, weights, queries, keys, shared, shared_slope, values, values_slope, qk_gain),
            [(wide, BF16), (thin, BF16), ((8, shared_width), F32)],
            name="attention_back",
        )
        made["value_grad"], made["shared_grad"] = value_grad, shared_grad
        yield
        smooth_grad, norm_grad, omega_grad = line(
            smooth_back_body,
            (update_grad, shared_grad, reset_grad, out_grad, value_grad, mix_weight, value_weight, slope_pre)
            + (normed, omega),
            [(tiles, F32), (tiles, F32), ((1, width), F32)],
            name="smooth_back",
        )
        yield
        later, begin, grad_strips = line(
            rise_body,
            (meta, smooth_grad, logk, keep),
            [(states, F32), (state, F32), (strip, F32)],
            name="states_back",
        )
        other_begin = swap(begin, "seq", 1)
        yield
        window = line(
            lambda *refs: pair_body(True, rows, *refs),
            (meta, begin, other_begin, logk),
            [(state, F32)],
            name="chip_grad",
        )[0]
        returned = [chip_after(window, 1)]
        yield
        chips = 1
        while 4 * chips < lax.axis_size("seq"):
            window = line(
                lambda *refs, chips=chips: window_body(chips, rows, *refs),
                (meta, window, returned[-1], logk),
                [(state, F32)],
                name="window_grad",
            )[0]
            chips *= 2
            returned.append(chip_after(window, chips))
            yield
        later = line(
            lambda *refs: carry_back_body(len(returned), *refs),
            (meta, other_begin, *returned, logk, later),
            [(states, F32)],
            name="carry_back",
        )[0]
        yield
        backs = []
        for tile in range(width // 128):
            backs.append(
                line(
                    lambda *refs, tile=tile: state_back_body(tile, *refs),
                    (strips, grad_strips, entering, later, keep, mix),
                    [((rows, 128), F32), ((2 * hidden, 128), F32)],
                    scratch=[((CHUNK, hidden, chunks, 128), F32)],
                    name="state_back",
                )
            )
            yield
        results["input_grad"], results["packed"] = line(
            lambda *refs: close_body(len(backs), *refs),
            (*[b[0] for b in backs], *[b[1] for b in backs], tokens, gain1, norm_grad, input_part)
            + (omega_grad, gain2_grad, small),
            [(full, F32), ((SMALL_ROWS, value_width + shared_width), F32)],
            name="norm_back",
        )
        yield
        results["block_out"] = line(block_body, (residual, expanded, ffn_out), [(full, F32)], name="block_out")[0]

    work = compute()
    for item in "".join(ORDER):
        if item.isdigit():
            advance(int(item))
        else:
            next(work, None)
    for _ in work:
        pass
    for i in range(len(pieces), len(makers)):
        advance(i)
    while not all(p.done for p in pieces):
        for i in range(len(pieces)):
            advance(i)
    sums = outputs.arrays
    small = results["small"]
    return (
        results["block_out"],
        results["input_grad"],
        small[4][0],
        sums["value"],
        *[g.T for g in small[:4]],
        small[6][0],
        sums["mix"],
        small[7],
        small[8],
        small[9][0],
        sums["out"],
        small[5][0],
        sums["ffn_in"],
        sums["ffn_out"],
    )


def solution(mesh):
    rows = P(("dp", "seq"), None)
    in_specs = (rows, rows, P("dp", None)) + (P(),) * 15
    out_specs = (rows, rows) + (P(),) * 15
    return jax.shard_map(shards, mesh=mesh, in_specs=in_specs, out_specs=out_specs, check_vma=False)
```
